32 devices in a mesh: narrow: 4 (over y, core), wide: 8 (over z, x).
Axes of the slice: x: 2, y: 2, z: 4, core: 2. Of those that a mesh axis runs over, the one named last changes fastest.
Arguments:
- layer_in: float32 [128, 384, 384], P(('narrow', 'wide')), may hold values from -6 to 6
- cotangent: float32 [128, 384, 384], P(('narrow', 'wide')), may hold values from -6 to 6
- qkv_master: float32 [1152, 384], P('wide'), may hold values from -0.3125 to 0.3125
- proj_master: float32 [384, 384], P('wide'), may hold values from -0.3125 to 0.3125
- up_master: float32 [1536, 384], P('wide'), may hold values from -0.3125 to 0.3125
- down_master: float32 [384, 1536], P('wide'), may hold values from -0.15625 to 0.15625
- vector_master: float32 [4608], P('wide'), may hold values from -0.3 to 1.4, as said below
- qkv_first: float32 [1152, 384], P('wide'), may hold values from -640 to 640
- proj_first: float32 [384, 384], P('wide'), may hold values from -640 to 640
- up_first: float32 [1536, 384], P('wide'), may hold values from -640 to 640
- down_first: float32 [384, 1536], P('wide'), may hold values from -640 to 640
- vector_first: float32 [4608], P('wide'), may hold values from -1280 to 1280
- qkv_second: float32 [1152, 384], P('wide'), may hold values from 12288 to 49152
- proj_second: float32 [384, 384], P('wide'), may hold values from 12288 to 49152
- up_second: float32 [1536, 384], P('wide'), may hold values from 12288 to 49152
- down_second: float32 [384, 1536], P('wide'), may hold values from 12288 to 49152
- vector_second: float32 [4608], P('wide'), may hold values from 49152 to 196608
Outputs:
- layer_out: float32 [128, 384, 384], P(('narrow', 'wide'))
- input_grad: float32 [128, 384, 384], P(('narrow', 'wide'))
- qkv_updated: float32 [1152, 384], P('wide')
- qkv_first_out: float32 [1152, 384], P('wide')
- qkv_second_out: float32 [1152, 384], P('wide')
- qkv_copy: bfloat16 [1152, 384], P('wide')
- proj_updated: float32 [384, 384], P('wide')
- proj_first_out: float32 [384, 384], P('wide')
- proj_second_out: float32 [384, 384], P('wide')
- proj_copy: bfloat16 [384, 384], P('wide')
- up_updated: float32 [1536, 384], P('wide')
- up_first_out: float32 [1536, 384], P('wide')
- up_second_out: float32 [1536, 384], P('wide')
- up_copy: bfloat16 [1536, 384], P('wide')
- down_updated: float32 [384, 1536], P('wide')
- down_first_out: float32 [384, 1536], P('wide')
- down_second_out: float32 [384, 1536], P('wide')
- down_copy: bfloat16 [384, 1536], P('wide')
- vector_updated: float32 [4608], P('wide')
- vector_first_out: float32 [4608], P('wide')
- vector_second_out: float32 [4608], P('wide')
- vector_copy: bfloat16 [4608], P('wide')
The draws below stay inside these ranges and needn't reach their ends.
Inputs may be any that keep to these rules, and one draw needn't show every extreme that they name: `vector_master`: entries of gain_one and gain_two lie in 0.6 to 1.4; all other entries lie in -0.3 to 0.3.
All inputs are finite; a program needn't handle non-finite values.
Results may differ from the reference program's by a relative error of at most 0.015.
Values may be sent and summed in bfloat16 or wider, within the bound.
No kernel may reach another device: no remote copies, remote signals or barrier semaphores. Data moves between devices by JAX's collectives and lax.ppermute only.
A program may use at most 128 MiB of HBM per device.

```python
import math
import jax
import jax.numpy as jnp
from jax import lax

D = 384
HEADS = 6
FF = 1536
STEP = 10
HEAD_DIM = 64
SEQ = 384
IMAGES = 128
TOKENS = 49152
VEC = 4608
N_NARROW = 4


def draw_vector_master(key, part):
    key = jax.random.fold_in(key, 7)
    position = jnp.arange(8 * D + FF)
    segment = position // D
    uniform_part = jax.random.uniform(key, (8 * D + FF,), jnp.float32, -0.5, 0.5)
    gain_mask = (segment == 0) | (segment == 2)
    return jnp.where(gain_mask, 1.0 + 0.8 * uniform_part, 0.6 * uniform_part)


def levels(stream_key, dims, shards, least, top_value):
    def one(dim, blocks):
        draws = jax.random.uniform(jax.random.fold_in(jax.random.fold_in(stream_key, 6), dim), (blocks,), jnp.float32, least / len(shards), top_value / len(shards))
        return jnp.repeat(jnp.exp(draws), dims[dim] // blocks).reshape((-1,) + (1,) * (len(dims) - dim - 1))

    factor_of = one(*shards[0])
    for cut in shards[1:]:
        factor_of = factor_of * one(*cut)
    return factor_of


def bell_draw(rng, shape, width, most, cuts=(), kind=jnp.bfloat16):
    level = levels(rng, shape, cuts, -0.22, 0.18) if cuts else 1.0
    array = jax.random.normal(rng, shape, jnp.float32) * width * level
    return jnp.minimum(jnp.maximum(array, -most), most).astype(kind)


def setup_inputs(seed: int = 0) -> dict:
    seeds = jax.random.split(jax.random.key(seed), 18)
    return {
        "layer_in": bell_draw(seeds[0], (IMAGES, SEQ, D), 1.0, 6.0, ((0, 32),), jnp.float32),
        "cotangent": bell_draw(seeds[1], (IMAGES, SEQ, D), 1.0, 6.0, ((0, 32),), jnp.float32),
        "qkv_master": bell_draw(seeds[2], (3 * D, D), D ** -0.5, 0.3125, ((0, 8),), jnp.float32),
        "proj_master": bell_draw(seeds[3], (D, D), D ** -0.5, 0.3125, ((0, 8),), jnp.float32),
        "up_master": bell_draw(seeds[4], (FF, D), D ** -0.5, 0.3125, ((0, 8),), jnp.float32),
        "down_master": bell_draw(seeds[5], (D, FF), FF ** -0.5, 0.15625, ((0, 8),), jnp.float32),
        "vector_master": draw_vector_master(jax.random.fold_in(seeds[17], 71), 0),
        "qkv_first": bell_draw(seeds[7], (3 * D, D), (0.5 * TOKENS ** 0.5), 640.0, ((0, 8),), jnp.float32),
        "proj_first": bell_draw(seeds[8], (D, D), (0.5 * TOKENS ** 0.5), 640.0, ((0, 8),), jnp.float32),
        "up_first": bell_draw(seeds[9], (FF, D), (0.5 * TOKENS ** 0.5), 640.0, ((0, 8),), jnp.float32),
        "down_first": bell_draw(seeds[10], (D, FF), (0.5 * TOKENS ** 0.5), 640.0, ((0, 8),), jnp.float32),
        "vector_first": bell_draw(seeds[11], (VEC,), (TOKENS ** 0.5), 1280.0, ((0, 8),), jnp.float32),
        "qkv_second": jnp.clip(jnp.exp(math.log(49152.0) - 1.3862944 * jax.random.uniform(seeds[12], (3 * D, D), jnp.float32) ** levels(seeds[12], (3 * D, D), ((0, 8),), -0.2, 0.2)), 12288.0, 49152.0),
        "proj_second": jnp.clip(jnp.exp(math.log(49152.0) - 1.3862944 * jax.random.uniform(seeds[13], (D, D), jnp.float32) ** levels(seeds[13], (D, D), ((0, 8),), -0.2, 0.2)), 12288.0, 49152.0),
        "up_second": jnp.clip(jnp.exp(math.log(49152.0) - 1.3862944 * jax.random.uniform(seeds[14], (FF, D), jnp.float32) ** levels(seeds[14], (FF, D), ((0, 8),), -0.2, 0.2)), 12288.0, 49152.0),
        "down_second": jnp.clip(jnp.exp(math.log(49152.0) - 1.3862944 * jax.random.uniform(seeds[15], (D, FF), jnp.float32) ** levels(seeds[15], (D, FF), ((0, 8),), -0.2, 0.2)), 12288.0, 49152.0),
        "vector_second": jnp.clip(jnp.exp(math.log(196608.0) - 1.3862944 * jax.random.uniform(seeds[16], (VEC,), jnp.float32) ** levels(seeds[16], (VEC,), ((0, 8),), -0.2, 0.2)), 49152.0, 196608.0),
    }


@jax.custom_vjp
def low(v):
    return lax.optimization_barrier(v.astype(jnp.bfloat16)).astype(jnp.float32)

@jax.custom_vjp
def low_back(v):
    return v

def low_keep(v):
    return (low(v), None)

def low_pass(kept, grad):
    return (grad,)

def back_keep(v):
    return (v, None)

def back_low(kept, grad):
    return (low(grad),)
low.defvjp(low_keep, low_pass)
low_back.defvjp(back_keep, back_low)
norm_eps = 1e-06
adam_eps = 1e-08
beta_first = 0.5
beta_second = 0.5
matrix_decay = 0.01
vector_rate = 0.3
highest = lax.Precision.HIGHEST

def layer_norm(values, norm_gain, norm_shift):
    centred = values - lax.optimization_barrier(jnp.mean(values, axis=-1, keepdims=True))
    variance = lax.optimization_barrier(jnp.mean(centred * centred, axis=-1, keepdims=True))
    return centred * lax.rsqrt(variance + norm_eps) * norm_gain + norm_shift

def gelu_exact(values):
    return jax.nn.gelu(values, approximate=False)

def unpack(vector, model_width):
    pieces = [vector[position * model_width:(position + 1) * model_width] for position in range(8)]
    return pieces + [vector[8 * model_width:]]

def matmul_rows(operand, weight):
    return jnp.dot(operand, weight.T, precision=highest)

def group_forward(image_block, weights):
    qkv_weight, proj_weight, up_weight, down_weight, vector = weights
    group_size = image_block.shape[0]
    gain_one, shift_one, gain_two, shift_two, query_bias, value_bias, proj_bias, down_bias, up_bias = unpack(vector, D)
    token_rows = image_block.reshape(group_size * SEQ, D)
    normed_one = low(layer_norm(token_rows, gain_one, shift_one))
    joint_bias = jnp.concatenate([query_bias, jnp.zeros_like(query_bias), value_bias])
    qkv_joint = low(low_back(matmul_rows(normed_one, qkv_weight) + joint_bias))
    qkv_joint = qkv_joint.reshape(group_size, SEQ, 3, HEADS, HEAD_DIM)
    scores = jnp.einsum('bqhd,bkhd->bhqk', qkv_joint[:, :, 0], qkv_joint[:, :, 1], precision=highest)
    scores = low_back(scores * HEAD_DIM ** (-0.5))
    attn_probs = low(jax.nn.softmax(scores, axis=-1))
    heads_out = jnp.einsum('bhqk,bkhd->bqhd', attn_probs, qkv_joint[:, :, 2], precision=highest)
    heads_out = low(low_back(heads_out.reshape(group_size * SEQ, D)))
    middle = token_rows + low_back(matmul_rows(heads_out, proj_weight) + proj_bias)
    normed_two = low(layer_norm(middle, gain_two, shift_two))
    upward = low_back(matmul_rows(normed_two, up_weight) + up_bias)
    activated = low(gelu_exact(upward))
    layer_out = middle + low_back(matmul_rows(activated, down_weight) + down_bias)
    return layer_out.reshape(image_block.shape)

def adam_step(master, grad_sum, first_old, second_old, step_rate, weight_decay):
    first_new = beta_first * first_old + (1.0 - beta_first) * grad_sum
    second_new = beta_second * second_old + (1.0 - beta_second) * grad_sum * grad_sum
    first_hat = first_new / (1.0 - beta_first ** STEP)
    second_hat = second_new / (1.0 - beta_second ** STEP)
    updated = master - step_rate * (first_hat / (jnp.sqrt(second_hat) + adam_eps) + weight_decay * master)
    return (updated, first_new, second_new, updated.astype(jnp.bfloat16))

def reference(layer_in, cotangent, qkv_master, proj_master, up_master, down_master, vector_master, qkv_first, proj_first, up_first, down_first, vector_first, qkv_second, proj_second, up_second, down_second, vector_second):
    copies = (low(qkv_master), low(proj_master), low(up_master), low(down_master), low(vector_master))

    def whole_layer(inputs, qkv_weight, proj_weight, up_weight, down_weight, vector):
        weights = (qkv_weight, proj_weight, up_weight, down_weight, vector)
        blocks = inputs.reshape(IMAGES // N_NARROW, N_NARROW, SEQ, D)
        group_step = jax.checkpoint(lambda image_block: group_forward(image_block, weights))
        return lax.map(group_step, blocks).reshape(IMAGES, SEQ, D)
    layer_out, back_fn = jax.vjp(whole_layer, layer_in, copies[0], copies[1], copies[2], copies[3], copies[4])
    gradients = back_fn(cotangent)
    qkv_new = adam_step(qkv_master, gradients[1], qkv_first, qkv_second, 0.6 * D ** (-0.5), matrix_decay)
    proj_new = adam_step(proj_master, gradients[2], proj_first, proj_second, 0.6 * D ** (-0.5), matrix_decay)
    up_new = adam_step(up_master, gradients[3], up_first, up_second, 0.6 * D ** (-0.5), matrix_decay)
    down_new = adam_step(down_master, gradients[4], down_first, down_second, 0.6 * FF ** (-0.5), matrix_decay)
    vector_new = adam_step(vector_master, gradients[5], vector_first, vector_second, vector_rate, 0.0)
    return (layer_out, gradients[0], qkv_new[0], qkv_new[1], qkv_new[2], qkv_new[3], proj_new[0], proj_new[1], proj_new[2], proj_new[3], up_new[0], up_new[1], up_new[2], up_new[3], down_new[0], down_new[1], down_new[2], down_new[3], vector_new[0], vector_new[1], vector_new[2], vector_new[3])
```

```python
import functools
import jax, jax.numpy as jnp
from jax import lax
from jax.experimental import pallas as pl
from jax.experimental.pallas import tpu as pltpu
from jax.sharding import PartitionSpec as P

STEP = 10
beta_first = 0.5
beta_second = 0.5
adam_eps = 1e-08
matrix_decay = 0.01
vector_rate = 0.3
HEADS = 6
EPS = 1e-6
bf16, f32 = jnp.bfloat16, jnp.float32

def dot(a, b, ca, cb):
    return lax.dot_general(a, b, (((ca,), (cb,)), ((), ())), preferred_element_type=f32)

def norm_stats(v):
    mean = jnp.mean(v, axis=-1, keepdims=True)
    cen = v - mean
    var = jnp.mean(cen * cen, axis=-1, keepdims=True)
    rstd = lax.rsqrt(var + EPS)
    return cen * rstd, rstd

def attn_fwd(x_ref, w_ref, vrow_ref, vcol_ref, jt_ref, e_ref, il_ref, ot_ref, h_ref):
    xhat, _ = norm_stats(x_ref[0])
    h = (xhat * vrow_ref[0:1, :] + vrow_ref[1:2, :]).astype(bf16)
    h_ref[0] = h
    d = h.shape[1]
    hs = d // HEADS
    jt = dot(w_ref[...], h, 1, 1) + vcol_ref[:, 0:1]
    jt_ref[0] = jt.astype(bf16)
    for i in range(HEADS):
        qt = jt_ref[0, i * hs:(i + 1) * hs, :]
        kt = jt_ref[0, d + i * hs:d + (i + 1) * hs, :]
        vt = jt_ref[0, 2 * d + i * hs:2 * d + (i + 1) * hs, :]
        st = dot((kt * 0.125), qt, 0, 0)
        m = jnp.max(st, axis=0, keepdims=True)
        e = jnp.exp(st - m)
        l = jnp.sum(e, axis=0, keepdims=True)
        eb = e.astype(bf16)
        e_ref[0, i] = eb
        il = 1.0 / l
        il_ref[0, i:i + 1, :] = il
        ot = dot(vt, eb, 1, 0) * il
        ot_ref[0, i * hs:(i + 1) * hs, :] = ot.astype(bf16)

def call_attn_fwd(x, w, vrow, vcol):
    b, t, d = x.shape
    one = lambda *s: pl.BlockSpec((1,) + s, lambda i: (i,) + (0,) * len(s))
    full = lambda a: pl.BlockSpec(a.shape, lambda i: (0,) * a.ndim)
    return pl.pallas_call(
        attn_fwd, grid=(b,),
        in_specs=[one(t, d), full(w), full(vrow), full(vcol)],
        out_specs=[one(3 * d, t), one(HEADS, t, t), one(8, t), one(d, t), one(t, d)],
        out_shape=[jax.ShapeDtypeStruct((b, 3 * d, t), bf16), jax.ShapeDtypeStruct((b, HEADS, t, t), bf16),
                   jax.ShapeDtypeStruct((b, 8, t), f32), jax.ShapeDtypeStruct((b, d, t), bf16), jax.ShapeDtypeStruct((b, t, d), bf16)],
        compiler_params=pltpu.CompilerParams(vmem_limit_bytes=50 << 20), name="attn_fwd",
    )(x, w, vrow, vcol)

def gelu_pair(u):
    cdf = 0.5 + 0.5 * lax.erf(u * (0.5 ** 0.5))
    pdf = jnp.exp(u * u * -0.5) * 0.3989422804014327
    return u * cdf, cdf + u * pdf

def mlp(x_ref, ot_ref, cot_ref, wp_ref, wu_ref, wd_ref, vrow_ref, ub_ref,
        mid_ref, act_ref, dm_ref, dot_ref, dwp_ref, dwu_ref, dwd_ref, dv_ref, dub_ref):
    i = pl.program_id(0)
    @pl.when(i == 0)
    def _():
        dwp_ref[...] = jnp.zeros_like(dwp_ref)
        dwu_ref[...] = jnp.zeros_like(dwu_ref)
        dwd_ref[...] = jnp.zeros_like(dwd_ref)
        dv_ref[...] = jnp.zeros_like(dv_ref)
        dub_ref[...] = jnp.zeros_like(dub_ref)
    ot = ot_ref[0]
    mid = x_ref[0] + (dot(ot, wp_ref[...], 0, 1) + vrow_ref[6:7, :])
    mid_ref[0] = mid
    xhat, rstd = norm_stats(mid)
    h2 = (xhat * vrow_ref[2:3, :] + vrow_ref[3:4, :]).astype(bf16)
    u = dot(h2, wu_ref[...], 1, 1) + ub_ref[0:1, :]
    act, gp = gelu_pair(u)
    act = act.astype(bf16)
    act_ref[0] = act
    cot = cot_ref[0]
    g = cot.astype(bf16)
    dwd_ref[...] += dot(g, act, 0, 0)
    du = dot(g, wd_ref[...], 1, 0) * gp
    dul = du.astype(bf16)
    dwu_ref[...] += dot(dul, h2, 0, 0)
    dh2 = dot(dul, wu_ref[...], 1, 0)
    gy = dh2 * vrow_ref[2:3, :]
    m1 = jnp.mean(gy, axis=-1, keepdims=True)
    m2 = jnp.mean(gy * xhat, axis=-1, keepdims=True)
    dm = cot + rstd * (gy - m1 - xhat * m2)
    dm_ref[0] = dm
    dml = dm.astype(bf16)
    dwp_ref[...] += dot(dml, ot, 0, 1)
    dot_ref[0] = dot(wp_ref[...], dml, 0, 1).astype(bf16)
    dv_ref[2:3, :] += jnp.sum(dh2 * xhat, axis=0, keepdims=True)
    dv_ref[3:4, :] += jnp.sum(dh2, axis=0, keepdims=True)
    dv_ref[6:7, :] += jnp.sum(dml.astype(f32), axis=0, keepdims=True)
    dv_ref[7:8, :] += jnp.sum(g.astype(f32), axis=0, keepdims=True)
    dub_ref[0:1, :] += jnp.sum(dul.astype(f32), axis=0, keepdims=True)

def call_mlp(x, ot, cot, wp, wu, wd, vrow, ub):
    b, t, d = x.shape
    ff = wu.shape[0]
    one = lambda *s: pl.BlockSpec((1,) + s, lambda i: (i,) + (0,) * len(s))
    full = lambda a: pl.BlockSpec(a.shape, lambda i: (0,) * a.ndim)
    S = jax.ShapeDtypeStruct
    outs = [S((b, t, d), f32), S((b, t, ff), bf16), S((b, t, d), f32), S((b, d, t), bf16),
            S((d, d), f32), S((ff, d), f32), S((d, ff), f32), S((8, d), f32), S((8, ff), f32)]
    return pl.pallas_call(
        mlp, grid=(b,),
        in_specs=[one(t, d), one(d, t), one(t, d)] + [full(a) for a in (wp, wu, wd, vrow, ub)],
        out_specs=[one(t, d), one(t, ff), one(t, d), one(d, t)] + [full(a) for a in outs[4:]],
        out_shape=outs,
        compiler_params=pltpu.CompilerParams(vmem_limit_bytes=56 << 20), name="mlp",
    )(x, ot, cot, wp, wu, wd, vrow, ub)

def attn_bwd(jt_ref, e_ref, il_ref, ot_ref, dot_ref, h_ref, dj_ref, dw_ref):
    i = pl.program_id(0)
    @pl.when(i == 0)
    def _():
        dw_ref[...] = jnp.zeros_like(dw_ref)
    t, d = h_ref.shape[1:]
    hs = d // HEADS
    for i in range(HEADS):
        rows = slice(i * hs, (i + 1) * hs)
        qt = jt_ref[0, i * hs:(i + 1) * hs, :]
        kt = jt_ref[0, d + i * hs:d + (i + 1) * hs, :]
        vt = jt_ref[0, 2 * d + i * hs:2 * d + (i + 1) * hs, :]
        do = dot_ref[0, rows, :].astype(f32) * il_ref[0, i:i + 1, :]
        dd = jnp.sum(do * ot_ref[0, rows, :].astype(f32), axis=0, keepdims=True)
        dob = do.astype(bf16)
        eb = e_ref[0, i]
        dp = dot(vt, dob, 0, 0)
        ds = (eb.astype(f32) * (dp - dd)).astype(bf16)
        dj_ref[0, rows, :] = (dot(kt, ds, 1, 0) * 0.125).astype(bf16)
        dj_ref[0, d + i * hs:d + (i + 1) * hs, :] = (dot(qt, ds, 1, 1) * 0.125).astype(bf16)
        dj_ref[0, 2 * d + i * hs:2 * d + (i + 1) * hs, :] = dot(dob, eb, 1, 1).astype(bf16)
    hx = jnp.concatenate([h_ref[0], jnp.ones((t, 128), bf16)], axis=1)
    dw_ref[...] += dot(dj_ref[0], hx, 1, 0)

def call_attn_bwd(jt, e, il, ot, dot_, h):
    b, t, d = h.shape
    one = lambda *s: pl.BlockSpec((1,) + s, lambda i: (i,) + (0,) * len(s))
    S = jax.ShapeDtypeStruct
    return pl.pallas_call(
        attn_bwd, grid=(b,),
        in_specs=[one(3 * d, t), one(HEADS, t, t), one(8, t), one(d, t), one(d, t), one(t, d)],
        out_specs=[one(3 * d, t), pl.BlockSpec((3 * d, d + 128), lambda i: (0, 0))],
        out_shape=[S((b, 3 * d, t), bf16), S((3 * d, d + 128), f32)],
        compiler_params=pltpu.CompilerParams(vmem_limit_bytes=50 << 20), name="attn_bwd",
    )(jt, e, il, ot, dot_, h)

def tail(x_ref, dm_ref, dj_ref, w_ref, mid_ref, act_ref, wd_ref, vrow_ref, gx_ref, lo_ref):
    lo_ref[0] = mid_ref[0] + (dot(act_ref[0], wd_ref[...], 1, 1) + vrow_ref[7:8, :])
    dh = dot(dj_ref[0], w_ref[...], 0, 0)
    xhat, rstd = norm_stats(x_ref[0])
    gy = dh * vrow_ref[0:1, :]
    m1 = jnp.mean(gy, axis=-1, keepdims=True)
    m2 = jnp.mean(gy * xhat, axis=-1, keepdims=True)
    gx_ref[0] = dm_ref[0] + rstd * (gy - m1 - xhat * m2)

def call_tail(x, dm, dj, w, mid, act, wd, vrow):
    b, t, d = x.shape
    one = lambda *s: pl.BlockSpec((1,) + s, lambda i: (i,) + (0,) * len(s))
    full = lambda a: pl.BlockSpec(a.shape, lambda i: (0,) * a.ndim)
    S = jax.ShapeDtypeStruct
    return pl.pallas_call(
        tail, grid=(b,),
        in_specs=[one(t, d), one(t, d), one(3 * d, t), full(w), one(t, d), one(t, act.shape[2]), full(wd), full(vrow)],
        out_specs=[one(t, d), one(t, d)],
        out_shape=[S((b, t, d), f32), S((b, t, d), f32)],
        compiler_params=pltpu.CompilerParams(vmem_limit_bytes=50 << 20), name="tail",
    )(x, dm, dj, w, mid, act, wd, vrow)


class Links:
    def __init__(self, mesh):
        self.wide, self.narrow = mesh.shape["wide"], mesh.shape["narrow"]
        bits = [1 << k for k in range(self.wide.bit_length() - 1)]
        self.orders = (bits[::-1], bits[:1] + bits[:0:-1])
        self.masks = []
        for order in self.orders:
            masks = [0]
            for bit in order:
                masks = masks + [m ^ bit for m in masks]
            self.masks.append(masks)
        self.slots = [[masks.index(m) for m in range(self.wide)] for masks in self.masks]

    def permute(self, value, partner):
        pairs = []
        for n in range(self.narrow):
            for w in range(self.wide):
                n2, w2 = partner(n, w)
                pairs.append((n * self.wide + w, n2 * self.wide + w2))
        return lax.ppermute(value, ("narrow", "wide"), pairs)

    def core(self, value):
        return self.permute(value, lambda n, w: (n ^ 1, w))

    def step(self, value, k):
        return self.permute(value, lambda n, w: (n, w ^ self.orders[n % 2][k]))

    def others(self, value):
        total = value.astype(f32)
        bit = 2
        while bit < self.narrow:
            low = total.astype(bf16)
            total = low.astype(f32) + self.permute(low, lambda n, w, bit=bit: (n ^ bit, w)).astype(f32)
            bit *= 2
        return total

    def here(self):
        return lax.axis_index("wide"), lax.axis_index("narrow") % 2

    def gather(self, packed):
        me, core = self.here()
        rows, columns = packed.shape
        held = lax.dynamic_slice_in_dim(packed, core * (rows // 2), rows // 2)
        for k in range(len(self.orders[0])):
            held = jnp.concatenate([held, self.step(held, k)], axis=0)
        both = jnp.concatenate([held, self.core(held)], axis=0).reshape(2 * self.wide, rows // 2, columns)
        relative = jnp.arange(self.wide) ^ me
        first = jnp.take(jnp.array(self.slots[0]), relative) + core * self.wide
        second = jnp.take(jnp.array(self.slots[1]), relative) + (1 - core) * self.wide
        index = jnp.stack([first, second], axis=1).reshape(-1)
        return jnp.take(both, index, axis=0).reshape(self.wide, rows, columns)

    def reduce(self, packed):
        me, core = self.here()
        _, rows, columns = packed.shape
        halves = packed.reshape(2 * self.wide, rows // 2, columns)
        masks = jnp.array(self.masks)
        own = jnp.take(halves, (masks[core] ^ me) * 2 + core, axis=0)
        give = jnp.take(halves, (masks[1 - core] ^ me) * 2 + (1 - core), axis=0)
        held = own + self.core(give.astype(bf16)).astype(f32)
        for k in range(len(self.orders[0]) - 1, -1, -1):
            half = held.shape[0] // 2
            held = held[:half] + self.step(held[half:].astype(bf16), k).astype(f32)
        total = self.others(held[0])
        other = self.core(total)
        return jnp.where(core == 0, jnp.concatenate([total, other]), jnp.concatenate([other, total]))


def to_rows(block, columns):
    return jnp.concatenate([block[..., j:j + columns] for j in range(0, block.shape[-1], columns)], axis=-2)


def from_rows(block, count):
    return jnp.concatenate(jnp.split(block, count, axis=-2), axis=-1)


def padded(block, multiple):
    extra = -block.shape[-2] % multiple
    return jnp.pad(block, [(0, 0)] * (block.ndim - 2) + [(0, extra), (0, 0)])


def adam_step(master, grad_sum, first_old, second_old, step_rate, weight_decay):
    first_new = beta_first * first_old + (1.0 - beta_first) * grad_sum
    second_new = beta_second * second_old + (1.0 - beta_second) * grad_sum * grad_sum
    first_hat = first_new / (1.0 - beta_first**STEP)
    second_hat = second_new / (1.0 - beta_second**STEP)
    updated = master - step_rate * (
        first_hat / (jnp.sqrt(second_hat) + adam_eps) + weight_decay * master
    )
    return (updated, first_new, second_new, updated.astype(bf16))


def per_device(links, x, cot, qkv_m, proj_m, up_m, down_m, vec_m, qkv_f, proj_f, up_f, down_f, vec_f, qkv_s, proj_s, up_s, down_s, vec_s):
    n = links.wide
    d = x.shape[2]
    ff = down_m.shape[1]
    parts = ff // d
    q_rows, p_rows, u_rows, v_size = qkv_m.shape[0], proj_m.shape[0], up_m.shape[0], vec_m.shape[0]
    v_rows = -(-v_size // d)
    vec_block = jnp.pad(vec_m, (0, v_rows * d - v_size)).reshape(v_rows, d)
    first = padded(jnp.concatenate([qkv_m, vec_block]).astype(bf16), 32)
    second = padded(jnp.concatenate([proj_m, up_m, to_rows(down_m, d)]).astype(bf16), 32)
    first_all = links.gather(first)
    second_all = links.gather(second)
    wq = first_all[:, :q_rows].reshape(-1, d)
    vec = first_all[:, q_rows:q_rows + v_rows].reshape(n, v_rows * d)[:, :v_size].reshape(-1).astype(f32)
    wp = second_all[:, :p_rows].reshape(-1, d)
    wu = second_all[:, p_rows:p_rows + u_rows].reshape(-1, d)
    wd = from_rows(second_all[:, p_rows + u_rows:p_rows + u_rows + parts * p_rows], parts).reshape(-1, ff)
    vrow = vec[:8 * d].reshape(8, d)
    qkv_bias = jnp.concatenate([vrow[4], jnp.zeros_like(vrow[4]), vrow[5]])
    vcol = jnp.broadcast_to(qkv_bias[:, None], (3 * d, 8))
    ub = jnp.broadcast_to(vec[None, 8 * d:], (8, ff))

    jt, e, il, ot, h = call_attn_fwd(x, wq, vrow, vcol)
    mid, act, dm, dot_, dwp, dwu, dwd, dv, dub = call_mlp(x, ot, cot, wp, wu, wd, vrow, ub)
    grads = padded(jnp.concatenate([dwp.reshape(n, p_rows, d), dwu.reshape(n, u_rows, d), to_rows(dwd.reshape(n, p_rows, ff), d)], axis=1), 32)
    second_sum = links.reduce(grads)
    dj, dwx = call_attn_bwd(jt, e, il, ot, dot_, h)
    dwq, db = dwx[:, :d], dwx[:, d]
    wqf = wq.astype(f32)
    dg1 = jnp.sum(wqf * (dwq - db[:, None] * vrow[1]), axis=0) / vrow[0]
    ds1 = jnp.sum(wqf * db[:, None], axis=0)
    dvec = jnp.concatenate([dg1, ds1, dv[2], dv[3], db[:d], db[2 * d:], dv[6], dv[7], dub[0]]).reshape(n, v_size)
    dvec = jnp.pad(dvec, ((0, 0), (0, v_rows * d - v_size))).reshape(n, v_rows, d)
    first_sum = links.reduce(padded(jnp.concatenate([dwq.reshape(n, q_rows, d), dvec], axis=1), 32))
    gx, lo = call_tail(x, dm, dj, wq, mid, act, wd, vrow)

    g_q = first_sum[:q_rows]
    g_v = first_sum[q_rows:q_rows + v_rows].reshape(-1)[:v_size]
    g_p = second_sum[:p_rows]
    g_u = second_sum[p_rows:p_rows + u_rows]
    g_d = from_rows(second_sum[p_rows + u_rows:p_rows + u_rows + parts * p_rows], parts)
    return (
        lo, gx,
        *adam_step(qkv_m, g_q, qkv_f, qkv_s, 0.6 * d ** -0.5, matrix_decay),
        *adam_step(proj_m, g_p, proj_f, proj_s, 0.6 * d ** -0.5, matrix_decay),
        *adam_step(up_m, g_u, up_f, up_s, 0.6 * d ** -0.5, matrix_decay),
        *adam_step(down_m, g_d, down_f, down_s, 0.6 * ff ** -0.5, matrix_decay),
        *adam_step(vec_m, g_v, vec_f, vec_s, vector_rate, 0.0),
    )


def solution(mesh):
    tokens = P(("narrow", "wide"), None, None)
    matrix, vector = P("wide", None), P("wide")
    state = (matrix,) * 4 + (vector,)
    return jax.shard_map(
        functools.partial(per_device, Links(mesh)),
        mesh=mesh,
        in_specs=(tokens, tokens) + state * 3,
        out_specs=(tokens, tokens) + (matrix,) * 16 + (vector,) * 4,
        check_vma=False,
    )
```

```python
import functools

import jax
import jax.numpy as jnp
from jax import lax
from jax.experimental import pallas as pl
from jax.experimental.pallas import tpu as pltpu
from jax.sharding import PartitionSpec as P

STEP = 10
HEADS = 6
EPS = 1e-6
OWNERS = 8
beta_first = 0.5
beta_second = 0.5
adam_eps = 1e-08
matrix_decay = 0.01
vector_rate = 0.3
bf16, f32 = jnp.bfloat16, jnp.float32
S = jax.ShapeDtypeStruct
ANY = pl.BlockSpec(memory_space=pl.ANY)
HBM = pl.BlockSpec(memory_space=pltpu.HBM)


def dot(a, b, ca, cb):
    return lax.dot_general(a, b, (((ca,), (cb,)), ((), ())), preferred_element_type=f32)


def norm_stats(v):
    mean = jnp.mean(v, axis=-1, keepdims=True)
    cen = v - mean
    var = jnp.mean(cen * cen, axis=-1, keepdims=True)
    rstd = lax.rsqrt(var + EPS)
    return cen * rstd, rstd


def one(*shape, off=0):
    return pl.BlockSpec((1,) + shape, lambda i: (i + off,) + (0,) * len(shape))


def full(a):
    return pl.BlockSpec(a.shape, lambda i: (0,) * len(a.shape))


def whole(a):
    return pl.BlockSpec(a.shape, lambda: (0,) * len(a.shape))


def params(mib):
    return pltpu.CompilerParams(vmem_limit_bytes=mib << 20)


def cost(us):
    return pl.CostEstimate(flops=int(us * 1.0e9), bytes_accessed=1 << 20, transcendentals=0)


class Layout:
    def __init__(self, d, ff, masks, position):
        self.d, self.ff, self.cols = d, ff, ff // d
        self.masks, self.position = masks, position
        self.q, self.p, self.u = 3 * d // OWNERS, d // OWNERS, ff // OWNERS
        q0 = (self.q // 2 + 15) // 16 * 16
        self.first = ((("q", 0, q0, 0, 0),), (("q", q0, self.q - q0, 0, 0), ("v", 0, 16, 0, self.q - q0)))
        self.first_rows = max(q0, self.q - q0 + 16)
        p0 = 16
        down = tuple(("d", 0, self.p, j, j * self.p) for j in range(self.cols))
        self.second = (
            (("u", 0, self.u, 0, 0), ("p", 0, p0, 0, self.u)),
            down + (("p", p0, self.p - p0, 0, self.cols * self.p),),
        )
        self.second_rows = max(self.u + p0, self.cols * self.p + self.p - p0)
        self.piece = (8 * d + ff) // (3 * OWNERS)


def place(lay, piece, owner):
    name, start, rows, col, _ = piece
    size = {"q": lay.q, "p": lay.p, "u": lay.u, "d": lay.p, "v": 16}[name]
    at = owner * size + start
    if not isinstance(at, int):
        at = pl.multiple_of(at, 16)
    return pl.ds(at, rows), pl.ds(col * lay.d, lay.d)


def pack(lay, q_hbm, p_hbm, u_hbm, d_hbm, v_hbm, first_ref, second_ref, q_ref, p_ref, u_ref, d_ref, v_ref, sems):
    refs = {"q": q_ref, "p": p_ref, "u": u_ref, "d": d_ref}
    moves = [pltpu.make_async_copy(a, b, sems.at[i]) for i, (a, b) in enumerate(
        ((q_hbm, q_ref), (v_hbm, v_ref), (p_hbm, p_ref), (u_hbm, u_ref), (d_hbm, d_ref)))]
    for move in moves:
        move.start()
    for move in moves:
        move.wait()
    core = lay.position()[1]
    v = v_ref[...].reshape(1, v_ref.shape[0])

    def fill(halves, out_ref):
        end = 0
        for name, start, rows, col, at in halves:
            if name == "v":
                out_ref[at:at + rows, :] = jnp.zeros((rows, lay.d), bf16)
                for k in range(3):
                    out_ref[at + k:at + k + 1, :lay.piece] = v[:, k * lay.piece:(k + 1) * lay.piece].astype(bf16)
            else:
                out_ref[at:at + rows, :] = refs[name][start:start + rows, col * lay.d:(col + 1) * lay.d].astype(bf16)
            end = at + rows
        if end < out_ref.shape[0]:
            out_ref[end:, :] = jnp.zeros((out_ref.shape[0] - end, lay.d), bf16)

    for half in range(2):
        @pl.when(core == half)
        def _():
            fill(lay.first[half], first_ref)
            fill(lay.second[half], second_ref)


def call_pack(lay, q, p, u, d, v):
    outs = [S((lay.first_rows, lay.d), bf16), S((lay.second_rows, lay.d), bf16)]
    return pl.pallas_call(
        functools.partial(pack, lay), in_specs=[HBM] * 5,
        out_specs=[whole(a) for a in outs], out_shape=outs,
        scratch_shapes=[pltpu.VMEM(a.shape, f32) for a in (q, p, u, d, v)] + [pltpu.SemaphoreType.DMA((5,))],
        compiler_params=params(60), name="pack",
    )(q, p, u, d, v)


def fetch(lay, halves, mine_ref, other_ref, dests, sems):
    me, core = lay.position()

    def copies(half, src_ref, base):
        out = []
        for j in range(OWNERS):
            for piece in halves[half]:
                name, _, rows, _, at = piece
                r, c = place(lay, piece, me ^ lay.masks[half][j])
                dst = dests[name].at[r] if name != "d" else dests[name].at[r, c]
                out.append(pltpu.make_async_copy(src_ref.at[j, pl.ds(at, rows)], dst, sems.at[base + len(out)]))
        return out

    for half in range(2):
        @pl.when(core == half)
        def _():
            first = copies(half, mine_ref, 0)
            both = first + copies(1 - half, other_ref, len(first))
            for c in both:
                c.start()
            for c in both:
                c.wait()


def emit(lay, halves, arrays, keep_ref, give_ref):
    me, core = lay.position()

    def fill(half, out_ref):
        for j in range(OWNERS):
            end = 0
            for piece in halves[half]:
                name, _, rows, _, at = piece
                r, c = place(lay, piece, me ^ lay.masks[half][j])
                out_ref[j, at:at + rows, :] = arrays[name][r, c].astype(out_ref.dtype)
                end = at + rows
            if end < out_ref.shape[1]:
                out_ref[j, end:, :] = jnp.zeros((out_ref.shape[1] - end, lay.d), out_ref.dtype)

    for half in range(2):
        @pl.when(core == half)
        def _():
            fill(half, keep_ref)
            fill(1 - half, give_ref)


def attn_fwd_image(x_ref, w_ref, vrow_ref, vcol_ref, jt_ref, e_ref, il_ref, ot_ref, h_ref):
    xhat, _ = norm_stats(x_ref[0])
    h = (xhat * vrow_ref[0:1, :] + vrow_ref[1:2, :]).astype(bf16)
    h_ref[0] = h
    d = h.shape[1]
    hs = d // HEADS
    jt = dot(w_ref[...], h, 1, 1) + vcol_ref[:, 0:1]
    jt_ref[0] = jt.astype(bf16)
    for i in range(HEADS):
        qt = jt_ref[0, i * hs:(i + 1) * hs, :]
        kt = jt_ref[0, d + i * hs:d + (i + 1) * hs, :]
        vt = jt_ref[0, 2 * d + i * hs:2 * d + (i + 1) * hs, :]
        st = dot((kt * 0.125), qt, 0, 0)
        m = jnp.max(st, axis=0, keepdims=True)
        e = jnp.exp(st - m)
        l = jnp.sum(e, axis=0, keepdims=True)
        eb = e.astype(bf16)
        e_ref[0, i] = eb
        il = 1.0 / l
        il_ref[0, i:i + 1, :] = il
        ot = dot(vt, eb, 1, 0) * il
        ot_ref[0, i * hs:(i + 1) * hs, :] = ot.astype(bf16)


def attn_fwd_first(lay, mine_ref, other_ref, x_ref, jt_ref, e_ref, il_ref, ot_ref, h_ref, w_ref, vrow_ref, vcol_ref, vec_scr, sems):
    @pl.when(pl.program_id(0) == 0)
    def _():
        fetch(lay, lay.first, mine_ref, other_ref, {"q": w_ref, "v": vec_scr}, sems)
        d, s = lay.d, lay.piece
        vrow_ref[...] = jnp.zeros_like(vrow_ref)
        for r in range(8 + lay.cols):
            for k in range(2):
                g = 2 * r + k
                row = vec_scr[g // 3 * 16:g // 3 * 16 + 16, :].astype(f32)[g % 3:g % 3 + 1, :s]
                vrow_ref[r:r + 1, k * s:(k + 1) * s] = row
        cols = jnp.transpose(vrow_ref[0:8, :])
        vcol_ref[...] = jnp.zeros_like(vcol_ref)
        vcol_ref[0:d, 0:1] = cols[:, 4:5]
        vcol_ref[2 * d:3 * d, 0:1] = cols[:, 5:6]
    attn_fwd_image(x_ref, w_ref, vrow_ref, vcol_ref, jt_ref, e_ref, il_ref, ot_ref, h_ref)


def attn_fwd_rest(x_ref, w_ref, vrow_ref, vcol_ref, a, b, c, d, e, jt_ref, e_ref, il_ref, ot_ref, h_ref):
    attn_fwd_image(x_ref, w_ref, vrow_ref, vcol_ref, jt_ref, e_ref, il_ref, ot_ref, h_ref)


def fwd_outs(b, t, d):
    return [S((b, 3 * d, t), bf16), S((b, HEADS, t, t), bf16), S((b, 8, t), f32), S((b, d, t), bf16), S((b, t, d), bf16)]


def fwd_blocks(t, d, off):
    return [one(3 * d, t, off=off), one(HEADS, t, t, off=off), one(8, t, off=off), one(d, t, off=off), one(t, d, off=off)]


def call_attn_fwd_first(lay, mine, other, x, count):
    b, t, d = x.shape
    extra = [S((3 * d, d), bf16), S((16, d), f32), S((3 * d, 8), f32)]
    n_copies = OWNERS * (len(lay.first[0]) + len(lay.first[1]))
    return pl.pallas_call(
        functools.partial(attn_fwd_first, lay), grid=(count,),
        in_specs=[HBM, HBM, one(t, d)],
        out_specs=fwd_blocks(t, d, 0) + [full(a) for a in extra],
        out_shape=fwd_outs(b, t, d) + extra,
        scratch_shapes=[pltpu.VMEM((OWNERS * 16, d), bf16), pltpu.SemaphoreType.DMA((n_copies,))],
        compiler_params=params(60), cost_estimate=cost(4 * count), name="attn_fwd_first",
    )(mine, other, x)


def call_attn_fwd_rest(x, w, vrow, vcol, outs, off, count):
    b, t, d = x.shape
    return pl.pallas_call(
        attn_fwd_rest, grid=(count,),
        in_specs=[one(t, d, off=off), full(w), full(vrow), full(vcol)] + [ANY] * 5,
        out_specs=fwd_blocks(t, d, off), out_shape=fwd_outs(b, t, d),
        input_output_aliases={4 + k: k for k in range(5)},
        compiler_params=params(60), cost_estimate=cost(4 * count), name="attn_fwd_rest",
    )(x, w, vrow, vcol, *outs)


def gelu_pair(u):
    cdf = 0.5 + 0.5 * lax.erf(u * (0.5 ** 0.5))
    pdf = jnp.exp(u * u * -0.5) * 0.3989422804014327
    return u * cdf, cdf + u * pdf


def mlp(lay, count, mine_ref, other_ref, x_ref, ot_ref, cot_ref, vrow_ref,
        mid_ref, act_ref, dm_ref, dot_ref, wd_ref, dv_ref, keep_ref, give_ref,
        wp_ref, wu_ref, dwp_ref, dwu_ref, dwd_ref, sems):
    i = pl.program_id(0)
    d, cols = lay.d, lay.cols

    @pl.when(i == 0)
    def _():
        fetch(lay, lay.second, mine_ref, other_ref, {"p": wp_ref, "u": wu_ref, "d": wd_ref}, sems)
        dwp_ref[...] = jnp.zeros_like(dwp_ref)
        dwu_ref[...] = jnp.zeros_like(dwu_ref)
        dwd_ref[...] = jnp.zeros_like(dwd_ref)
        dv_ref[...] = jnp.zeros_like(dv_ref)

    ot = ot_ref[0]
    mid = x_ref[0] + (dot(ot, wp_ref[...], 0, 1) + vrow_ref[6:7, :])
    mid_ref[0] = mid
    xhat, rstd = norm_stats(mid)
    h2 = (xhat * vrow_ref[2:3, :] + vrow_ref[3:4, :]).astype(bf16)
    ub = jnp.concatenate([vrow_ref[8 + j:9 + j, :] for j in range(cols)], axis=1)
    u = dot(h2, wu_ref[...], 1, 1) + ub
    act, gp = gelu_pair(u)
    act = act.astype(bf16)
    act_ref[0] = act
    cot = cot_ref[0]
    g = cot.astype(bf16)
    dwd_ref[...] += dot(g, act, 0, 0)
    du = dot(g, wd_ref[...], 1, 0) * gp
    dul = du.astype(bf16)
    dwu_ref[...] += dot(dul, h2, 0, 0)
    dh2 = dot(dul, wu_ref[...], 1, 0)
    gy = dh2 * vrow_ref[2:3, :]
    m1 = jnp.mean(gy, axis=-1, keepdims=True)
    m2 = jnp.mean(gy * xhat, axis=-1, keepdims=True)
    dm = cot + rstd * (gy - m1 - xhat * m2)
    dm_ref[0] = dm
    dml = dm.astype(bf16)
    dwp_ref[...] += dot(dml, ot, 0, 1)
    dot_ref[0] = dot(wp_ref[...], dml, 0, 1).astype(bf16)
    dv_ref[2:3, :] += jnp.sum(dh2 * xhat, axis=0, keepdims=True)
    dv_ref[3:4, :] += jnp.sum(dh2, axis=0, keepdims=True)
    dv_ref[6:7, :] += jnp.sum(dml.astype(f32), axis=0, keepdims=True)
    dv_ref[7:8, :] += jnp.sum(g.astype(f32), axis=0, keepdims=True)
    dub = jnp.sum(dul.astype(f32), axis=0, keepdims=True)
    for j in range(cols):
        dv_ref[8 + j:9 + j, :] += dub[:, j * d:(j + 1) * d]

    @pl.when(i == count - 1)
    def _():
        emit(lay, lay.second, {"p": dwp_ref, "u": dwu_ref, "d": dwd_ref}, keep_ref, give_ref)


def call_mlp(lay, mine, other, x, ot, cot, vrow):
    b, t, d = x.shape
    ff = lay.ff
    acc = [S((d, ff), bf16), S((16, d), f32), S((OWNERS, lay.second_rows, d), f32), S((OWNERS, lay.second_rows, d), bf16)]
    outs = [S((b, t, d), f32), S((b, t, ff), bf16), S((b, t, d), f32), S((b, d, t), bf16)] + acc
    n_copies = OWNERS * (len(lay.second[0]) + len(lay.second[1]))
    return pl.pallas_call(
        functools.partial(mlp, lay, b), grid=(b,),
        in_specs=[HBM, HBM, one(t, d), one(d, t), one(t, d), full(vrow)],
        out_specs=[one(t, d), one(t, ff), one(t, d), one(d, t)] + [full(a) for a in acc],
        out_shape=outs,
        scratch_shapes=[pltpu.VMEM((d, d), bf16), pltpu.VMEM((ff, d), bf16), pltpu.VMEM((d, d), f32), pltpu.VMEM((ff, d), f32),
                        pltpu.VMEM((d, ff), f32), pltpu.SemaphoreType.DMA((n_copies,))],
        compiler_params=params(60), cost_estimate=cost(24), name="mlp",
    )(mine, other, x, ot, cot, vrow)


def attn_bwd_image(jt_ref, e_ref, il_ref, ot_ref, dot_ref, h_ref, dj_ref, dw_ref):
    t, d = h_ref.shape[1:]
    hs = d // HEADS
    for i in range(HEADS):
        rows = slice(i * hs, (i + 1) * hs)
        qt = jt_ref[0, i * hs:(i + 1) * hs, :]
        kt = jt_ref[0, d + i * hs:d + (i + 1) * hs, :]
        vt = jt_ref[0, 2 * d + i * hs:2 * d + (i + 1) * hs, :]
        do = dot_ref[0, rows, :].astype(f32) * il_ref[0, i:i + 1, :]
        dd = jnp.sum(do * ot_ref[0, rows, :].astype(f32), axis=0, keepdims=True)
        dob = do.astype(bf16)
        eb = e_ref[0, i]
        dp = dot(vt, dob, 0, 0)
        ds = (eb.astype(f32) * (dp - dd)).astype(bf16)
        dj_ref[0, rows, :] = (dot(kt, ds, 1, 0) * 0.125).astype(bf16)
        dj_ref[0, d + i * hs:d + (i + 1) * hs, :] = (dot(qt, ds, 1, 1) * 0.125).astype(bf16)
        dj_ref[0, 2 * d + i * hs:2 * d + (i + 1) * hs, :] = dot(dob, eb, 1, 1).astype(bf16)
    hx = jnp.concatenate([h_ref[0], jnp.ones((t, 128), bf16)], axis=1)
    dw_ref[...] += dot(dj_ref[0], hx, 1, 0)


def attn_bwd_first(jt_ref, e_ref, il_ref, ot_ref, dot_ref, h_ref, dj_ref, dw_ref):
    @pl.when(pl.program_id(0) == 0)
    def _():
        dw_ref[...] = jnp.zeros_like(dw_ref)
    attn_bwd_image(jt_ref, e_ref, il_ref, ot_ref, dot_ref, h_ref, dj_ref, dw_ref)


def attn_bwd_last(lay, count, jt_ref, e_ref, il_ref, ot_ref, dot_ref, h_ref, dw_in_ref, w_ref, vrow_ref, dv_ref, dj_in_ref,
                  dj_ref, keep_ref, give_ref, dw_ref, vec_scr):
    i = pl.program_id(0)

    @pl.when(i == 0)
    def _():
        dw_ref[...] = dw_in_ref[...]
    attn_bwd_image(jt_ref, e_ref, il_ref, ot_ref, dot_ref, h_ref, dj_ref, dw_ref)

    @pl.when(i == count - 1)
    def _():
        d, s = lay.d, lay.piece
        w = w_ref[...].astype(f32)
        db = dw_ref[:, d:d + 1]
        gain = jnp.sum(w * (dw_ref[:, 0:d] - db * vrow_ref[1:2, :]), axis=0, keepdims=True) / vrow_ref[0:1, :]
        shift = jnp.sum(w * db, axis=0, keepdims=True)
        biases = jnp.transpose(dw_ref[:, d:d + 8])
        rows = [gain, shift, dv_ref[2:3, :], dv_ref[3:4, :], biases[0:1, 0:d], biases[0:1, 2 * d:3 * d]]
        rows += [dv_ref[k:k + 1, :] for k in range(6, 8 + lay.cols)]
        vec_scr[...] = jnp.zeros_like(vec_scr)
        for g in range(3 * OWNERS):
            at = g // 3 * 16 + g % 3
            vec_scr[at:at + 1, 0:s] = rows[g // 2][:, g % 2 * s:(g % 2 + 1) * s]
        emit(lay, lay.first, {"q": dw_ref, "v": vec_scr}, keep_ref, give_ref)


def bwd_blocks(t, d, off):
    return [one(3 * d, t, off=off), one(HEADS, t, t, off=off), one(8, t, off=off), one(d, t, off=off), one(d, t, off=off), one(t, d, off=off)]


def call_attn_bwd_first(acts, count):
    b, t, d = acts[-1].shape
    dw = S((3 * d, d + 128), f32)
    return pl.pallas_call(
        attn_bwd_first, grid=(count,), in_specs=bwd_blocks(t, d, 0),
        out_specs=[one(3 * d, t), full(dw)], out_shape=[S((b, 3 * d, t), bf16), dw],
        compiler_params=params(60), cost_estimate=cost(4 * count), name="attn_bwd_first",
    )(*acts)


def call_attn_bwd_last(lay, acts, dw, w, vrow, dv, dj, off, count):
    b, t, d = acts[-1].shape
    slots = [S((OWNERS, lay.first_rows, d), f32), S((OWNERS, lay.first_rows, d), bf16)]
    return pl.pallas_call(
        functools.partial(attn_bwd_last, lay, count), grid=(count,),
        in_specs=bwd_blocks(t, d, off) + [full(dw), full(w), full(vrow), full(dv), ANY],
        out_specs=[one(3 * d, t, off=off)] + [full(a) for a in slots], out_shape=[S((b, 3 * d, t), bf16)] + slots,
        scratch_shapes=[pltpu.VMEM(dw.shape, f32), pltpu.VMEM((OWNERS * 16, d), f32)],
        input_output_aliases={10: 0},
        compiler_params=params(60), cost_estimate=cost(4 * count + 2), name="attn_bwd_last",
    )(*acts, dw, w, vrow, dv, dj)


def tail(x_ref, dm_ref, dj_ref, w_ref, mid_ref, act_ref, wd_ref, vrow_ref, gx_ref, lo_ref):
    lo_ref[0] = mid_ref[0] + (dot(act_ref[0], wd_ref[...], 1, 1) + vrow_ref[7:8, :])
    dh = dot(dj_ref[0], w_ref[...], 0, 0)
    xhat, rstd = norm_stats(x_ref[0])
    gy = dh * vrow_ref[0:1, :]
    m1 = jnp.mean(gy, axis=-1, keepdims=True)
    m2 = jnp.mean(gy * xhat, axis=-1, keepdims=True)
    gx_ref[0] = dm_ref[0] + rstd * (gy - m1 - xhat * m2)


def call_tail(x, dm, dj, w, mid, act, wd, vrow):
    b, t, d = x.shape
    return pl.pallas_call(
        tail, grid=(b,),
        in_specs=[one(t, d), one(t, d), one(3 * d, t), full(w), one(t, d), one(t, act.shape[2]), full(wd), full(vrow)],
        out_specs=[one(t, d), one(t, d)],
        out_shape=[S((b, t, d), f32), S((b, t, d), f32)],
        compiler_params=params(60), cost_estimate=cost(10), name="tail",
    )(x, dm, dj, w, mid, act, wd, vrow)


def adam_values(master, first, second, grad, rate, decay):
    first_new = beta_first * first + (1.0 - beta_first) * grad
    second_new = beta_second * second + (1.0 - beta_second) * grad * grad
    first_hat = first_new * (1.0 / (1.0 - beta_first ** STEP))
    second_hat = second_new * (1.0 / (1.0 - beta_second ** STEP))
    new = master - rate * (first_hat / (jnp.sqrt(second_hat) + adam_eps) + decay * master)
    return new, first_new, second_new, new.astype(bf16)


def adam_rows(refs, outs, rows, grad, rate, decay):
    for out, value in zip(outs, adam_values(*(r[rows] for r in refs), grad, rate, decay)):
        out[rows] = value


def adam(lay, halves, names, mine_ref, other_ref, *refs):
    core = lay.position()[1]
    count = len(names)
    states = {name: refs[3 * k:3 * k + 3] for k, name in enumerate(names)}
    outs = {name: refs[3 * count + 4 * k:3 * count + 4 * k + 4] for k, name in enumerate(names)}
    rates = {"q": 0.6 * lay.d ** -0.5, "p": 0.6 * lay.d ** -0.5, "u": 0.6 * lay.d ** -0.5, "d": 0.6 * lay.ff ** -0.5, "v": vector_rate}

    def step(half, src_ref):
        for name, start, rows, col, at in halves[half]:
            if name == "v":
                grad = jnp.concatenate([src_ref[at + k:at + k + 1, :lay.piece] for k in range(3)], axis=1)
                size = 3 * lay.piece
                new = adam_values(*(r[...].reshape(1, size) for r in states[name]), grad, rates[name], 0.0)
                for out, value in zip(outs[name], new):
                    out[...] = value.reshape(size)
            else:
                span = (slice(start, start + rows), slice(col * lay.d, (col + 1) * lay.d))
                adam_rows(states[name], outs[name], span, src_ref[at:at + rows, :], rates[name], matrix_decay)

    for half in range(2):
        @pl.when(core == half)
        def _():
            step(half, mine_ref)
            step(1 - half, other_ref)


def call_adam(lay, halves, mine, other, states):
    names = tuple(states)
    flat = [a for name in names for a in states[name]]
    outs = [S(states[name][0].shape, t) for name in names for t in (f32, f32, f32, bf16)]
    got = pl.pallas_call(
        functools.partial(adam, lay, halves, names),
        in_specs=[whole(a) for a in (mine, other, *flat)], out_specs=[whole(a) for a in outs], out_shape=outs,
        compiler_params=params(60), cost_estimate=cost(3), name="adam",
    )(mine, other, *flat)
    return {name: got[4 * k:4 * k + 4] for k, name in enumerate(names)}


class Links:
    def __init__(self, mesh):
        self.wide, self.narrow = mesh.shape["wide"], mesh.shape["narrow"]
        bits = [1 << k for k in range(self.wide.bit_length() - 1)]
        self.orders = (bits[::-1], bits[:1] + bits[:0:-1])
        self.rounds = len(bits)
        self.masks = []
        for order in self.orders:
            masks = [0]
            for bit in order:
                masks = masks + [m ^ bit for m in masks]
            self.masks.append(masks)
        self.slots = [[masks.index(m) for m in range(self.wide)] for masks in self.masks]

    def permute(self, value, partner):
        pairs = []
        for n in range(self.narrow):
            for w in range(self.wide):
                n2, w2 = partner(n, w)
                pairs.append((n * self.wide + w, n2 * self.wide + w2))
        return lax.ppermute(value, ("narrow", "wide"), pairs)

    def core(self, value):
        return self.permute(value, lambda n, w: (n ^ 1, w))

    def step(self, value, k):
        return self.permute(value, lambda n, w: (n, w ^ self.orders[n % 2][k]))

    def others(self, value):
        total = value.astype(f32)
        bit = 2
        while bit < self.narrow:
            low = total.astype(bf16)
            total = low.astype(f32) + self.permute(low, lambda n, w, bit=bit: (n ^ bit, w)).astype(f32)
            bit *= 2
        return total

    def here(self):
        return lax.axis_index("wide"), lax.axis_index("narrow") % 2

    def gather(self, half):
        moving = Gather(self, half)
        for _ in range(self.rounds):
            moving.round()
        return moving.core()

    def reduce(self, keep, give):
        moving = Reduce(self, keep, give)
        moving.core()
        for _ in range(self.rounds):
            moving.round()
        moving.others()
        return moving.finish()


    def gather_rows(self, packed):
        me, core = self.here()
        rows, columns = packed.shape
        mine, other = self.gather(lax.dynamic_slice_in_dim(packed, core * (rows // 2), rows // 2))
        both = jnp.concatenate([mine, other], axis=0)
        relative = jnp.arange(self.wide) ^ me
        first = jnp.take(jnp.array(self.slots[0]), relative) + core * self.wide
        second = jnp.take(jnp.array(self.slots[1]), relative) + (1 - core) * self.wide
        index = jnp.stack([first, second], axis=1).reshape(-1)
        return jnp.take(both, index, axis=0).reshape(self.wide, rows, columns)

    def reduce_rows(self, packed):
        me, core = self.here()
        _, rows, columns = packed.shape
        halves = packed.reshape(2 * self.wide, rows // 2, columns)
        masks = jnp.array(self.masks)
        keep = jnp.take(halves, (masks[core] ^ me) * 2 + core, axis=0)
        give = jnp.take(halves, (masks[1 - core] ^ me) * 2 + (1 - core), axis=0)
        total, other = self.reduce(keep, give.astype(bf16))
        return jnp.where(core == 0, jnp.concatenate([total, other]), jnp.concatenate([other, total]))


class Gather:
    def __init__(self, links, half):
        self.links, self.held, self.k = links, half[None], 0

    def round(self):
        self.held = jnp.concatenate([self.held, self.links.step(self.held, self.k)], axis=0)
        self.k += 1

    def core(self):
        return self.held, self.links.core(self.held)


class Reduce:
    def __init__(self, links, keep, give):
        self.links, self.held, self.give, self.k = links, keep, give, links.rounds

    def core(self):
        self.held = self.held + self.links.core(self.give).astype(f32)

    def round(self):
        self.k -= 1
        half = self.held.shape[0] // 2
        self.held = self.held[:half] + self.links.step(self.held[half:].astype(bf16), self.k).astype(f32)

    def others(self):
        self.held = self.links.others(self.held[0])

    def finish(self):
        return self.held, self.links.core(self.held)


class Here:
    def __init__(self, held, other):
        self.held, self.other = held, other

    def round(self):
        pass

    def others(self):
        pass

    def core(self):
        return self.held, self.other

    finish = core


def to_rows(block, columns):
    return jnp.concatenate([block[..., j:j + columns] for j in range(0, block.shape[-1], columns)], axis=-2)


def from_rows(block, count):
    return jnp.concatenate(jnp.split(block, count, axis=-2), axis=-1)


def padded(block, multiple):
    extra = -block.shape[-2] % multiple
    return jnp.pad(block, [(0, 0)] * (block.ndim - 2) + [(0, extra), (0, 0)])


def to_slots(lay, halves, rows, arrays):
    out = []
    for half in halves:
        parts = []
        for name, start, count, col, _ in half:
            block = arrays[name].reshape(OWNERS, -1, arrays[name].shape[-1])
            parts.append(block[:, start:start + count, col * lay.d:(col + 1) * lay.d])
        block = jnp.concatenate(parts, axis=1)
        out.append(jnp.pad(block, ((0, 0), (0, rows - block.shape[1]), (0, 0))))
    return out


def from_slots(halves, both):
    found = {}
    for half, block in zip(halves, both):
        for name, start, count, col, at in half:
            found.setdefault(name, {})[(start, col)] = block[:, at:at + count].astype(f32)
    out = {}
    for name, parts in found.items():
        axis = 2 if max(col for _, col in parts) else 1
        block = jnp.concatenate([parts[key] for key in sorted(parts)], axis=axis)
        out[name] = block.reshape(-1, block.shape[-1])
    return out


FIRST_IMAGES = 2


def after(value, *earlier):
    return lax.optimization_barrier((value, *earlier))[0]


def compute(lay, x, cot, gather, reduce, rounds):
    b = x.shape[0]
    k = min(FIRST_IMAGES, b - 1)
    one, two = gather
    one.round()
    two.held = after(two.held, one.held)
    two.round()
    one.round()
    one.held, two.held = lax.optimization_barrier((one.held, two.held))
    for _ in range(rounds - 2):
        one.round()
    first = one.core()
    two.held, *first = lax.optimization_barrier((two.held, *first))
    *outs, wq, vrow, vcol = call_attn_fwd_first(lay, *first, x, k)
    for _ in range(rounds - 2):
        two.round()
    *outs, two.held = lax.optimization_barrier((*outs, two.held))
    jt, e, il, ot, h = call_attn_fwd_rest(x, wq, vrow, vcol, outs, k, b - k)
    two.round()
    ot, two.held = lax.optimization_barrier((ot, two.held))
    second = two.core()
    mid, act, dm, dot_, wd, dv, keep, give = call_mlp(lay, *second, x, ot, cot, vrow)
    down = reduce(keep, give)
    down.core()
    acts = (jt, e, il, ot, after(dot_, down.held), h)
    dj, dw = call_attn_bwd_first(acts, k)
    down.round()
    dw = after(dw, down.held)
    dj, keep, give = call_attn_bwd_last(lay, acts, dw, wq, vrow, dv, dj, k, b - k)
    for _ in range(rounds - 2):
        down.round()
    up = reduce(keep, give)
    up.core()
    dj, up.held = lax.optimization_barrier((dj, up.held))
    up.round()
    gx, lo = call_tail(x, dm, dj, wq, mid, act, wd, vrow)
    up.held = after(up.held, gx)
    for _ in range(rounds - 1):
        up.round()
    down.round()
    down.others()
    second_sum = down.finish()
    up.others()
    return lo, gx, up.finish(), second_sum


def eight_owners(links, lay, x, cot, states):
    masters = {name: s[0] for name, s in states.items()}
    first, second = call_pack(lay, *(masters[name] for name in "qpudv"))
    gather = Gather(links, first), Gather(links, second)
    lo, gx, first_sum, second_sum = compute(lay, x, cot, gather, functools.partial(Reduce, links), links.rounds)
    new = call_adam(lay, lay.second, *second_sum, {name: states[name] for name in "pud"})
    new |= call_adam(lay, lay.first, *first_sum, {name: states[name] for name in "qv"})
    return lo, gx, new


def any_owners(links, lay, x, cot, states):
    n, d = links.wide, lay.d
    masters = {name: s[0] for name, s in states.items()}
    v_size = masters["v"].shape[0]
    v_rows = -(-v_size // d)

    def vec_rows(v):
        return jnp.pad(v, ((0, 0), (0, v_rows * d - v_size))).reshape(-1, v_rows, d)

    def split(block):
        at, out = 0, {}
        for name in "qpu":
            rows = masters[name].shape[0]
            out[name] = block[:, at:at + rows]
            at += rows
        rows = masters["d"].shape[0]
        out["d"] = from_rows(block[:, at:at + rows * lay.cols], lay.cols)
        at += rows * lay.cols
        out["v"] = block[:, at:at + v_rows].reshape(-1, 1, v_rows * d)[:, :, :v_size]
        return {name: a.reshape(-1, a.shape[2]) for name, a in out.items()}

    def join(a, lead):
        blocks = [a[name].reshape(lead, -1, d) for name in "qpu"]
        blocks += [to_rows(a["d"].reshape(lead, -1, lay.ff), d), vec_rows(a["v"].reshape(lead, v_size))]
        return padded(jnp.concatenate(blocks, axis=1), 32)

    def eighths(v):
        return jnp.pad(v.reshape(OWNERS, 3, lay.piece), ((0, 0), (0, 13), (0, d - lay.piece))).reshape(-1, d)

    got = split(links.gather_rows(join(masters, 1)[0].astype(bf16)))
    got["v"] = eighths(got["v"])
    gather = Here(*to_slots(lay, lay.first, lay.first_rows, got)), Here(*to_slots(lay, lay.second, lay.second_rows, got))
    lo, gx, first_sum, second_sum = compute(lay, x, cot, gather, Here, 3)
    grads = from_slots(lay.first, first_sum) | from_slots(lay.second, second_sum)
    grads["v"] = grads["v"].reshape(OWNERS, 16, d)[:, :3, :lay.piece]
    mine = split(links.reduce_rows(join(grads, n))[None])
    rates = {"q": 0.6 * d ** -0.5, "p": 0.6 * d ** -0.5, "u": 0.6 * d ** -0.5, "d": 0.6 * lay.ff ** -0.5, "v": vector_rate}
    new = {}
    for name, refs in states.items():
        new[name] = adam_values(*refs, mine[name].reshape(refs[0].shape), rates[name], 0.0 if name == "v" else matrix_decay)
    return lo, gx, new


def per_device(links, x, cot, *arrays):
    if links.wide == OWNERS:
        run, masks, position = eight_owners, links.masks, links.here
    else:
        run, masks, position = any_owners, [list(range(OWNERS))] * 2, lambda: (0, 0)
    lay = Layout(x.shape[2], arrays[3].shape[1], masks, position)
    names = "qpudv"
    states = {name: arrays[k::5] for k, name in enumerate(names)}
    lo, gx, new = run(links, lay, x, cot, states)
    return (lo, gx, *(a for name in names for a in new[name]))


def solution(mesh):
    tokens = P(("narrow", "wide"), None, None)
    matrix, vector = P("wide", None), P("wide")
    state = (matrix,) * 4 + (vector,)
    return jax.shard_map(
        functools.partial(per_device, Links(mesh)),
        mesh=mesh,
        in_specs=(tokens, tokens) + state * 3,
        out_specs=(tokens, tokens) + (matrix,) * 16 + (vector,) * 4,
        check_vma=False,
    )
```

```python
import functools

import jax
import jax.numpy as jnp
from jax import lax
from jax.experimental import pallas as pl
from jax.experimental.pallas import tpu as pltpu
from jax.sharding import PartitionSpec as P

STEP = 10
HEADS = 6
EPS = 1e-6
OWNERS = 8
MLP_MIB = 26
beta_first = 0.5
beta_second = 0.5
adam_eps = 1e-08
matrix_decay = 0.01
vector_rate = 0.3
bf16, f32 = jnp.bfloat16, jnp.float32
S = jax.ShapeDtypeStruct
ANY = pl.BlockSpec(memory_space=pl.ANY)
HBM = pl.BlockSpec(memory_space=pltpu.HBM)


def dot(a, b, ca, cb):
    return lax.dot_general(a, b, (((ca,), (cb,)), ((), ())), preferred_element_type=f32)


def norm_stats(v):
    mean = jnp.mean(v, axis=-1, keepdims=True)
    cen = v - mean
    var = jnp.mean(cen * cen, axis=-1, keepdims=True)
    rstd = lax.rsqrt(var + EPS)
    return cen * rstd, rstd


def one(*shape, off=0):
    return pl.BlockSpec((1,) + shape, lambda i: (i + off,) + (0,) * len(shape))


def full(a):
    return pl.BlockSpec(a.shape, lambda i: (0,) * len(a.shape))


def whole(a):
    return pl.BlockSpec(a.shape, lambda: (0,) * len(a.shape))


def params(mib):
    return pltpu.CompilerParams(vmem_limit_bytes=mib << 20)


def cost(us):
    return pl.CostEstimate(flops=int(us * 1.0e9), bytes_accessed=1 << 20, transcendentals=0)


class Layout:
    def __init__(self, d, ff, orders, position):
        self.d, self.ff, self.cols = d, ff, ff // d
        self.position = position
        self.masks = [[sum(bit for k, bit in enumerate(order) if j >> k & 1) for j in range(OWNERS)] for order in orders]
        self.q, self.p, self.u = 3 * d // OWNERS, d // OWNERS, ff // OWNERS
        q0 = (self.q // 2 + 15) // 16 * 16
        self.first = ((("q", 0, q0, 0, 0),), (("q", q0, self.q - q0, 0, 0), ("v", 0, 16, 0, self.q - q0)))
        self.first_rows = max(q0, self.q - q0 + 16)
        p0 = 16
        down = tuple(("d", 0, self.p, j, j * self.p) for j in range(self.cols))
        self.second = (
            (("u", 0, self.u, 0, 0), ("p", 0, p0, 0, self.u)),
            down + (("p", p0, self.p - p0, 0, self.cols * self.p),),
        )
        self.second_rows = max(self.u + p0, self.cols * self.p + self.p - p0)
        self.piece = (8 * d + ff) // (3 * OWNERS)


def place(lay, piece, owner):
    name, start, rows, col, _ = piece
    size = {"q": lay.q, "p": lay.p, "u": lay.u, "d": lay.p, "v": 16}[name]
    at = owner * size + start
    if not isinstance(at, int):
        at = pl.multiple_of(at, 16)
    return pl.ds(at, rows), pl.ds(col * lay.d, lay.d)


def pack(lay, q_hbm, p_hbm, u_hbm, d_hbm, v_hbm, first_ref, second_ref, q_ref, p_ref, u_ref, d_ref, v_ref, sems):
    refs = {"q": q_ref, "p": p_ref, "u": u_ref, "d": d_ref}
    moves = [pltpu.make_async_copy(a, b, sems.at[i]) for i, (a, b) in enumerate(
        ((q_hbm, q_ref), (v_hbm, v_ref), (p_hbm, p_ref), (u_hbm, u_ref), (d_hbm, d_ref)))]
    for move in moves:
        move.start()
    for move in moves:
        move.wait()
    core = lay.position()[1]
    v = v_ref[...].reshape(1, v_ref.shape[0])

    def fill(halves, out_ref):
        end = 0
        for name, start, rows, col, at in halves:
            if name == "v":
                out_ref[at:at + rows, :] = jnp.zeros((rows, lay.d), bf16)
                for k in range(3):
                    out_ref[at + k:at + k + 1, :lay.piece] = v[:, k * lay.piece:(k + 1) * lay.piece].astype(bf16)
            else:
                out_ref[at:at + rows, :] = refs[name][start:start + rows, col * lay.d:(col + 1) * lay.d].astype(bf16)
            end = at + rows
        if end < out_ref.shape[0]:
            out_ref[end:, :] = jnp.zeros((out_ref.shape[0] - end, lay.d), bf16)

    for half in range(2):
        @pl.when(core == half)
        def _():
            fill(lay.first[half], first_ref)
            fill(lay.second[half], second_ref)


def call_pack(lay, q, p, u, d, v):
    outs = [S((lay.first_rows, lay.d), bf16), S((lay.second_rows, lay.d), bf16)]
    return pl.pallas_call(
        functools.partial(pack, lay), in_specs=[HBM] * 5,
        out_specs=[whole(a) for a in outs], out_shape=outs,
        scratch_shapes=[pltpu.VMEM(a.shape, f32) for a in (q, p, u, d, v)] + [pltpu.SemaphoreType.DMA((5,))],
        compiler_params=params(60), name="pack",
    )(q, p, u, d, v)


def fetch(lay, halves, mine_ref, other_ref, dests, sems):
    me, core = lay.position()

    def copies(half, src_ref, base):
        out = []
        for j in range(OWNERS):
            for piece in halves[half]:
                name, _, rows, _, at = piece
                r, c = place(lay, piece, me ^ lay.masks[half][j])
                dst = dests[name].at[r] if name != "d" else dests[name].at[r, c]
                out.append(pltpu.make_async_copy(src_ref.at[j, pl.ds(at, rows)], dst, sems.at[base + len(out)]))
        return out

    for half in range(2):
        @pl.when(core == half)
        def _():
            first = copies(half, mine_ref, 0)
            both = first + copies(1 - half, other_ref, len(first))
            for c in both:
                c.start()
            for c in both:
                c.wait()


def emit(lay, halves, arrays, keep_ref, give_ref):
    me, core = lay.position()

    def fill(half, out_ref):
        for j in range(OWNERS):
            end = 0
            for piece in halves[half]:
                name, _, rows, _, at = piece
                r, c = place(lay, piece, me ^ lay.masks[half][j])
                out_ref[j, at:at + rows, :] = arrays[name][r, c].astype(out_ref.dtype)
                end = at + rows
            if end < out_ref.shape[1]:
                out_ref[j, end:, :] = jnp.zeros((out_ref.shape[1] - end, lay.d), out_ref.dtype)

    for half in range(2):
        @pl.when(core == half)
        def _():
            fill(half, keep_ref)
            fill(1 - half, give_ref)


def attn_fwd_image(x_ref, w_ref, vrow_ref, vcol_ref, jt_ref, e_ref, il_ref, ot_ref, h_ref):
    xhat, _ = norm_stats(x_ref[0])
    h = (xhat * vrow_ref[0:1, :] + vrow_ref[1:2, :]).astype(bf16)
    h_ref[0] = h
    d = h.shape[1]
    hs = d // HEADS
    jt = dot(w_ref[...], h, 1, 1) + vcol_ref[:, 0:1]
    jt_ref[0] = jt.astype(bf16)
    for i in range(HEADS):
        qt = jt_ref[0, i * hs:(i + 1) * hs, :]
        kt = jt_ref[0, d + i * hs:d + (i + 1) * hs, :]
        vt = jt_ref[0, 2 * d + i * hs:2 * d + (i + 1) * hs, :]
        st = dot((kt * 0.125), qt, 0, 0)
        m = jnp.max(st, axis=0, keepdims=True)
        e = jnp.exp(st - m)
        l = jnp.sum(e, axis=0, keepdims=True)
        eb = e.astype(bf16)
        e_ref[0, i] = eb
        il = 1.0 / l
        il_ref[0, i:i + 1, :] = il
        ot = dot(vt, eb, 1, 0) * il
        ot_ref[0, i * hs:(i + 1) * hs, :] = ot.astype(bf16)


def attn_fwd_first(lay, mine_ref, other_ref, x_ref, jt_ref, e_ref, il_ref, ot_ref, h_ref, w_ref, vrow_ref, vcol_ref, vec_scr, sems):
    @pl.when(pl.program_id(0) == 0)
    def _():
        fetch(lay, lay.first, mine_ref, other_ref, {"q": w_ref, "v": vec_scr}, sems)
        d, s = lay.d, lay.piece
        vrow_ref[...] = jnp.zeros_like(vrow_ref)
        for r in range(8 + lay.cols):
            for k in range(2):
                g = 2 * r + k
                row = vec_scr[g // 3 * 16:g // 3 * 16 + 16, :].astype(f32)[g % 3:g % 3 + 1, :s]
                vrow_ref[r:r + 1, k * s:(k + 1) * s] = row
        cols = jnp.transpose(vrow_ref[0:8, :])
        vcol_ref[...] = jnp.zeros_like(vcol_ref)
        vcol_ref[0:d, 0:1] = cols[:, 4:5]
        vcol_ref[2 * d:3 * d, 0:1] = cols[:, 5:6]
    attn_fwd_image(x_ref, w_ref, vrow_ref, vcol_ref, jt_ref, e_ref, il_ref, ot_ref, h_ref)


def attn_fwd_rest(x_ref, w_ref, vrow_ref, vcol_ref, a, b, c, d, e, jt_ref, e_ref, il_ref, ot_ref, h_ref):
    attn_fwd_image(x_ref, w_ref, vrow_ref, vcol_ref, jt_ref, e_ref, il_ref, ot_ref, h_ref)


def fwd_outs(b, t, d):
    return [S((b, 3 * d, t), bf16), S((b, HEADS, t, t), bf16), S((b, 8, t), f32), S((b, d, t), bf16), S((b, t, d), bf16)]


def fwd_blocks(t, d, off):
    return [one(3 * d, t, off=off), one(HEADS, t, t, off=off), one(8, t, off=off), one(d, t, off=off), one(t, d, off=off)]


def call_attn_fwd_first(lay, mine, other, x, count):
    b, t, d = x.shape
    extra = [S((3 * d, d), bf16), S((16, d), f32), S((3 * d, 8), f32)]
    n_copies = OWNERS * (len(lay.first[0]) + len(lay.first[1]))
    return pl.pallas_call(
        functools.partial(attn_fwd_first, lay), grid=(count,),
        in_specs=[HBM, HBM, one(t, d)],
        out_specs=fwd_blocks(t, d, 0) + [full(a) for a in extra],
        out_shape=fwd_outs(b, t, d) + extra,
        scratch_shapes=[pltpu.VMEM((OWNERS * 16, d), bf16), pltpu.SemaphoreType.DMA((n_copies,))],
        compiler_params=params(24), cost_estimate=cost(4 * count), name="attn_fwd_first",
    )(mine, other, x)


def call_attn_fwd_rest(x, w, vrow, vcol, outs, off, count):
    b, t, d = x.shape
    return pl.pallas_call(
        attn_fwd_rest, grid=(count,),
        in_specs=[one(t, d, off=off), full(w), full(vrow), full(vcol)] + [ANY] * 5,
        out_specs=fwd_blocks(t, d, off), out_shape=fwd_outs(b, t, d),
        input_output_aliases={4 + k: k for k in range(5)},
        compiler_params=params(24), cost_estimate=cost(4 * count), name="attn_fwd_rest",
    )(x, w, vrow, vcol, *outs)


def gelu_pair(u):
    cdf = 0.5 + 0.5 * lax.erf(u * (0.5 ** 0.5))
    pdf = jnp.exp(u * u * -0.5) * 0.3989422804014327
    return u * cdf, cdf + u * pdf


def mlp(lay, count, mine_ref, other_ref, x_ref, ot_ref, cot_ref, vrow_ref,
        mid_ref, act_ref, dm_ref, dot_ref, wd_ref, dv_ref, keep_ref, give_ref,
        wp_ref, wu_ref, dwp_ref, dwu_ref, dwd_ref, sems):
    i = pl.program_id(0)
    d, cols = lay.d, lay.cols

    @pl.when(i == 0)
    def _():
        fetch(lay, lay.second, mine_ref, other_ref, {"p": wp_ref, "u": wu_ref, "d": wd_ref}, sems)
        dwp_ref[...] = jnp.zeros_like(dwp_ref)
        dwu_ref[...] = jnp.zeros_like(dwu_ref)
        dwd_ref[...] = jnp.zeros_like(dwd_ref)
        dv_ref[...] = jnp.zeros_like(dv_ref)

    ot = ot_ref[0]
    mid = x_ref[0] + (dot(ot, wp_ref[...], 0, 1) + vrow_ref[6:7, :])
    mid_ref[0] = mid
    xhat, rstd = norm_stats(mid)
    h2 = (xhat * vrow_ref[2:3, :] + vrow_ref[3:4, :]).astype(bf16)
    ub = jnp.concatenate([vrow_ref[8 + j:9 + j, :] for j in range(cols)], axis=1)
    u = dot(h2, wu_ref[...], 1, 1) + ub
    act, gp = gelu_pair(u)
    act = act.astype(bf16)
    act_ref[0] = act
    cot = cot_ref[0]
    g = cot.astype(bf16)
    dwd_ref[...] += dot(g, act, 0, 0)
    du = dot(g, wd_ref[...], 1, 0) * gp
    dul = du.astype(bf16)
    dwu_ref[...] += dot(dul, h2, 0, 0)
    dh2 = dot(dul, wu_ref[...], 1, 0)
    gy = dh2 * vrow_ref[2:3, :]
    m1 = jnp.mean(gy, axis=-1, keepdims=True)
    m2 = jnp.mean(gy * xhat, axis=-1, keepdims=True)
    dm = cot + rstd * (gy - m1 - xhat * m2)
    dm_ref[0] = dm
    dml = dm.astype(bf16)
    dwp_ref[...] += dot(dml, ot, 0, 1)
    dot_ref[0] = dot(wp_ref[...], dml, 0, 1).astype(bf16)
    dv_ref[2:3, :] += jnp.sum(dh2 * xhat, axis=0, keepdims=True)
    dv_ref[3:4, :] += jnp.sum(dh2, axis=0, keepdims=True)
    dv_ref[6:7, :] += jnp.sum(dml.astype(f32), axis=0, keepdims=True)
    dv_ref[7:8, :] += jnp.sum(g.astype(f32), axis=0, keepdims=True)
    dub = jnp.sum(dul.astype(f32), axis=0, keepdims=True)
    for j in range(cols):
        dv_ref[8 + j:9 + j, :] += dub[:, j * d:(j + 1) * d]

    @pl.when(i == count - 1)
    def _():
        emit(lay, lay.second, {"p": dwp_ref, "u": dwu_ref, "d": dwd_ref}, keep_ref, give_ref)


def call_mlp(lay, mine, other, x, ot, cot, vrow):
    b, t, d = x.shape
    ff = lay.ff
    hbm = pltpu.HBM
    acc = [hbm((d, ff), bf16), S((16, d), f32), hbm((OWNERS, lay.second_rows, d), f32), S((OWNERS, lay.second_rows, d), bf16)]
    outs = [hbm((b, t, d), f32), hbm((b, t, ff), bf16), hbm((b, t, d), f32), S((b, d, t), bf16)] + acc
    n_copies = OWNERS * (len(lay.second[0]) + len(lay.second[1]))
    return pl.pallas_call(
        functools.partial(mlp, lay, b), grid=(b,),
        in_specs=[HBM, HBM, one(t, d), one(d, t), one(t, d), full(vrow)],
        out_specs=[one(t, d), one(t, ff), one(t, d), one(d, t)] + [full(a) for a in acc],
        out_shape=outs,
        scratch_shapes=[pltpu.VMEM((d, d), bf16), pltpu.VMEM((ff, d), bf16), pltpu.VMEM((d, d), f32), pltpu.VMEM((ff, d), f32),
                        pltpu.VMEM((d, ff), f32), pltpu.SemaphoreType.DMA((n_copies,))],
        compiler_params=params(MLP_MIB), cost_estimate=cost(24), name="mlp",
    )(mine, other, x, ot, cot, vrow)


def attn_bwd_image(jt_ref, e_ref, il_ref, ot_ref, dot_ref, h_ref, dj_ref, dw_ref):
    t, d = h_ref.shape[1:]
    hs = d // HEADS
    for i in range(HEADS):
        rows = slice(i * hs, (i + 1) * hs)
        qt = jt_ref[0, i * hs:(i + 1) * hs, :]
        kt = jt_ref[0, d + i * hs:d + (i + 1) * hs, :]
        vt = jt_ref[0, 2 * d + i * hs:2 * d + (i + 1) * hs, :]
        do = dot_ref[0, rows, :].astype(f32) * il_ref[0, i:i + 1, :]
        dd = jnp.sum(do * ot_ref[0, rows, :].astype(f32), axis=0, keepdims=True)
        dob = do.astype(bf16)
        eb = e_ref[0, i]
        dp = dot(vt, dob, 0, 0)
        ds = (eb.astype(f32) * (dp - dd)).astype(bf16)
        dj_ref[0, rows, :] = (dot(kt, ds, 1, 0) * 0.125).astype(bf16)
        dj_ref[0, d + i * hs:d + (i + 1) * hs, :] = (dot(qt, ds, 1, 1) * 0.125).astype(bf16)
        dj_ref[0, 2 * d + i * hs:2 * d + (i + 1) * hs, :] = dot(dob, eb, 1, 1).astype(bf16)
    hx = jnp.concatenate([h_ref[0], jnp.ones((t, 128), bf16)], axis=1)
    dw_ref[...] += dot(dj_ref[0], hx, 1, 0)


def attn_bwd_first(jt_ref, e_ref, il_ref, ot_ref, dot_ref, h_ref, dj_ref, dw_ref):
    @pl.when(pl.program_id(0) == 0)
    def _():
        dw_ref[...] = jnp.zeros_like(dw_ref)
    attn_bwd_image(jt_ref, e_ref, il_ref, ot_ref, dot_ref, h_ref, dj_ref, dw_ref)


def attn_bwd_last(lay, count, jt_ref, e_ref, il_ref, ot_ref, dot_ref, h_ref, dw_in_ref, w_ref, vrow_ref, dv_ref, dj_in_ref,
                  dj_ref, keep_ref, give_ref, dw_ref, vec_scr):
    i = pl.program_id(0)

    @pl.when(i == 0)
    def _():
        dw_ref[...] = dw_in_ref[...]
    attn_bwd_image(jt_ref, e_ref, il_ref, ot_ref, dot_ref, h_ref, dj_ref, dw_ref)

    @pl.when(i == count - 1)
    def _():
        d, s = lay.d, lay.piece
        w = w_ref[...].astype(f32)
        db = dw_ref[:, d:d + 1]
        gain = jnp.sum(w * (dw_ref[:, 0:d] - db * vrow_ref[1:2, :]), axis=0, keepdims=True) / vrow_ref[0:1, :]
        shift = jnp.sum(w * db, axis=0, keepdims=True)
        biases = jnp.transpose(dw_ref[:, d:d + 8])
        rows = [gain, shift, dv_ref[2:3, :], dv_ref[3:4, :], biases[0:1, 0:d], biases[0:1, 2 * d:3 * d]]
        rows += [dv_ref[k:k + 1, :] for k in range(6, 8 + lay.cols)]
        vec_scr[...] = jnp.zeros_like(vec_scr)
        for g in range(3 * OWNERS):
            at = g // 3 * 16 + g % 3
            vec_scr[at:at + 1, 0:s] = rows[g // 2][:, g % 2 * s:(g % 2 + 1) * s]
        emit(lay, lay.first, {"q": dw_ref, "v": vec_scr}, keep_ref, give_ref)


def bwd_blocks(t, d, off):
    return [one(3 * d, t, off=off), one(HEADS, t, t, off=off), one(8, t, off=off), one(d, t, off=off), one(d, t, off=off), one(t, d, off=off)]


def call_attn_bwd_first(acts, count):
    b, t, d = acts[-1].shape
    dw = S((3 * d, d + 128), f32)
    return pl.pallas_call(
        attn_bwd_first, grid=(count,), in_specs=bwd_blocks(t, d, 0),
        out_specs=[one(3 * d, t), full(dw)], out_shape=[S((b, 3 * d, t), bf16), dw],
        compiler_params=params(24), cost_estimate=cost(4 * count), name="attn_bwd_first",
    )(*acts)


def call_attn_bwd_last(lay, acts, dw, w, vrow, dv, dj, off, count):
    b, t, d = acts[-1].shape
    slots = [S((OWNERS, lay.first_rows, d), f32), S((OWNERS, lay.first_rows, d), bf16)]
    return pl.pallas_call(
        functools.partial(attn_bwd_last, lay, count), grid=(count,),
        in_specs=bwd_blocks(t, d, off) + [full(dw), full(w), full(vrow), full(dv), ANY],
        out_specs=[one(3 * d, t, off=off)] + [full(a) for a in slots], out_shape=[S((b, 3 * d, t), bf16)] + slots,
        scratch_shapes=[pltpu.VMEM(dw.shape, f32), pltpu.VMEM((OWNERS * 16, d), f32)],
        input_output_aliases={10: 0},
        compiler_params=params(28), cost_estimate=cost(4 * count + 2), name="attn_bwd_last",
    )(*acts, dw, w, vrow, dv, dj)


def layer_end(mid_ref, act_ref, wd_ref, vrow_ref, lo_ref):
    lo_ref[0] = mid_ref[0] + (dot(act_ref[0], wd_ref[...], 1, 1) + vrow_ref[7:8, :])


def call_layer_end(mid, act, wd, vrow):
    b, t, d = mid.shape
    return pl.pallas_call(
        layer_end, grid=(b,), in_specs=[one(t, d), one(t, act.shape[2]), full(wd), full(vrow)],
        out_specs=one(t, d), out_shape=S((b, t, d), f32),
        compiler_params=params(16), cost_estimate=cost(4), name="layer_end",
    )(mid, act, wd, vrow)


def input_end(x_ref, dm_ref, dj_ref, w_ref, vrow_ref, gx_ref):
    dh = dot(dj_ref[0], w_ref[...], 0, 0)
    xhat, rstd = norm_stats(x_ref[0])
    gy = dh * vrow_ref[0:1, :]
    m1 = jnp.mean(gy, axis=-1, keepdims=True)
    m2 = jnp.mean(gy * xhat, axis=-1, keepdims=True)
    gx_ref[0] = dm_ref[0] + rstd * (gy - m1 - xhat * m2)


def call_input_end(x, dm, dj, w, vrow):
    b, t, d = x.shape
    return pl.pallas_call(
        input_end, grid=(b,), in_specs=[one(t, d), one(t, d), one(3 * d, t), full(w), full(vrow)],
        out_specs=one(t, d), out_shape=S((b, t, d), f32),
        compiler_params=params(16), cost_estimate=cost(4), name="input_end",
    )(x, dm, dj, w, vrow)


def adam_values(master, first, second, grad, rate, decay):
    first_new = beta_first * first + (1.0 - beta_first) * grad
    second_new = beta_second * second + (1.0 - beta_second) * grad * grad
    first_hat = first_new * (1.0 / (1.0 - beta_first ** STEP))
    second_hat = second_new * (1.0 / (1.0 - beta_second ** STEP))
    new = master - rate * (first_hat / (jnp.sqrt(second_hat) + adam_eps) + decay * master)
    return new, first_new, second_new, new.astype(bf16)


def adam_rows(refs, outs, rows, grad, rate, decay):
    for out, value in zip(outs, adam_values(*(r[rows] for r in refs), grad, rate, decay)):
        out[rows] = value


def adam(lay, halves, names, mine_ref, other_ref, *refs):
    core = lay.position()[1]
    count = len(names)
    states = {name: refs[3 * k:3 * k + 3] for k, name in enumerate(names)}
    outs = {name: refs[3 * count + 4 * k:3 * count + 4 * k + 4] for k, name in enumerate(names)}
    rates = {"q": 0.6 * lay.d ** -0.5, "p": 0.6 * lay.d ** -0.5, "u": 0.6 * lay.d ** -0.5, "d": 0.6 * lay.ff ** -0.5, "v": vector_rate}

    def step(half, src_ref):
        for name, start, rows, col, at in halves[half]:
            if name == "v":
                grad = jnp.concatenate([src_ref[at + k:at + k + 1, :lay.piece] for k in range(3)], axis=1)
                size = 3 * lay.piece
                new = adam_values(*(r[...].reshape(1, size) for r in states[name]), grad, rates[name], 0.0)
                for out, value in zip(outs[name], new):
                    out[...] = value.reshape(size)
            else:
                span = (slice(start, start + rows), slice(col * lay.d, (col + 1) * lay.d))
                adam_rows(states[name], outs[name], span, src_ref[at:at + rows, :], rates[name], matrix_decay)

    for half in range(2):
        @pl.when(core == half)
        def _():
            step(half, mine_ref)
            step(1 - half, other_ref)


def call_adam(lay, halves, mine, other, states):
    names = tuple(states)
    flat = [a for name in names for a in states[name]]
    outs = [S(states[name][0].shape, t) for name in names for t in (f32, f32, f32, bf16)]
    got = pl.pallas_call(
        functools.partial(adam, lay, halves, names),
        in_specs=[whole(a) for a in (mine, other, *flat)], out_specs=[whole(a) for a in outs], out_shape=outs,
        compiler_params=params(16), cost_estimate=cost(3), name="adam",
    )(mine, other, *flat)
    return {name: got[4 * k:4 * k + 4] for k, name in enumerate(names)}


class Links:
    def __init__(self, mesh):
        self.wide, self.narrow = mesh.shape["wide"], mesh.shape["narrow"]
        bits = [1 << k for k in range(self.wide.bit_length() - 1)]
        self.orders = (bits[::-1], bits[:1] + bits[:0:-1])
        self.rounds = len(bits)
        self.masks = []
        for order in self.orders:
            masks = [0]
            for bit in order:
                masks = masks + [m ^ bit for m in masks]
            self.masks.append(masks)
        self.slots = [[masks.index(m) for m in range(self.wide)] for masks in self.masks]

    def permute(self, value, partner):
        pairs = []
        for n in range(self.narrow):
            for w in range(self.wide):
                n2, w2 = partner(n, w)
                pairs.append((n * self.wide + w, n2 * self.wide + w2))
        return lax.ppermute(value, ("narrow", "wide"), pairs)

    def core(self, value):
        return self.permute(value, lambda n, w: (n ^ 1, w))

    def step(self, value, k):
        return self.permute(value, lambda n, w: (n, w ^ self.orders[n % 2][k]))

    def others(self, value):
        total = value.astype(f32)
        bit = 2
        while bit < self.narrow:
            low = total.astype(bf16)
            total = low.astype(f32) + self.permute(low, lambda n, w, bit=bit: (n ^ bit, w)).astype(f32)
            bit *= 2
        return total

    def here(self):
        return lax.axis_index("wide"), lax.axis_index("narrow") % 2

    def gather(self, half):
        moving = Gather(self, half)
        for _ in range(self.rounds):
            moving.round()
        return moving.core()

    def reduce(self, keep, give):
        moving = Reduce(self, keep, give)
        moving.core()
        for _ in range(self.rounds):
            moving.round()
        moving.others()
        return moving.finish()


    def gather_rows(self, packed):
        me, core = self.here()
        rows, columns = packed.shape
        mine, other = self.gather(lax.dynamic_slice_in_dim(packed, core * (rows // 2), rows // 2))
        both = jnp.concatenate([mine, other], axis=0)
        relative = jnp.arange(self.wide) ^ me
        first = jnp.take(jnp.array(self.slots[0]), relative) + core * self.wide
        second = jnp.take(jnp.array(self.slots[1]), relative) + (1 - core) * self.wide
        index = jnp.stack([first, second], axis=1).reshape(-1)
        return jnp.take(both, index, axis=0).reshape(self.wide, rows, columns)

    def reduce_rows(self, packed):
        me, core = self.here()
        _, rows, columns = packed.shape
        halves = packed.reshape(2 * self.wide, rows // 2, columns)
        masks = jnp.array(self.masks)
        keep = jnp.take(halves, (masks[core] ^ me) * 2 + core, axis=0)
        give = jnp.take(halves, (masks[1 - core] ^ me) * 2 + (1 - core), axis=0)
        total, other = self.reduce(keep, give.astype(bf16))
        return jnp.where(core == 0, jnp.concatenate([total, other]), jnp.concatenate([other, total]))


class Gather:
    def __init__(self, links, half):
        self.links, self.held, self.k = links, half[None], 0

    def round(self):
        self.held = jnp.concatenate([self.held, self.links.step(self.held, self.k)], axis=0)
        self.k += 1

    def core(self):
        return self.held, self.links.core(self.held)


class Reduce:
    def __init__(self, links, keep, give):
        self.links, self.held, self.give, self.k = links, keep, give, links.rounds

    def core(self):
        self.held = self.held + self.links.core(self.give).astype(f32)

    def round(self):
        self.k -= 1
        half = self.held.shape[0] // 2
        self.held = self.held[:half] + self.links.step(self.held[half:].astype(bf16), self.k).astype(f32)

    def others(self):
        self.held = self.links.others(self.held[0])

    def finish(self):
        return self.held, self.links.core(self.held)


class Here:
    def __init__(self, held, other):
        self.held, self.other = held, other

    def round(self):
        pass

    def others(self):
        pass

    def core(self):
        return self.held, self.other

    finish = core


def to_rows(block, columns):
    return jnp.concatenate([block[..., j:j + columns] for j in range(0, block.shape[-1], columns)], axis=-2)


def from_rows(block, count):
    return jnp.concatenate(jnp.split(block, count, axis=-2), axis=-1)


def padded(block, multiple):
    extra = -block.shape[-2] % multiple
    return jnp.pad(block, [(0, 0)] * (block.ndim - 2) + [(0, extra), (0, 0)])


def to_slots(lay, halves, rows, arrays):
    out = []
    for half in halves:
        parts = []
        for name, start, count, col, _ in half:
            block = arrays[name].reshape(OWNERS, -1, arrays[name].shape[-1])
            parts.append(block[:, start:start + count, col * lay.d:(col + 1) * lay.d])
        block = jnp.concatenate(parts, axis=1)
        out.append(jnp.pad(block, ((0, 0), (0, rows - block.shape[1]), (0, 0))))
    return out


def from_slots(halves, both):
    found = {}
    for half, block in zip(halves, both):
        for name, start, count, col, at in half:
            found.setdefault(name, {})[(start, col)] = block[:, at:at + count].astype(f32)
    out = {}
    for name, parts in found.items():
        axis = 2 if max(col for _, col in parts) else 1
        block = jnp.concatenate([parts[key] for key in sorted(parts)], axis=axis)
        out[name] = block.reshape(-1, block.shape[-1])
    return out


FIRST_IMAGES = 2


def after(value, *earlier):
    return lax.optimization_barrier((value, *earlier))[0]


def compute(lay, x, cot, gather, reduce, finish_second, rounds):
    b = x.shape[0]
    k = min(FIRST_IMAGES, b - 1)
    one, two = gather
    one.round()
    two.held = after(two.held, one.held)
    two.round()
    for _ in range(rounds - 1):
        one.round()
    one.held, two.held = lax.optimization_barrier((one.held, two.held))
    first = one.core()
    two.held, *first = lax.optimization_barrier((two.held, *first))
    *outs, wq, vrow, vcol = call_attn_fwd_first(lay, *first, x, k)
    for _ in range(rounds - 2):
        two.round()
    *outs, two.held = lax.optimization_barrier((*outs, two.held))
    jt, e, il, ot, h = call_attn_fwd_rest(x, wq, vrow, vcol, outs, k, b - k)
    two.round()
    ot, two.held = lax.optimization_barrier((ot, two.held))
    second = two.core()
    mid, act, dm, dot_, wd, dv, keep, give = call_mlp(lay, *second, x, ot, cot, vrow)
    down = reduce(keep, give)
    down.core()
    acts = (jt, e, il, ot, after(dot_, down.held), h)
    dj, dw = call_attn_bwd_first(acts, k)
    down.round()
    dw, down.held = lax.optimization_barrier((dw, down.held))
    dj, keep, give = call_attn_bwd_last(lay, acts, dw, wq, vrow, dv, dj, k, b - k)
    for _ in range(rounds - 2):
        down.round()
    up = reduce(keep, give)
    up.core()
    dj, up.held = lax.optimization_barrier((dj, up.held))
    up.round()
    gx = call_input_end(x, dm, dj, wq, vrow)
    gx, up.held = lax.optimization_barrier((gx, up.held))
    lo = call_layer_end(after(mid, gx), act, wd, vrow)
    up.round()
    lo, up.held = lax.optimization_barrier((lo, up.held))
    for _ in range(rounds - 2):
        up.round()
    down.round()
    down.others()
    second_new = finish_second(*down.finish())
    up.others()
    return lo, gx, up.finish(), second_new


def eight_owners(links, lay, x, cot, states):
    masters = {name: s[0] for name, s in states.items()}
    first, second = call_pack(lay, *(masters[name] for name in "qpudv"))
    gather = Gather(links, first), Gather(links, second)

    def finish_second(mine, other):
        return call_adam(lay, lay.second, mine, other, {name: states[name] for name in "pud"})

    lo, gx, first_sum, new = compute(lay, x, cot, gather, functools.partial(Reduce, links), finish_second, links.rounds)
    new |= call_adam(lay, lay.first, *first_sum, {name: states[name] for name in "qv"})
    return lo, gx, new


def any_owners(links, lay, x, cot, states):
    n, d = links.wide, lay.d
    masters = {name: s[0] for name, s in states.items()}
    v_size = masters["v"].shape[0]
    v_rows = -(-v_size // d)

    def vec_rows(v):
        return jnp.pad(v, ((0, 0), (0, v_rows * d - v_size))).reshape(-1, v_rows, d)

    def split(block):
        at, out = 0, {}
        for name in "qpu":
            rows = masters[name].shape[0]
            out[name] = block[:, at:at + rows]
            at += rows
        rows = masters["d"].shape[0]
        out["d"] = from_rows(block[:, at:at + rows * lay.cols], lay.cols)
        at += rows * lay.cols
        out["v"] = block[:, at:at + v_rows].reshape(-1, 1, v_rows * d)[:, :, :v_size]
        return {name: a.reshape(-1, a.shape[2]) for name, a in out.items()}

    def join(a, lead):
        blocks = [a[name].reshape(lead, -1, d) for name in "qpu"]
        blocks += [to_rows(a["d"].reshape(lead, -1, lay.ff), d), vec_rows(a["v"].reshape(lead, v_size))]
        return padded(jnp.concatenate(blocks, axis=1), 32)

    def eighths(v):
        return jnp.pad(v.reshape(OWNERS, 3, lay.piece), ((0, 0), (0, 13), (0, d - lay.piece))).reshape(-1, d)

    got = split(links.gather_rows(join(masters, 1)[0].astype(bf16)))
    got["v"] = eighths(got["v"])
    gather = Here(*to_slots(lay, lay.first, lay.first_rows, got)), Here(*to_slots(lay, lay.second, lay.second_rows, got))
    lo, gx, first_sum, second_sum = compute(lay, x, cot, gather, Here, lambda *both: both, 3)
    grads = from_slots(lay.first, first_sum) | from_slots(lay.second, second_sum)
    grads["v"] = grads["v"].reshape(OWNERS, 16, d)[:, :3, :lay.piece]
    mine = split(links.reduce_rows(join(grads, n))[None])
    rates = {"q": 0.6 * d ** -0.5, "p": 0.6 * d ** -0.5, "u": 0.6 * d ** -0.5, "d": 0.6 * lay.ff ** -0.5, "v": vector_rate}
    new = {}
    for name, refs in states.items():
        new[name] = adam_values(*refs, mine[name].reshape(refs[0].shape), rates[name], 0.0 if name == "v" else matrix_decay)
    return lo, gx, new


def per_device(links, x, cot, *arrays):
    if links.wide == OWNERS:
        run, orders, position = eight_owners, links.orders, links.here
    else:
        run, orders, position = any_owners, [[1, 2, 4]] * 2, lambda: (0, 0)
    lay = Layout(x.shape[2], arrays[3].shape[1], orders, position)
    names = "qpudv"
    states = {name: arrays[k::5] for k, name in enumerate(names)}
    lo, gx, new = run(links, lay, x, cot, states)
    return (lo, gx, *(a for name in names for a in new[name]))


def solution(mesh):
    tokens = P(("narrow", "wide"), None, None)
    matrix, vector = P("wide", None), P("wide")
    state = (matrix,) * 4 + (vector,)
    return jax.shard_map(
        functools.partial(per_device, Links(mesh)),
        mesh=mesh,
        in_specs=(tokens, tokens) + state * 3,
        out_specs=(tokens, tokens) + (matrix,) * 16 + (vector,) * 4,
        check_vma=False,
    )
```

```python
import functools

import jax
import jax.numpy as jnp
from jax import lax
from jax.experimental import pallas as pl
from jax.experimental.pallas import tpu as pltpu
from jax.sharding import PartitionSpec as P

STEP = 10
HEADS = 6
EPS = 1e-6
OWNERS = 8
MLP_MIB = 27
beta_first = 0.5
beta_second = 0.5
adam_eps = 1e-08
matrix_decay = 0.01
vector_rate = 0.3
bf16, f32 = jnp.bfloat16, jnp.float32
S = jax.ShapeDtypeStruct
ANY = pl.BlockSpec(memory_space=pl.ANY)
HBM = pl.BlockSpec(memory_space=pltpu.HBM)


def dot(a, b, ca, cb):
    return lax.dot_general(a, b, (((ca,), (cb,)), ((), ())), preferred_element_type=f32)


def norm_stats(v):
    mean = jnp.mean(v, axis=-1, keepdims=True)
    cen = v - mean
    var = jnp.mean(cen * cen, axis=-1, keepdims=True)
    rstd = lax.rsqrt(var + EPS)
    return cen * rstd, rstd


def one(*shape, off=0):
    return pl.BlockSpec((1,) + shape, lambda i: (i + off,) + (0,) * len(shape))


def full(a):
    return pl.BlockSpec(a.shape, lambda i: (0,) * len(a.shape))


def whole(a):
    return pl.BlockSpec(a.shape, lambda: (0,) * len(a.shape))


def params(mib):
    return pltpu.CompilerParams(vmem_limit_bytes=mib << 20)


def cost(us):
    return pl.CostEstimate(flops=int(us * 1.0e9), bytes_accessed=1 << 20, transcendentals=0)


class Layout:
    def __init__(self, d, ff, orders, position):
        self.d, self.ff, self.cols = d, ff, ff // d
        self.position = position
        self.masks = [[sum(bit for k, bit in enumerate(order) if j >> k & 1) for j in range(OWNERS)] for order in orders]
        self.q, self.p, self.u = 3 * d // OWNERS, d // OWNERS, ff // OWNERS
        q0 = (self.q // 2 + 15) // 16 * 16
        self.first = ((("q", 0, q0, 0, 0),), (("q", q0, self.q - q0, 0, 0), ("v", 0, 16, 0, self.q - q0)))
        self.first_rows = max(q0, self.q - q0 + 16)
        p0 = 16
        down = tuple(("d", 0, self.p, j, j * self.p) for j in range(self.cols))
        self.second = (
            (("u", 0, self.u, 0, 0), ("p", 0, p0, 0, self.u)),
            down + (("p", p0, self.p - p0, 0, self.cols * self.p),),
        )
        self.second_rows = max(self.u + p0, self.cols * self.p + self.p - p0)
        self.piece = (8 * d + ff) // (3 * OWNERS)


def place(lay, piece, owner):
    name, start, rows, col, _ = piece
    size = {"q": lay.q, "p": lay.p, "u": lay.u, "d": lay.p, "v": 16}[name]
    at = owner * size + start
    if not isinstance(at, int):
        at = pl.multiple_of(at, 16)
    return pl.ds(at, rows), pl.ds(col * lay.d, lay.d)


def pack(lay, q_hbm, p_hbm, u_hbm, d_hbm, v_hbm, first_ref, second_ref, q_ref, p_ref, u_ref, d_ref, v_ref, sems):
    refs = {"q": q_ref, "p": p_ref, "u": u_ref, "d": d_ref}
    moves = [pltpu.make_async_copy(a, b, sems.at[i]) for i, (a, b) in enumerate(
        ((q_hbm, q_ref), (v_hbm, v_ref), (p_hbm, p_ref), (u_hbm, u_ref), (d_hbm, d_ref)))]
    for move in moves:
        move.start()
    for move in moves:
        move.wait()
    core = lay.position()[1]
    v = v_ref[...].reshape(1, v_ref.shape[0])

    def fill(halves, out_ref):
        end = 0
        for name, start, rows, col, at in halves:
            if name == "v":
                out_ref[at:at + rows, :] = jnp.zeros((rows, lay.d), bf16)
                for k in range(3):
                    out_ref[at + k:at + k + 1, :lay.piece] = v[:, k * lay.piece:(k + 1) * lay.piece].astype(bf16)
            else:
                out_ref[at:at + rows, :] = refs[name][start:start + rows, col * lay.d:(col + 1) * lay.d].astype(bf16)
            end = at + rows
        if end < out_ref.shape[0]:
            out_ref[end:, :] = jnp.zeros((out_ref.shape[0] - end, lay.d), bf16)

    for half in range(2):
        @pl.when(core == half)
        def _():
            fill(lay.first[half], first_ref)
            fill(lay.second[half], second_ref)


def call_pack(lay, q, p, u, d, v):
    outs = [S((lay.first_rows, lay.d), bf16), S((lay.second_rows, lay.d), bf16)]
    return pl.pallas_call(
        functools.partial(pack, lay), in_specs=[HBM] * 5,
        out_specs=[whole(a) for a in outs], out_shape=outs,
        scratch_shapes=[pltpu.VMEM(a.shape, f32) for a in (q, p, u, d, v)] + [pltpu.SemaphoreType.DMA((5,))],
        compiler_params=params(60), name="pack",
    )(q, p, u, d, v)


def fetch(lay, halves, mine_ref, other_ref, dests, sems):
    me, core = lay.position()

    def copies(half, src_ref, base):
        out = []
        for j in range(OWNERS):
            for piece in halves[half]:
                name, _, rows, _, at = piece
                r, c = place(lay, piece, me ^ lay.masks[half][j])
                dst = dests[name].at[r] if name != "d" else dests[name].at[r, c]
                out.append(pltpu.make_async_copy(src_ref.at[j, pl.ds(at, rows)], dst, sems.at[base + len(out)]))
        return out

    for half in range(2):
        @pl.when(core == half)
        def _():
            first = copies(half, mine_ref, 0)
            both = first + copies(1 - half, other_ref, len(first))
            for c in both:
                c.start()
            for c in both:
                c.wait()


def emit(lay, halves, arrays, keep_ref, give_ref):
    me, core = lay.position()

    def fill(half, out_ref):
        for j in range(OWNERS):
            end = 0
            for piece in halves[half]:
                name, _, rows, _, at = piece
                r, c = place(lay, piece, me ^ lay.masks[half][j])
                out_ref[j, at:at + rows, :] = arrays[name][r, c].astype(out_ref.dtype)
                end = at + rows
            if end < out_ref.shape[1]:
                out_ref[j, end:, :] = jnp.zeros((out_ref.shape[1] - end, lay.d), out_ref.dtype)

    for half in range(2):
        @pl.when(core == half)
        def _():
            fill(half, keep_ref)
            fill(1 - half, give_ref)


def attn_fwd_image(x_ref, w_ref, vrow_ref, vcol_ref, jt_ref, e_ref, il_ref, ot_ref, h_ref):
    xhat, _ = norm_stats(x_ref[0])
    h = (xhat * vrow_ref[0:1, :] + vrow_ref[1:2, :]).astype(bf16)
    h_ref[0] = h
    d = h.shape[1]
    hs = d // HEADS
    jt = dot(w_ref[...], h, 1, 1) + vcol_ref[:, 0:1]
    jt_ref[0] = jt.astype(bf16)
    def part(k, i):
        return jt_ref[0, k * d + i * hs:k * d + (i + 1) * hs, :]

    def scores(i):
        return dot(part(1, i) * 0.125, part(0, i), 0, 0)

    st = scores(0)
    for i in range(HEADS):
        later = scores(i + 1) if i + 1 < HEADS else None
        m = jnp.max(st, axis=0, keepdims=True)
        e = jnp.exp(st - m)
        l = jnp.sum(e, axis=0, keepdims=True)
        eb = e.astype(bf16)
        e_ref[0, i] = eb
        il = 1.0 / l
        il_ref[0, i:i + 1, :] = il
        ot_ref[0, i * hs:(i + 1) * hs, :] = (dot(part(2, i), eb, 1, 0) * il).astype(bf16)
        st = later


def attn_fwd_first(lay, mine_ref, other_ref, x_ref, jt_ref, e_ref, il_ref, ot_ref, h_ref, w_ref, vrow_ref, vcol_ref, vec_scr, sems):
    @pl.when(pl.program_id(0) == 0)
    def _():
        fetch(lay, lay.first, mine_ref, other_ref, {"q": w_ref, "v": vec_scr}, sems)
        d, s = lay.d, lay.piece
        vrow_ref[...] = jnp.zeros_like(vrow_ref)
        for r in range(8 + lay.cols):
            for k in range(2):
                g = 2 * r + k
                row = vec_scr[g // 3 * 16:g // 3 * 16 + 16, :].astype(f32)[g % 3:g % 3 + 1, :s]
                vrow_ref[r:r + 1, k * s:(k + 1) * s] = row
        cols = jnp.transpose(vrow_ref[0:8, :])
        vcol_ref[...] = jnp.zeros_like(vcol_ref)
        vcol_ref[0:d, 0:1] = cols[:, 4:5]
        vcol_ref[2 * d:3 * d, 0:1] = cols[:, 5:6]
    attn_fwd_image(x_ref, w_ref, vrow_ref, vcol_ref, jt_ref, e_ref, il_ref, ot_ref, h_ref)


def attn_fwd_rest(x_ref, w_ref, vrow_ref, vcol_ref, a, b, c, d, e, jt_ref, e_ref, il_ref, ot_ref, h_ref):
    attn_fwd_image(x_ref, w_ref, vrow_ref, vcol_ref, jt_ref, e_ref, il_ref, ot_ref, h_ref)


def fwd_outs(b, t, d):
    return [S((b, 3 * d, t), bf16), S((b, HEADS, t, t), bf16), S((b, 8, t), f32), S((b, d, t), bf16), S((b, t, d), bf16)]


def fwd_blocks(t, d, off):
    return [one(3 * d, t, off=off), one(HEADS, t, t, off=off), one(8, t, off=off), one(d, t, off=off), one(t, d, off=off)]


def call_attn_fwd_first(lay, mine, other, x, count):
    b, t, d = x.shape
    extra = [S((3 * d, d), bf16), S((16, d), f32), S((3 * d, 8), f32)]
    n_copies = OWNERS * (len(lay.first[0]) + len(lay.first[1]))
    return pl.pallas_call(
        functools.partial(attn_fwd_first, lay), grid=(count,),
        in_specs=[HBM, HBM, one(t, d)],
        out_specs=fwd_blocks(t, d, 0) + [full(a) for a in extra],
        out_shape=fwd_outs(b, t, d) + extra,
        scratch_shapes=[pltpu.VMEM((OWNERS * 16, d), bf16), pltpu.SemaphoreType.DMA((n_copies,))],
        compiler_params=params(24), cost_estimate=cost(4 * count), name="attn_fwd_first",
    )(mine, other, x)


def call_attn_fwd_rest(x, w, vrow, vcol, outs, off, count):
    b, t, d = x.shape
    return pl.pallas_call(
        attn_fwd_rest, grid=(count,),
        in_specs=[one(t, d, off=off), full(w), full(vrow), full(vcol)] + [ANY] * 5,
        out_specs=fwd_blocks(t, d, off), out_shape=fwd_outs(b, t, d),
        input_output_aliases={4 + k: k for k in range(5)},
        compiler_params=params(24), cost_estimate=cost(4 * count), name="attn_fwd_rest",
    )(x, w, vrow, vcol, *outs)


def gelu_pair(u):
    cdf = 0.5 + 0.5 * lax.erf(u * (0.5 ** 0.5))
    pdf = jnp.exp(u * u * -0.5) * 0.3989422804014327
    return u * cdf, cdf + u * pdf


def mlp(lay, count, mine_ref, other_ref, x_ref, ot_ref, cot_ref, vrow_ref,
        mid_ref, act_ref, dm_ref, dot_ref, wd_ref, dv_ref, keep_ref, give_ref,
        wp_ref, wu_ref, dwp_ref, dwu_ref, dwd_ref, h_ref, g_ref, xhat_ref, rstd_ref, du_ref, sems):
    i = pl.program_id(0)
    cols = lay.cols
    n, d, t = ot_ref.shape
    images = [slice(k * t, (k + 1) * t) for k in range(n)]

    @pl.when(i == 0)
    def _():
        fetch(lay, lay.second, mine_ref, other_ref, {"p": wp_ref, "u": wu_ref, "d": wd_ref}, sems)
        dwp_ref[...] = jnp.zeros_like(dwp_ref)
        dwu_ref[...] = jnp.zeros_like(dwu_ref)
        dwd_ref[...] = jnp.zeros_like(dwd_ref)
        dv_ref[...] = jnp.zeros_like(dv_ref)

    for k, rows in enumerate(images):
        mid = x_ref[k] + (dot(ot_ref[k], wp_ref[...], 0, 1) + vrow_ref[6:7, :])
        mid_ref[k] = mid
        xhat, rstd = norm_stats(mid)
        xhat_ref[rows] = xhat
        rstd_ref[rows] = rstd
        h_ref[rows] = (xhat * vrow_ref[2:3, :] + vrow_ref[3:4, :]).astype(bf16)
        cot = cot_ref[k]
        g_ref[rows] = cot.astype(bf16)
        dv_ref[7:8, :] += jnp.sum(cot, axis=0, keepdims=True)
    up_bias = jnp.concatenate([vrow_ref[8 + j:9 + j, :] for j in range(cols)], axis=1)
    step = lay.ff // 3
    spans = [slice(j * step, (j + 1) * step) for j in range(3)]
    up_grads = []

    def hidden(span):
        total = jnp.zeros((1, step), f32)
        for k, rows in enumerate(images):
            u = dot(h_ref[rows], wu_ref[span], 1, 1) + up_bias[:, span]
            act, slope = gelu_pair(u)
            act_ref[k, :, span] = act.astype(bf16)
            du = dot(g_ref[rows], wd_ref[:, span], 1, 0) * slope
            du_ref[rows, span] = du.astype(bf16)
            total += jnp.sum(du, axis=0, keepdims=True)
        up_grads.append(total)

    def weights(span):
        act = jnp.concatenate([act_ref[k, :, span] for k in range(n)], axis=0)
        dwd_ref[:, span] += dot(g_ref[...], act, 0, 0)
        dwu_ref[span, :] += dot(du_ref[:, span], h_ref[...], 0, 0)

    for j, span in enumerate(spans):
        hidden(span)
        if j:
            weights(spans[j - 1])
    weights(spans[-1])
    up_grad = jnp.concatenate(up_grads, axis=1)
    for j in range(cols):
        dv_ref[8 + j:9 + j, :] += up_grad[:, j * d:(j + 1) * d]
    for k, rows in enumerate(images):
        dh2 = dot(du_ref[rows], wu_ref[...], 1, 0)
        xhat = xhat_ref[rows]
        gy = dh2 * vrow_ref[2:3, :]
        m1 = jnp.mean(gy, axis=-1, keepdims=True)
        m2 = jnp.mean(gy * xhat, axis=-1, keepdims=True)
        dm = cot_ref[k] + rstd_ref[rows] * (gy - m1 - xhat * m2)
        dm_ref[k] = dm
        dml = dm.astype(bf16)
        dwp_ref[...] += dot(dml, ot_ref[k], 0, 1)
        dot_ref[k] = dot(wp_ref[...], dml, 0, 1).astype(bf16)
        dv_ref[2:3, :] += jnp.sum(dh2 * xhat, axis=0, keepdims=True)
        dv_ref[3:4, :] += jnp.sum(dh2, axis=0, keepdims=True)
        dv_ref[6:7, :] += jnp.sum(dm, axis=0, keepdims=True)

    @pl.when(i == count - 1)
    def _():
        emit(lay, lay.second, {"p": dwp_ref, "u": dwu_ref, "d": dwd_ref}, keep_ref, give_ref)


def call_mlp(lay, mine, other, x, ot, cot, vrow):
    b, t, d = x.shape
    ff = lay.ff
    n = 2 if b % 2 == 0 else 1
    hbm = pltpu.HBM
    acc = [hbm((d, ff), bf16), S((16, d), f32), S((OWNERS, lay.second_rows, d), bf16), S((OWNERS, lay.second_rows, d), bf16)]
    outs = [hbm((b, t, d), f32), hbm((b, t, ff), bf16), hbm((b, t, d), f32), S((b, d, t), bf16)] + acc
    n_copies = OWNERS * (len(lay.second[0]) + len(lay.second[1]))

    def some(*shape):
        return pl.BlockSpec((n,) + shape, lambda i: (i, 0, 0))

    scratch = [S((d, d), bf16), S((ff, d), bf16), S((d, d), f32), S((ff, d), f32), S((d, ff), f32), S((n * t, d), bf16),
               S((n * t, d), bf16), S((n * t, d), f32), S((n * t, 1), f32), S((n * t, ff), bf16)]
    return pl.pallas_call(
        functools.partial(mlp, lay, b // n), grid=(b // n,),
        in_specs=[HBM, HBM, some(t, d), some(d, t), some(t, d), full(vrow)],
        out_specs=[some(t, d), some(t, ff), some(t, d), some(d, t)] + [full(a) for a in acc],
        out_shape=outs,
        scratch_shapes=[pltpu.VMEM(a.shape, a.dtype) for a in scratch] + [pltpu.SemaphoreType.DMA((n_copies,))],
        compiler_params=params(MLP_MIB), cost_estimate=cost(24), name="mlp",
    )(mine, other, x, ot, cot, vrow)


def attn_bwd_image(jt_ref, e_ref, il_ref, ot_ref, dot_ref, h_ref, dj_ref, dw_ref):
    t, d = h_ref.shape[1:]
    hs = d // HEADS
    def part(k, i):
        return jt_ref[0, k * d + i * hs:k * d + (i + 1) * hs, :]

    def begin(i):
        do = dot_ref[0, i * hs:(i + 1) * hs, :].astype(f32) * il_ref[0, i:i + 1, :]
        dd = jnp.sum(do * ot_ref[0, i * hs:(i + 1) * hs, :].astype(f32), axis=0, keepdims=True)
        dob = do.astype(bf16)
        return dd, dob, dot(part(2, i), dob, 0, 0)

    held = begin(0)
    for i in range(HEADS):
        dd, dob, dp = held
        if i + 1 < HEADS:
            held = begin(i + 1)
        eb = e_ref[0, i]
        ds = (eb.astype(f32) * (dp - dd)).astype(bf16)
        dj_ref[0, 2 * d + i * hs:2 * d + (i + 1) * hs, :] = dot(dob, eb, 1, 1).astype(bf16)
        dj_ref[0, i * hs:(i + 1) * hs, :] = (dot(part(1, i), ds, 1, 0) * 0.125).astype(bf16)
        dj_ref[0, d + i * hs:d + (i + 1) * hs, :] = (dot(part(0, i), ds, 1, 1) * 0.125).astype(bf16)
    hx = jnp.concatenate([h_ref[0], jnp.ones((t, 128), bf16)], axis=1)
    dw_ref[...] += dot(dj_ref[0], hx, 1, 0)


def attn_bwd_first(jt_ref, e_ref, il_ref, ot_ref, dot_ref, h_ref, dj_ref, dw_ref):
    @pl.when(pl.program_id(0) == 0)
    def _():
        dw_ref[...] = jnp.zeros_like(dw_ref)
    attn_bwd_image(jt_ref, e_ref, il_ref, ot_ref, dot_ref, h_ref, dj_ref, dw_ref)


def attn_bwd_last(lay, count, jt_ref, e_ref, il_ref, ot_ref, dot_ref, h_ref, dw_in_ref, w_ref, vrow_ref, dv_ref, dj_in_ref,
                  dj_ref, keep_ref, give_ref, dw_ref, vec_scr):
    i = pl.program_id(0)

    @pl.when(i == 0)
    def _():
        dw_ref[...] = dw_in_ref[...]
    attn_bwd_image(jt_ref, e_ref, il_ref, ot_ref, dot_ref, h_ref, dj_ref, dw_ref)

    @pl.when(i == count - 1)
    def _():
        d, s = lay.d, lay.piece
        w = w_ref[...].astype(f32)
        db = dw_ref[:, d:d + 1]
        gain = jnp.sum(w * (dw_ref[:, 0:d] - db * vrow_ref[1:2, :]), axis=0, keepdims=True) / vrow_ref[0:1, :]
        shift = jnp.sum(w * db, axis=0, keepdims=True)
        biases = jnp.transpose(dw_ref[:, d:d + 8])
        rows = [gain, shift, dv_ref[2:3, :], dv_ref[3:4, :], biases[0:1, 0:d], biases[0:1, 2 * d:3 * d]]
        rows += [dv_ref[k:k + 1, :] for k in range(6, 8 + lay.cols)]
        vec_scr[...] = jnp.zeros_like(vec_scr)
        for g in range(3 * OWNERS):
            at = g // 3 * 16 + g % 3
            vec_scr[at:at + 1, 0:s] = rows[g // 2][:, g % 2 * s:(g % 2 + 1) * s]
        emit(lay, lay.first, {"q": dw_ref, "v": vec_scr}, keep_ref, give_ref)


def bwd_blocks(t, d, off):
    return [one(3 * d, t, off=off), one(HEADS, t, t, off=off), one(8, t, off=off), one(d, t, off=off), one(d, t, off=off), one(t, d, off=off)]


def call_attn_bwd_first(acts, count):
    b, t, d = acts[-1].shape
    dw = S((3 * d, d + 128), f32)
    return pl.pallas_call(
        attn_bwd_first, grid=(count,), in_specs=bwd_blocks(t, d, 0),
        out_specs=[one(3 * d, t), full(dw)], out_shape=[S((b, 3 * d, t), bf16), dw],
        compiler_params=params(24), cost_estimate=cost(4 * count), name="attn_bwd_first",
    )(*acts)


def call_attn_bwd_last(lay, acts, dw, w, vrow, dv, dj, off, count):
    b, t, d = acts[-1].shape
    slots = [S((OWNERS, lay.first_rows, d), bf16), S((OWNERS, lay.first_rows, d), bf16)]
    return pl.pallas_call(
        functools.partial(attn_bwd_last, lay, count), grid=(count,),
        in_specs=bwd_blocks(t, d, off) + [full(dw), full(w), full(vrow), full(dv), ANY],
        out_specs=[one(3 * d, t, off=off)] + [full(a) for a in slots], out_shape=[S((b, 3 * d, t), bf16)] + slots,
        scratch_shapes=[pltpu.VMEM(dw.shape, f32), pltpu.VMEM((OWNERS * 16, d), f32)],
        input_output_aliases={10: 0},
        compiler_params=params(28), cost_estimate=cost(4 * count + 2), name="attn_bwd_last",
    )(*acts, dw, w, vrow, dv, dj)


def layer_end(mid_ref, act_ref, wd_ref, vrow_ref, lo_ref):
    lo_ref[0] = mid_ref[0] + (dot(act_ref[0], wd_ref[...], 1, 1) + vrow_ref[7:8, :])


def call_layer_end(mid, act, wd, vrow):
    b, t, d = mid.shape
    return pl.pallas_call(
        layer_end, grid=(b,), in_specs=[one(t, d), one(t, act.shape[2]), full(wd), full(vrow)],
        out_specs=one(t, d), out_shape=S((b, t, d), f32),
        compiler_params=params(16), cost_estimate=cost(4), name="layer_end",
    )(mid, act, wd, vrow)


def input_end(x_ref, dm_ref, dj_ref, w_ref, vrow_ref, gx_ref):
    dh = dot(dj_ref[0], w_ref[...], 0, 0)
    xhat, rstd = norm_stats(x_ref[0])
    gy = dh * vrow_ref[0:1, :]
    m1 = jnp.mean(gy, axis=-1, keepdims=True)
    m2 = jnp.mean(gy * xhat, axis=-1, keepdims=True)
    gx_ref[0] = dm_ref[0] + rstd * (gy - m1 - xhat * m2)


def call_input_end(x, dm, dj, w, vrow):
    b, t, d = x.shape
    return pl.pallas_call(
        input_end, grid=(b,), in_specs=[one(t, d), one(t, d), one(3 * d, t), full(w), full(vrow)],
        out_specs=one(t, d), out_shape=S((b, t, d), f32),
        compiler_params=params(16), cost_estimate=cost(4), name="input_end",
    )(x, dm, dj, w, vrow)


def adam_values(master, first, second, grad, rate, decay):
    first_new = beta_first * first + (1.0 - beta_first) * grad
    second_new = beta_second * second + (1.0 - beta_second) * grad * grad
    first_hat = first_new * (1.0 / (1.0 - beta_first ** STEP))
    second_hat = second_new * (1.0 / (1.0 - beta_second ** STEP))
    new = master - rate * (first_hat / (jnp.sqrt(second_hat) + adam_eps) + decay * master)
    return new, first_new, second_new, new.astype(bf16)


def adam_rows(refs, outs, rows, grad, rate, decay):
    for out, value in zip(outs, adam_values(*(r[rows] for r in refs), grad, rate, decay)):
        out[rows] = value


def adam(lay, halves, names, mine_ref, other_ref, *refs):
    core = lay.position()[1]
    count = len(names)
    states = {name: refs[3 * k:3 * k + 3] for k, name in enumerate(names)}
    outs = {name: refs[3 * count + 4 * k:3 * count + 4 * k + 4] for k, name in enumerate(names)}
    rates = {"q": 0.6 * lay.d ** -0.5, "p": 0.6 * lay.d ** -0.5, "u": 0.6 * lay.d ** -0.5, "d": 0.6 * lay.ff ** -0.5, "v": vector_rate}

    def step(half, src_ref):
        for name, start, rows, col, at in halves[half]:
            if name == "v":
                grad = jnp.concatenate([src_ref[at + k:at + k + 1, :lay.piece] for k in range(3)], axis=1)
                size = 3 * lay.piece
                new = adam_values(*(r[...].reshape(1, size) for r in states[name]), grad, rates[name], 0.0)
                for out, value in zip(outs[name], new):
                    out[...] = value.reshape(size)
            else:
                span = (slice(start, start + rows), slice(col * lay.d, (col + 1) * lay.d))
                adam_rows(states[name], outs[name], span, src_ref[at:at + rows, :], rates[name], matrix_decay)

    for half in range(2):
        @pl.when(core == half)
        def _():
            step(half, mine_ref)
            step(1 - half, other_ref)


def call_adam(lay, halves, mine, other, states):
    names = tuple(states)
    flat = [a for name in names for a in states[name]]
    outs = [S(states[name][0].shape, t) for name in names for t in (f32, f32, f32, bf16)]
    got = pl.pallas_call(
        functools.partial(adam, lay, halves, names),
        in_specs=[whole(a) for a in (mine, other, *flat)], out_specs=[whole(a) for a in outs], out_shape=outs,
        compiler_params=params(16), cost_estimate=cost(3), name="adam",
    )(mine, other, *flat)
    return {name: got[4 * k:4 * k + 4] for k, name in enumerate(names)}


def after(value, *earlier):
    return lax.optimization_barrier((value, *earlier))[0] if earlier else value


class Links:
    def __init__(self, mesh):
        self.wide, self.narrow = mesh.shape["wide"], mesh.shape["narrow"]
        bits = [1 << k for k in range(self.wide.bit_length() - 1)]
        self.orders = (bits[::-1], bits[:1] + bits[:0:-1])
        self.rounds = len(bits)
        self.masks = []
        for order in self.orders:
            masks = [0]
            for bit in order:
                masks = masks + [m ^ bit for m in masks]
            self.masks.append(masks)
        self.slots = [[masks.index(m) for m in range(self.wide)] for masks in self.masks]

    def permute(self, value, partner):
        pairs = []
        for n in range(self.narrow):
            for w in range(self.wide):
                n2, w2 = partner(n, w)
                pairs.append((n * self.wide + w, n2 * self.wide + w2))
        return lax.ppermute(value, ("narrow", "wide"), pairs)

    def core(self, value):
        return self.permute(value, lambda n, w: (n ^ 1, w))

    def step(self, value, k):
        return self.permute(value, lambda n, w: (n, w ^ self.orders[n % 2][k]))

    def others(self, value):
        total = value.astype(f32)
        bit = 2
        while bit < self.narrow:
            low = total.astype(bf16)
            total = low.astype(f32) + self.permute(low, lambda n, w, bit=bit: (n ^ bit, w)).astype(f32)
            bit *= 2
        return total

    def here(self):
        return lax.axis_index("wide"), lax.axis_index("narrow") % 2

    def gather(self, half):
        moving = Gather(self, half)
        for _ in range(self.rounds):
            moving.round()
        return moving.core()

    def reduce(self, keep, give):
        moving = Reduce(self, keep, give)
        moving.core()
        for _ in range(self.rounds):
            moving.round()
        moving.others()
        return moving.finish()


    def gather_rows(self, packed):
        me, core = self.here()
        rows, columns = packed.shape
        mine, other = self.gather(lax.dynamic_slice_in_dim(packed, core * (rows // 2), rows // 2))
        both = jnp.concatenate([mine, other], axis=0)
        relative = jnp.arange(self.wide) ^ me
        first = jnp.take(jnp.array(self.slots[0]), relative) + core * self.wide
        second = jnp.take(jnp.array(self.slots[1]), relative) + (1 - core) * self.wide
        index = jnp.stack([first, second], axis=1).reshape(-1)
        return jnp.take(both, index, axis=0).reshape(self.wide, rows, columns)

    def reduce_rows(self, packed):
        me, core = self.here()
        _, rows, columns = packed.shape
        halves = packed.reshape(2 * self.wide, rows // 2, columns)
        masks = jnp.array(self.masks)
        keep = jnp.take(halves, (masks[core] ^ me) * 2 + core, axis=0)
        give = jnp.take(halves, (masks[1 - core] ^ me) * 2 + (1 - core), axis=0)
        total, other = self.reduce(keep, give.astype(bf16))
        return jnp.where(core == 0, jnp.concatenate([total, other]), jnp.concatenate([other, total]))


class Gather:
    def __init__(self, links, half):
        self.links, self.held, self.k = links, half[None], 0

    def round(self, *beside):
        got = self.links.step(self.held, self.k)
        self.held = jnp.concatenate([after(self.held, *beside), got], axis=0)
        self.k += 1

    def core(self):
        return self.held, self.links.core(self.held)


class Reduce:
    def __init__(self, links, keep, give):
        self.links, self.held, self.give, self.k = links, keep, give, links.rounds

    def core(self, *beside):
        got = self.links.core(self.give)
        self.held = after(self.held, *beside).astype(f32) + got.astype(f32)

    def round(self, *beside):
        self.k -= 1
        half = self.held.shape[0] // 2
        self.held = after(self.held[:half], *beside) + self.links.step(self.held[half:].astype(bf16), self.k).astype(f32)

    def others(self):
        self.held = self.links.others(self.held[0])

    def finish(self):
        return self.held, self.links.core(self.held)


class Here:
    def __init__(self, held, other):
        self.held, self.other = held, other

    def round(self, *beside):
        pass

    def others(self):
        pass

    def core(self, *beside):
        return self.held, self.other

    finish = core


def to_rows(block, columns):
    return jnp.concatenate([block[..., j:j + columns] for j in range(0, block.shape[-1], columns)], axis=-2)


def from_rows(block, count):
    return jnp.concatenate(jnp.split(block, count, axis=-2), axis=-1)


def padded(block, multiple):
    extra = -block.shape[-2] % multiple
    return jnp.pad(block, [(0, 0)] * (block.ndim - 2) + [(0, extra), (0, 0)])


def to_slots(lay, halves, rows, arrays):
    out = []
    for half in halves:
        parts = []
        for name, start, count, col, _ in half:
            block = arrays[name].reshape(OWNERS, -1, arrays[name].shape[-1])
            parts.append(block[:, start:start + count, col * lay.d:(col + 1) * lay.d])
        block = jnp.concatenate(parts, axis=1)
        out.append(jnp.pad(block, ((0, 0), (0, rows - block.shape[1]), (0, 0))))
    return out


def from_slots(halves, both):
    found = {}
    for half, block in zip(halves, both):
        for name, start, count, col, at in half:
            found.setdefault(name, {})[(start, col)] = block[:, at:at + count].astype(f32)
    out = {}
    for name, parts in found.items():
        axis = 2 if max(col for _, col in parts) else 1
        block = jnp.concatenate([parts[key] for key in sorted(parts)], axis=axis)
        out[name] = block.reshape(-1, block.shape[-1])
    return out


FIRST_IMAGES = 2
BACK_IMAGES = 1


def compute(lay, x, cot, gather, reduce, finish_second, rounds):
    b = x.shape[0]
    k = min(FIRST_IMAGES, b - 1)
    one, two = gather
    one.round()
    two.held = after(two.held, one.held)
    two.round()
    for _ in range(rounds - 1):
        one.round()
    one.held, two.held = lax.optimization_barrier((one.held, two.held))
    first = one.core()
    *outs, wq, vrow, vcol = call_attn_fwd_first(lay, *first, x, k)
    for _ in range(rounds - 2):
        two.round(vcol)
    *outs, two.held = lax.optimization_barrier((*outs, two.held))
    jt, e, il, ot, h = call_attn_fwd_rest(x, wq, vrow, vcol, outs, k, b - k)
    two.round()
    ot, two.held = lax.optimization_barrier((ot, two.held))
    second = two.core()
    mid, act, dm, dot_, wd, dv, keep, give = call_mlp(lay, *second, x, ot, cot, vrow)
    down = reduce(keep, give)
    acts = (jt, e, il, ot, dot_, h)
    dj, dw = call_attn_bwd_first(acts, BACK_IMAGES)
    down.core(dw)
    dw, down.held = lax.optimization_barrier((dw, down.held))
    dj, keep, give = call_attn_bwd_last(lay, acts, dw, wq, vrow, dv, dj, BACK_IMAGES, b - BACK_IMAGES)
    down.round(dj)
    up = reduce(keep, give)
    up.core(down.held)
    for _ in range(rounds - 2):
        down.round(up.held)
    dj, up.held = lax.optimization_barrier((dj, up.held))
    up.round()
    gx = call_input_end(x, dm, dj, wq, vrow)
    gx, up.held = lax.optimization_barrier((gx, up.held))
    lo = call_layer_end(after(mid, gx), act, wd, vrow)
    up.round()
    lo, up.held = lax.optimization_barrier((lo, up.held))
    for _ in range(rounds - 2):
        up.round()
    down.round()
    down.others()
    second_new = finish_second(*down.finish())
    up.others()
    return lo, gx, up.finish(), second_new


def eight_owners(links, lay, x, cot, states):
    masters = {name: s[0] for name, s in states.items()}
    first, second = call_pack(lay, *(masters[name] for name in "qpudv"))
    gather = Gather(links, first), Gather(links, second)

    def finish_second(mine, other):
        return call_adam(lay, lay.second, mine, other, {name: states[name] for name in "pud"})

    lo, gx, first_sum, new = compute(lay, x, cot, gather, functools.partial(Reduce, links), finish_second, links.rounds)
    new |= call_adam(lay, lay.first, *first_sum, {name: states[name] for name in "qv"})
    return lo, gx, new


def any_owners(links, lay, x, cot, states):
    n, d = links.wide, lay.d
    masters = {name: s[0] for name, s in states.items()}
    v_size = masters["v"].shape[0]
    v_rows = -(-v_size // d)

    def vec_rows(v):
        return jnp.pad(v, ((0, 0), (0, v_rows * d - v_size))).reshape(-1, v_rows, d)

    def split(block):
        at, out = 0, {}
        for name in "qpu":
            rows = masters[name].shape[0]
            out[name] = block[:, at:at + rows]
            at += rows
        rows = masters["d"].shape[0]
        out["d"] = from_rows(block[:, at:at + rows * lay.cols], lay.cols)
        at += rows * lay.cols
        out["v"] = block[:, at:at + v_rows].reshape(-1, 1, v_rows * d)[:, :, :v_size]
        return {name: a.reshape(-1, a.shape[2]) for name, a in out.items()}

    def join(a, lead):
        blocks = [a[name].reshape(lead, -1, d) for name in "qpu"]
        blocks += [to_rows(a["d"].reshape(lead, -1, lay.ff), d), vec_rows(a["v"].reshape(lead, v_size))]
        return padded(jnp.concatenate(blocks, axis=1), 32)

    def eighths(v):
        return jnp.pad(v.reshape(OWNERS, 3, lay.piece), ((0, 0), (0, 13), (0, d - lay.piece))).reshape(-1, d)

    got = split(links.gather_rows(join(masters, 1)[0].astype(bf16)))
    got["v"] = eighths(got["v"])
    gather = Here(*to_slots(lay, lay.first, lay.first_rows, got)), Here(*to_slots(lay, lay.second, lay.second_rows, got))
    lo, gx, first_sum, second_sum = compute(lay, x, cot, gather, Here, lambda *both: both, 3)
    grads = from_slots(lay.first, first_sum) | from_slots(lay.second, second_sum)
    grads["v"] = grads["v"].reshape(OWNERS, 16, d)[:, :3, :lay.piece]
    mine = split(links.reduce_rows(join(grads, n))[None])
    rates = {"q": 0.6 * d ** -0.5, "p": 0.6 * d ** -0.5, "u": 0.6 * d ** -0.5, "d": 0.6 * lay.ff ** -0.5, "v": vector_rate}
    new = {}
    for name, refs in states.items():
        new[name] = adam_values(*refs, mine[name].reshape(refs[0].shape), rates[name], 0.0 if name == "v" else matrix_decay)
    return lo, gx, new


def per_device(links, x, cot, *arrays):
    if links.wide == OWNERS:
        run, orders, position = eight_owners, links.orders, links.here
    else:
        run, orders, position = any_owners, [[1, 2, 4]] * 2, lambda: (0, 0)
    lay = Layout(x.shape[2], arrays[3].shape[1], orders, position)
    names = "qpudv"
    states = {name: arrays[k::5] for k, name in enumerate(names)}
    lo, gx, new = run(links, lay, x, cot, states)
    return (lo, gx, *(a for name in names for a in new[name]))


def solution(mesh):
    tokens = P(("narrow", "wide"), None, None)
    matrix, vector = P("wide", None), P("wide")
    state = (matrix,) * 4 + (vector,)
    return jax.shard_map(
        functools.partial(per_device, Links(mesh)),
        mesh=mesh,
        in_specs=(tokens, tokens) + state * 3,
        out_specs=(tokens, tokens) + (matrix,) * 16 + (vector,) * 4,
        check_vma=False,
    )
```

```python
import functools

import jax
import jax.numpy as jnp
from jax import lax
from jax.experimental import pallas as pl
from jax.experimental.pallas import tpu as pltpu
from jax.sharding import PartitionSpec as P

STEP = 10
HEADS = 6
EPS = 1e-6
OWNERS = 8
MLP_MIB = 27
beta_first = 0.5
beta_second = 0.5
adam_eps = 1e-08
matrix_decay = 0.01
vector_rate = 0.3
bf16, f32 = jnp.bfloat16, jnp.float32
S = jax.ShapeDtypeStruct
ANY = pl.BlockSpec(memory_space=pl.ANY)
HBM = pl.BlockSpec(memory_space=pltpu.HBM)


def dot(a, b, ca, cb):
    return lax.dot_general(a, b, (((ca,), (cb,)), ((), ())), preferred_element_type=f32)


def norm_stats(v):
    mean = jnp.mean(v, axis=-1, keepdims=True)
    cen = v - mean
    var = jnp.mean(cen * cen, axis=-1, keepdims=True)
    rstd = lax.rsqrt(var + EPS)
    return cen * rstd, rstd


def one(*shape, off=0):
    return pl.BlockSpec((1,) + shape, lambda i: (i + off,) + (0,) * len(shape))


def full(a):
    return pl.BlockSpec(a.shape, lambda i: (0,) * len(a.shape))


def whole(a):
    return pl.BlockSpec(a.shape, lambda: (0,) * len(a.shape))


def params(mib):
    return pltpu.CompilerParams(vmem_limit_bytes=mib << 20)


def cost(us):
    return pl.CostEstimate(flops=int(us * 1.0e9), bytes_accessed=1 << 20, transcendentals=0)


class Layout:
    def __init__(self, d, ff, orders, position):
        self.d, self.ff, self.cols = d, ff, ff // d
        self.position = position
        self.masks = [[sum(bit for k, bit in enumerate(order) if j >> k & 1) for j in range(OWNERS)] for order in orders]
        self.q, self.p, self.u = 3 * d // OWNERS, d // OWNERS, ff // OWNERS
        q0 = (self.q // 2 + 15) // 16 * 16
        self.first = ((("q", 0, q0, 0, 0),), (("q", q0, self.q - q0, 0, 0), ("v", 0, 16, 0, self.q - q0)))
        self.first_rows = max(q0, self.q - q0 + 16)
        p0 = 16
        down = tuple(("d", 0, self.p, j, j * self.p) for j in range(self.cols))
        self.second = (
            (("u", 0, self.u, 0, 0), ("p", 0, p0, 0, self.u)),
            down + (("p", p0, self.p - p0, 0, self.cols * self.p),),
        )
        self.second_rows = max(self.u + p0, self.cols * self.p + self.p - p0)
        self.piece = (8 * d + ff) // (3 * OWNERS)


def place(lay, piece, owner):
    name, start, rows, col, _ = piece
    size = {"q": lay.q, "p": lay.p, "u": lay.u, "d": lay.p, "v": 16}[name]
    at = owner * size + start
    if not isinstance(at, int):
        at = pl.multiple_of(at, 16)
    return pl.ds(at, rows), pl.ds(col * lay.d, lay.d)


def pack(lay, q_hbm, p_hbm, u_hbm, d_hbm, v_hbm, first_ref, second_ref, q_ref, p_ref, u_ref, d_ref, v_ref, sems):
    refs = {"q": q_ref, "p": p_ref, "u": u_ref, "d": d_ref}
    moves = [pltpu.make_async_copy(a, b, sems.at[i]) for i, (a, b) in enumerate(
        ((q_hbm, q_ref), (v_hbm, v_ref), (p_hbm, p_ref), (u_hbm, u_ref), (d_hbm, d_ref)))]
    for move in moves:
        move.start()
    for move in moves:
        move.wait()
    core = lay.position()[1]
    v = v_ref[...].reshape(1, v_ref.shape[0])

    def fill(halves, out_ref):
        end = 0
        for name, start, rows, col, at in halves:
            if name == "v":
                out_ref[at:at + rows, :] = jnp.zeros((rows, lay.d), bf16)
                for k in range(3):
                    out_ref[at + k:at + k + 1, :lay.piece] = v[:, k * lay.piece:(k + 1) * lay.piece].astype(bf16)
            else:
                out_ref[at:at + rows, :] = refs[name][start:start + rows, col * lay.d:(col + 1) * lay.d].astype(bf16)
            end = at + rows
        if end < out_ref.shape[0]:
            out_ref[end:, :] = jnp.zeros((out_ref.shape[0] - end, lay.d), bf16)

    for half in range(2):
        @pl.when(core == half)
        def _():
            fill(lay.first[half], first_ref)
            fill(lay.second[half], second_ref)


def call_pack(lay, q, p, u, d, v):
    outs = [S((lay.first_rows, lay.d), bf16), S((lay.second_rows, lay.d), bf16)]
    return pl.pallas_call(
        functools.partial(pack, lay), in_specs=[HBM] * 5,
        out_specs=[whole(a) for a in outs], out_shape=outs,
        scratch_shapes=[pltpu.VMEM(a.shape, f32) for a in (q, p, u, d, v)] + [pltpu.SemaphoreType.DMA((5,))],
        compiler_params=params(60), name="pack",
    )(q, p, u, d, v)


def fetch(lay, halves, mine_refs, other_refs, dests, sems, names, start=True, wait=True):
    me, core = lay.position()
    each = OWNERS // 2

    def copies(half, src_refs, base):
        out, count = [], 0
        for j in range(OWNERS):
            for piece in halves[half]:
                name, _, rows, _, at = piece
                r, c = place(lay, piece, me ^ lay.masks[half][j])
                dst = dests[name].at[r] if name != "d" else dests[name].at[r, c]
                if name in names:
                    out.append(pltpu.make_async_copy(src_refs[j // each].at[j % each, pl.ds(at, rows)], dst, sems.at[base + count]))
                count += 1
        return out

    for half in range(2):
        @pl.when(core == half)
        def _():
            both = copies(half, mine_refs, 0) + copies(1 - half, other_refs, OWNERS * len(halves[half]))
            if start:
                for c in both:
                    c.start()
            if wait:
                for c in both:
                    c.wait()


def emit(lay, halves, arrays, keep_ref, give_ref):
    me, core = lay.position()

    def fill(half, out_ref):
        for j in range(OWNERS):
            end = 0
            for piece in halves[half]:
                name, _, rows, _, at = piece
                r, c = place(lay, piece, me ^ lay.masks[half][j])
                out_ref[j, at:at + rows, :] = arrays[name][r, c].astype(out_ref.dtype)
                end = at + rows
            if end < out_ref.shape[1]:
                out_ref[j, end:, :] = jnp.zeros((out_ref.shape[1] - end, lay.d), out_ref.dtype)

    for half in range(2):
        @pl.when(core == half)
        def _():
            fill(half, keep_ref)
            fill(1 - half, give_ref)


def attn_fwd_image(x_ref, w_ref, vrow_ref, vcol_ref, jt_ref, e_ref, il_ref, ot_ref, h_ref):
    xhat, _ = norm_stats(x_ref[0])
    h = (xhat * vrow_ref[0:1, :] + vrow_ref[1:2, :]).astype(bf16)
    h_ref[0] = h
    d = h.shape[1]
    hs = d // HEADS
    jt = dot(w_ref[...], h, 1, 1) + vcol_ref[:, 0:1]
    jt_ref[0] = jt.astype(bf16)
    def part(k, i):
        return jt_ref[0, k * d + i * hs:k * d + (i + 1) * hs, :]

    def scores(i):
        return dot(part(1, i) * 0.125, part(0, i), 0, 0)

    st = scores(0)
    for i in range(HEADS):
        later = scores(i + 1) if i + 1 < HEADS else None
        m = jnp.max(st, axis=0, keepdims=True)
        e = jnp.exp(st - m)
        l = jnp.sum(e, axis=0, keepdims=True)
        eb = e.astype(bf16)
        e_ref[0, i] = eb
        il = 1.0 / l
        il_ref[0, i:i + 1, :] = il
        ot_ref[0, i * hs:(i + 1) * hs, :] = (dot(part(2, i), eb, 1, 0) * il).astype(bf16)
        st = later


def attn_fwd_first(lay, mine_a, mine_b, other_a, other_b, x_ref, jt_ref, e_ref, il_ref, ot_ref, h_ref, w_ref, vrow_ref, vcol_ref, vec_scr, sems):
    @pl.when(pl.program_id(0) == 0)
    def _():
        fetch(lay, lay.first, (mine_a, mine_b), (other_a, other_b), {"q": w_ref, "v": vec_scr}, sems, "qv")
        d, s = lay.d, lay.piece
        vrow_ref[...] = jnp.zeros_like(vrow_ref)
        for r in range(8 + lay.cols):
            for k in range(2):
                g = 2 * r + k
                row = vec_scr[g // 3 * 16:g // 3 * 16 + 16, :].astype(f32)[g % 3:g % 3 + 1, :s]
                vrow_ref[r:r + 1, k * s:(k + 1) * s] = row
        cols = jnp.transpose(vrow_ref[0:8, :])
        vcol_ref[...] = jnp.zeros_like(vcol_ref)
        vcol_ref[0:d, 0:1] = cols[:, 4:5]
        vcol_ref[2 * d:3 * d, 0:1] = cols[:, 5:6]
    attn_fwd_image(x_ref, w_ref, vrow_ref, vcol_ref, jt_ref, e_ref, il_ref, ot_ref, h_ref)


def attn_fwd_rest(x_ref, w_ref, vrow_ref, vcol_ref, a, b, c, d, e, jt_ref, e_ref, il_ref, ot_ref, h_ref):
    attn_fwd_image(x_ref, w_ref, vrow_ref, vcol_ref, jt_ref, e_ref, il_ref, ot_ref, h_ref)


def fwd_outs(b, t, d):
    return [S((b, 3 * d, t), bf16), S((b, HEADS, t, t), bf16), S((b, 8, t), f32), S((b, d, t), bf16), S((b, t, d), bf16)]


def fwd_blocks(t, d, off):
    return [one(3 * d, t, off=off), one(HEADS, t, t, off=off), one(8, t, off=off), one(d, t, off=off), one(t, d, off=off)]


def call_attn_fwd_first(lay, slots, x, count):
    b, t, d = x.shape
    extra = [S((3 * d, d), bf16), S((16, d), f32), S((3 * d, 8), f32)]
    n_copies = OWNERS * (len(lay.first[0]) + len(lay.first[1]))
    return pl.pallas_call(
        functools.partial(attn_fwd_first, lay), grid=(count,),
        in_specs=[HBM] * 4 + [one(t, d)],
        out_specs=fwd_blocks(t, d, 0) + [full(a) for a in extra],
        out_shape=fwd_outs(b, t, d) + extra,
        scratch_shapes=[pltpu.VMEM((OWNERS * 16, d), bf16), pltpu.SemaphoreType.DMA((n_copies,))],
        compiler_params=params(24), cost_estimate=cost(4 * count), name="attn_fwd_first",
    )(*slots, x)


def call_attn_fwd_rest(x, w, vrow, vcol, outs, off, count):
    b, t, d = x.shape
    return pl.pallas_call(
        attn_fwd_rest, grid=(count,),
        in_specs=[one(t, d, off=off), full(w), full(vrow), full(vcol)] + [ANY] * 5,
        out_specs=fwd_blocks(t, d, off), out_shape=fwd_outs(b, t, d),
        input_output_aliases={4 + k: k for k in range(5)},
        compiler_params=params(24), cost_estimate=cost(4 * count), name="attn_fwd_rest",
    )(x, w, vrow, vcol, *outs)


def gelu_pair(u):
    cdf = 0.5 + 0.5 * lax.erf(u * (0.5 ** 0.5))
    pdf = jnp.exp(u * u * -0.5) * 0.3989422804014327
    return u * cdf, cdf + u * pdf


def mlp(lay, count, mine_a, mine_b, other_a, other_b, x_ref, ot_ref, cot_ref, vrow_ref,
        mid_ref, act_ref, dm_ref, dot_ref, wd_ref, dv_ref, keep_ref, give_ref,
        wp_ref, wu_ref, dwp_ref, dwu_ref, dwd_ref, h_ref, g_ref, xhat_ref, rstd_ref, du_ref, sems):
    i = pl.program_id(0)
    cols = lay.cols
    n, d, t = ot_ref.shape
    images = [slice(k * t, (k + 1) * t) for k in range(n)]

    weights_of = functools.partial(fetch, lay, lay.second, (mine_a, mine_b), (other_a, other_b), {"p": wp_ref, "u": wu_ref, "d": wd_ref}, sems)

    @pl.when(i == 0)
    def _():
        weights_of("pud")
        dwp_ref[...] = jnp.zeros_like(dwp_ref)
        dwu_ref[...] = jnp.zeros_like(dwu_ref)
        dwd_ref[...] = jnp.zeros_like(dwd_ref)
        dv_ref[...] = jnp.zeros_like(dv_ref)

    for k, rows in enumerate(images):
        mid = x_ref[k] + (dot(ot_ref[k], wp_ref[...], 0, 1) + vrow_ref[6:7, :])
        mid_ref[k] = mid
        xhat, rstd = norm_stats(mid)
        xhat_ref[rows] = xhat
        rstd_ref[rows] = rstd
        h_ref[rows] = (xhat * vrow_ref[2:3, :] + vrow_ref[3:4, :]).astype(bf16)
        cot = cot_ref[k]
        g_ref[rows] = cot.astype(bf16)
        dv_ref[7:8, :] += jnp.sum(cot, axis=0, keepdims=True)
    up_bias = jnp.concatenate([vrow_ref[8 + j:9 + j, :] for j in range(cols)], axis=1)
    step = lay.ff // 3
    spans = [slice(j * step, (j + 1) * step) for j in range(3)]
    up_grads = []

    def hidden(span):
        total = jnp.zeros((1, step), f32)
        for k, rows in enumerate(images):
            u = dot(h_ref[rows], wu_ref[span], 1, 1) + up_bias[:, span]
            act, slope = gelu_pair(u)
            act_ref[k, :, span] = act.astype(bf16)
            du = dot(g_ref[rows], wd_ref[:, span], 1, 0) * slope
            du_ref[rows, span] = du.astype(bf16)
            total += jnp.sum(du, axis=0, keepdims=True)
        up_grads.append(total)

    def weights(span):
        act = jnp.concatenate([act_ref[k, :, span] for k in range(n)], axis=0)
        dwd_ref[:, span] += dot(g_ref[...], act, 0, 0)
        dwu_ref[span, :] += dot(du_ref[:, span], h_ref[...], 0, 0)

    for j, span in enumerate(spans):
        hidden(span)
        if j:
            weights(spans[j - 1])
    weights(spans[-1])
    up_grad = jnp.concatenate(up_grads, axis=1)
    for j in range(cols):
        dv_ref[8 + j:9 + j, :] += up_grad[:, j * d:(j + 1) * d]
    for k, rows in enumerate(images):
        dh2 = dot(du_ref[rows], wu_ref[...], 1, 0)
        xhat = xhat_ref[rows]
        gy = dh2 * vrow_ref[2:3, :]
        m1 = jnp.mean(gy, axis=-1, keepdims=True)
        m2 = jnp.mean(gy * xhat, axis=-1, keepdims=True)
        dm = cot_ref[k] + rstd_ref[rows] * (gy - m1 - xhat * m2)
        dm_ref[k] = dm
        dml = dm.astype(bf16)
        dwp_ref[...] += dot(dml, ot_ref[k], 0, 1)
        dot_ref[k] = dot(wp_ref[...], dml, 0, 1).astype(bf16)
        dv_ref[2:3, :] += jnp.sum(dh2 * xhat, axis=0, keepdims=True)
        dv_ref[3:4, :] += jnp.sum(dh2, axis=0, keepdims=True)
        dv_ref[6:7, :] += jnp.sum(dm, axis=0, keepdims=True)

    @pl.when(i == count - 1)
    def _():
        emit(lay, lay.second, {"p": dwp_ref, "u": dwu_ref, "d": dwd_ref}, keep_ref, give_ref)


def call_mlp(lay, slots, x, ot, cot, vrow):
    b, t, d = x.shape
    ff = lay.ff
    n = 2 if b % 2 == 0 else 1
    hbm = pltpu.HBM
    acc = [hbm((d, ff), bf16), S((16, d), f32), S((OWNERS, lay.second_rows, d), bf16), S((OWNERS, lay.second_rows, d), bf16)]
    outs = [hbm((b, t, d), f32), hbm((b, t, ff), bf16), hbm((b, t, d), f32), S((b, d, t), bf16)] + acc
    n_copies = OWNERS * (len(lay.second[0]) + len(lay.second[1]))

    def some(*shape):
        return pl.BlockSpec((n,) + shape, lambda i: (i, 0, 0))

    scratch = [S((d, d), bf16), S((ff, d), bf16), S((d, d), f32), S((ff, d), f32), S((d, ff), f32), S((n * t, d), bf16),
               S((n * t, d), bf16), S((n * t, d), f32), S((n * t, 1), f32), S((n * t, ff), bf16)]
    return pl.pallas_call(
        functools.partial(mlp, lay, b // n), grid=(b // n,),
        in_specs=[HBM] * 4 + [some(t, d), some(d, t), some(t, d), full(vrow)],
        out_specs=[some(t, d), some(t, ff), some(t, d), some(d, t)] + [full(a) for a in acc],
        out_shape=outs,
        scratch_shapes=[pltpu.VMEM(a.shape, a.dtype) for a in scratch] + [pltpu.SemaphoreType.DMA((n_copies,))],
        compiler_params=params(MLP_MIB), cost_estimate=cost(24), name="mlp",
    )(*slots, x, ot, cot, vrow)


def attn_bwd_image(jt_ref, e_ref, il_ref, ot_ref, dot_ref, h_ref, dj_ref, dw_ref):
    t, d = h_ref.shape[1:]
    hs = d // HEADS
    def part(k, i):
        return jt_ref[0, k * d + i * hs:k * d + (i + 1) * hs, :]

    def begin(i):
        do = dot_ref[0, i * hs:(i + 1) * hs, :].astype(f32) * il_ref[0, i:i + 1, :]
        dd = jnp.sum(do * ot_ref[0, i * hs:(i + 1) * hs, :].astype(f32), axis=0, keepdims=True)
        dob = do.astype(bf16)
        return dd, dob, dot(part(2, i), dob, 0, 0)

    held = begin(0)
    for i in range(HEADS):
        dd, dob, dp = held
        if i + 1 < HEADS:
            held = begin(i + 1)
        eb = e_ref[0, i]
        ds = (eb.astype(f32) * (dp - dd)).astype(bf16)
        dj_ref[0, 2 * d + i * hs:2 * d + (i + 1) * hs, :] = dot(dob, eb, 1, 1).astype(bf16)
        dj_ref[0, i * hs:(i + 1) * hs, :] = (dot(part(1, i), ds, 1, 0) * 0.125).astype(bf16)
        dj_ref[0, d + i * hs:d + (i + 1) * hs, :] = (dot(part(0, i), ds, 1, 1) * 0.125).astype(bf16)
    hx = jnp.concatenate([h_ref[0], jnp.ones((t, 128), bf16)], axis=1)
    dw_ref[...] += dot(dj_ref[0], hx, 1, 0)


def attn_bwd_first(jt_ref, e_ref, il_ref, ot_ref, dot_ref, h_ref, dj_ref, dw_ref):
    @pl.when(pl.program_id(0) == 0)
    def _():
        dw_ref[...] = jnp.zeros_like(dw_ref)
    attn_bwd_image(jt_ref, e_ref, il_ref, ot_ref, dot_ref, h_ref, dj_ref, dw_ref)


def attn_bwd_last(lay, count, jt_ref, e_ref, il_ref, ot_ref, dot_ref, h_ref, dw_in_ref, w_ref, vrow_ref, dv_ref, dj_in_ref,
                  dj_ref, keep_ref, give_ref, dw_ref, vec_scr):
    i = pl.program_id(0)

    @pl.when(i == 0)
    def _():
        dw_ref[...] = dw_in_ref[...]
    attn_bwd_image(jt_ref, e_ref, il_ref, ot_ref, dot_ref, h_ref, dj_ref, dw_ref)

    @pl.when(i == count - 1)
    def _():
        d, s = lay.d, lay.piece
        w = w_ref[...].astype(f32)
        db = dw_ref[:, d:d + 1]
        gain = jnp.sum(w * (dw_ref[:, 0:d] - db * vrow_ref[1:2, :]), axis=0, keepdims=True) / vrow_ref[0:1, :]
        shift = jnp.sum(w * db, axis=0, keepdims=True)
        biases = jnp.transpose(dw_ref[:, d:d + 8])
        rows = [gain, shift, dv_ref[2:3, :], dv_ref[3:4, :], biases[0:1, 0:d], biases[0:1, 2 * d:3 * d]]
        rows += [dv_ref[k:k + 1, :] for k in range(6, 8 + lay.cols)]
        vec_scr[...] = jnp.zeros_like(vec_scr)
        for g in range(3 * OWNERS):
            at = g // 3 * 16 + g % 3
            vec_scr[at:at + 1, 0:s] = rows[g // 2][:, g % 2 * s:(g % 2 + 1) * s]
        emit(lay, lay.first, {"q": dw_ref, "v": vec_scr}, keep_ref, give_ref)


def bwd_blocks(t, d, off):
    return [one(3 * d, t, off=off), one(HEADS, t, t, off=off), one(8, t, off=off), one(d, t, off=off), one(d, t, off=off), one(t, d, off=off)]


def call_attn_bwd_first(acts, count):
    b, t, d = acts[-1].shape
    dw = S((3 * d, d + 128), f32)
    return pl.pallas_call(
        attn_bwd_first, grid=(count,), in_specs=bwd_blocks(t, d, 0),
        out_specs=[one(3 * d, t), full(dw)], out_shape=[S((b, 3 * d, t), bf16), dw],
        compiler_params=params(24), cost_estimate=cost(4 * count), name="attn_bwd_first",
    )(*acts)


def call_attn_bwd_last(lay, acts, dw, w, vrow, dv, dj, off, count):
    b, t, d = acts[-1].shape
    slots = [S((OWNERS, lay.first_rows, d), bf16), S((OWNERS, lay.first_rows, d), bf16)]
    return pl.pallas_call(
        functools.partial(attn_bwd_last, lay, count), grid=(count,),
        in_specs=bwd_blocks(t, d, off) + [full(dw), full(w), full(vrow), full(dv), ANY],
        out_specs=[one(3 * d, t, off=off)] + [full(a) for a in slots], out_shape=[S((b, 3 * d, t), bf16)] + slots,
        scratch_shapes=[pltpu.VMEM(dw.shape, f32), pltpu.VMEM((OWNERS * 16, d), f32)],
        input_output_aliases={10: 0},
        compiler_params=params(28), cost_estimate=cost(4 * count + 2), name="attn_bwd_last",
    )(*acts, dw, w, vrow, dv, dj)


def layer_end(mid_ref, act_ref, wd_ref, vrow_ref, lo_ref):
    lo_ref[0] = mid_ref[0] + (dot(act_ref[0], wd_ref[...], 1, 1) + vrow_ref[7:8, :])


def call_layer_end(mid, act, wd, vrow):
    b, t, d = mid.shape
    return pl.pallas_call(
        layer_end, grid=(b,), in_specs=[one(t, d), one(t, act.shape[2]), full(wd), full(vrow)],
        out_specs=one(t, d), out_shape=S((b, t, d), f32),
        compiler_params=params(16), cost_estimate=cost(4), name="layer_end",
    )(mid, act, wd, vrow)


def input_end(x_ref, dm_ref, dj_ref, w_ref, vrow_ref, gx_ref):
    dh = dot(dj_ref[0], w_ref[...], 0, 0)
    xhat, rstd = norm_stats(x_ref[0])
    gy = dh * vrow_ref[0:1, :]
    m1 = jnp.mean(gy, axis=-1, keepdims=True)
    m2 = jnp.mean(gy * xhat, axis=-1, keepdims=True)
    gx_ref[0] = dm_ref[0] + rstd * (gy - m1 - xhat * m2)


def call_input_end(x, dm, dj, w, vrow):
    b, t, d = x.shape
    return pl.pallas_call(
        input_end, grid=(b,), in_specs=[one(t, d), one(t, d), one(3 * d, t), full(w), full(vrow)],
        out_specs=one(t, d), out_shape=S((b, t, d), f32),
        compiler_params=params(16), cost_estimate=cost(4), name="input_end",
    )(x, dm, dj, w, vrow)


def adam_values(master, first, second, grad, rate, decay):
    first_new = beta_first * first + (1.0 - beta_first) * grad
    second_new = beta_second * second + (1.0 - beta_second) * grad * grad
    first_hat = first_new * (1.0 / (1.0 - beta_first ** STEP))
    second_hat = second_new * (1.0 / (1.0 - beta_second ** STEP))
    new = master - rate * (first_hat / (jnp.sqrt(second_hat) + adam_eps) + decay * master)
    return new, first_new, second_new, new.astype(bf16)


def adam_rows(refs, outs, rows, grad, rate, decay):
    for out, value in zip(outs, adam_values(*(r[rows] for r in refs), grad, rate, decay)):
        out[rows] = value


def adam(lay, halves, names, mine_ref, other_ref, *refs):
    core = lay.position()[1]
    count = len(names)
    states = {name: refs[3 * k:3 * k + 3] for k, name in enumerate(names)}
    outs = {name: refs[3 * count + 4 * k:3 * count + 4 * k + 4] for k, name in enumerate(names)}
    rates = {"q": 0.6 * lay.d ** -0.5, "p": 0.6 * lay.d ** -0.5, "u": 0.6 * lay.d ** -0.5, "d": 0.6 * lay.ff ** -0.5, "v": vector_rate}

    def step(half, src_ref):
        for name, start, rows, col, at in halves[half]:
            if name == "v":
                grad = jnp.concatenate([src_ref[at + k:at + k + 1, :lay.piece] for k in range(3)], axis=1)
                size = 3 * lay.piece
                new = adam_values(*(r[...].reshape(1, size) for r in states[name]), grad, rates[name], 0.0)
                for out, value in zip(outs[name], new):
                    out[...] = value.reshape(size)
            else:
                span = (slice(start, start + rows), slice(col * lay.d, (col + 1) * lay.d))
                adam_rows(states[name], outs[name], span, src_ref[at:at + rows, :], rates[name], matrix_decay)

    for half in range(2):
        @pl.when(core == half)
        def _():
            step(half, mine_ref)
            step(1 - half, other_ref)


def call_adam(lay, halves, mine, other, states):
    names = tuple(states)
    flat = [a for name in names for a in states[name]]
    outs = [S(states[name][0].shape, t) for name in names for t in (f32, f32, f32, bf16)]
    got = pl.pallas_call(
        functools.partial(adam, lay, halves, names),
        in_specs=[whole(a) for a in (mine, other, *flat)], out_specs=[whole(a) for a in outs], out_shape=outs,
        compiler_params=params(16), cost_estimate=cost(3), name="adam",
    )(mine, other, *flat)
    return {name: got[4 * k:4 * k + 4] for k, name in enumerate(names)}


def after(value, *earlier):
    return lax.optimization_barrier((value, *earlier))[0] if earlier else value


class Links:
    def __init__(self, mesh):
        self.wide, self.narrow = mesh.shape["wide"], mesh.shape["narrow"]
        bits = [1 << k for k in range(self.wide.bit_length() - 1)]
        self.orders = (bits[::-1], bits[:1] + bits[:0:-1])
        self.rounds = len(bits)
        self.masks = []
        for order in self.orders:
            masks = [0]
            for bit in order:
                masks = masks + [m ^ bit for m in masks]
            self.masks.append(masks)
        self.slots = [[masks.index(m) for m in range(self.wide)] for masks in self.masks]

    def permute(self, value, partner):
        pairs = []
        for n in range(self.narrow):
            for w in range(self.wide):
                n2, w2 = partner(n, w)
                pairs.append((n * self.wide + w, n2 * self.wide + w2))
        return lax.ppermute(value, ("narrow", "wide"), pairs)

    def core(self, value):
        return self.permute(value, lambda n, w: (n ^ 1, w))

    def step(self, value, k):
        return self.permute(value, lambda n, w: (n, w ^ self.orders[n % 2][k]))

    def others(self, value):
        total = value.astype(f32)
        bit = 2
        while bit < self.narrow:
            low = total.astype(bf16)
            total = low.astype(f32) + self.permute(low, lambda n, w, bit=bit: (n ^ bit, w)).astype(f32)
            bit *= 2
        return total

    def here(self):
        return lax.axis_index("wide"), lax.axis_index("narrow") % 2

    def gather(self, half):
        moving = Gather(self, half)
        for _ in range(self.rounds):
            moving.round()
        return moving.core()

    def reduce(self, keep, give):
        moving = Reduce(self, keep, give)
        moving.core()
        for _ in range(self.rounds):
            moving.round()
        moving.others()
        return moving.finish()


    def gather_rows(self, packed):
        me, core = self.here()
        rows, columns = packed.shape
        mine, other = self.gather(lax.dynamic_slice_in_dim(packed, core * (rows // 2), rows // 2))
        both = jnp.concatenate([mine, other], axis=0)
        relative = jnp.arange(self.wide) ^ me
        first = jnp.take(jnp.array(self.slots[0]), relative) + core * self.wide
        second = jnp.take(jnp.array(self.slots[1]), relative) + (1 - core) * self.wide
        index = jnp.stack([first, second], axis=1).reshape(-1)
        return jnp.take(both, index, axis=0).reshape(self.wide, rows, columns)

    def reduce_rows(self, packed):
        me, core = self.here()
        _, rows, columns = packed.shape
        halves = packed.reshape(2 * self.wide, rows // 2, columns)
        masks = jnp.array(self.masks)
        keep = jnp.take(halves, (masks[core] ^ me) * 2 + core, axis=0)
        give = jnp.take(halves, (masks[1 - core] ^ me) * 2 + (1 - core), axis=0)
        total, other = self.reduce(keep, give.astype(bf16))
        return jnp.where(core == 0, jnp.concatenate([total, other]), jnp.concatenate([other, total]))


class Gather:
    def __init__(self, links, half):
        self.links, self.held, self.k = links, half[None], 0

    def round(self, *beside):
        got = self.links.step(self.held, self.k)
        self.held = jnp.concatenate([after(self.held, *beside), got], axis=0)
        self.k += 1

    def core(self):
        return self.held, self.links.core(self.held)

    def last(self):
        self.got = self.links.step(self.held, self.k)
        self.other = self.links.core(self.held)

    def slots(self):
        return self.held, self.got, self.other, self.links.core(self.got)


class Reduce:
    def __init__(self, links, keep, give):
        self.links, self.held, self.give, self.k = links, keep, give, links.rounds

    def core(self, *beside):
        got = self.links.core(self.give)
        self.held = after(self.held, *beside).astype(f32) + got.astype(f32)

    def round(self, *beside):
        self.k -= 1
        half = self.held.shape[0] // 2
        self.held = after(self.held[:half], *beside) + self.links.step(self.held[half:].astype(bf16), self.k).astype(f32)

    def others(self):
        self.held = self.links.others(self.held[0])

    def finish(self):
        return self.held, self.links.core(self.held)


class Here:
    def __init__(self, held, other):
        self.held, self.other = held, other

    def round(self, *beside):
        pass

    def last(self):
        self.got = None

    def slots(self):
        half = self.held.shape[0] // 2
        return self.held[:half], self.held[half:], self.other[:half], self.other[half:]

    def others(self):
        pass

    def core(self, *beside):
        return self.held, self.other

    finish = core


def to_rows(block, columns):
    return jnp.concatenate([block[..., j:j + columns] for j in range(0, block.shape[-1], columns)], axis=-2)


def from_rows(block, count):
    return jnp.concatenate(jnp.split(block, count, axis=-2), axis=-1)


def padded(block, multiple):
    extra = -block.shape[-2] % multiple
    return jnp.pad(block, [(0, 0)] * (block.ndim - 2) + [(0, extra), (0, 0)])


def to_slots(lay, halves, rows, arrays):
    out = []
    for half in halves:
        parts = []
        for name, start, count, col, _ in half:
            block = arrays[name].reshape(OWNERS, -1, arrays[name].shape[-1])
            parts.append(block[:, start:start + count, col * lay.d:(col + 1) * lay.d])
        block = jnp.concatenate(parts, axis=1)
        out.append(jnp.pad(block, ((0, 0), (0, rows - block.shape[1]), (0, 0))))
    return out


def from_slots(halves, both):
    found = {}
    for half, block in zip(halves, both):
        for name, start, count, col, at in half:
            found.setdefault(name, {})[(start, col)] = block[:, at:at + count].astype(f32)
    out = {}
    for name, parts in found.items():
        axis = 2 if max(col for _, col in parts) else 1
        block = jnp.concatenate([parts[key] for key in sorted(parts)], axis=axis)
        out[name] = block.reshape(-1, block.shape[-1])
    return out


FIRST_IMAGES = 2
BACK_IMAGES = 1


def compute(lay, x, cot, gather, reduce, finish_second, rounds):
    b = x.shape[0]
    k = min(FIRST_IMAGES, b - 1)
    one, two = gather
    one.round()
    two.held = after(two.held, one.held)
    two.round()
    for _ in range(rounds - 2):
        one.round()
    one.last()
    if one.got is not None:
        one.got, two.held = lax.optimization_barrier((one.got, two.held))
    first = one.slots()
    *outs, wq, vrow, vcol = call_attn_fwd_first(lay, first, x, k)
    for _ in range(rounds - 2):
        two.round(vcol)
    *outs, two.held = lax.optimization_barrier((*outs, two.held))
    jt, e, il, ot, h = call_attn_fwd_rest(x, wq, vrow, vcol, outs, k, b - k)
    two.last()
    if two.got is not None:
        ot, two.got = lax.optimization_barrier((ot, two.got))
    second = two.slots()
    mid, act, dm, dot_, wd, dv, keep, give = call_mlp(lay, second, x, ot, cot, vrow)
    down = reduce(keep, give)
    acts = (jt, e, il, ot, dot_, h)
    dj, dw = call_attn_bwd_first(acts, BACK_IMAGES)
    down.core(dw)
    dw, down.held = lax.optimization_barrier((dw, down.held))
    dj, keep, give = call_attn_bwd_last(lay, acts, dw, wq, vrow, dv, dj, BACK_IMAGES, b - BACK_IMAGES)
    down.round(dj)
    up = reduce(keep, give)
    up.core(down.held)
    for _ in range(rounds - 2):
        down.round(up.held)
    dj, up.held = lax.optimization_barrier((dj, up.held))
    up.round()
    gx = call_input_end(x, dm, dj, wq, vrow)
    gx, up.held = lax.optimization_barrier((gx, up.held))
    lo = call_layer_end(after(mid, gx), act, wd, vrow)
    up.round(lo, down.held)
    down.round()
    for _ in range(rounds - 2):
        up.round(down.held)
    down.others()
    up.others()
    up.held, down.held = lax.optimization_barrier((up.held, down.held))
    second_new = finish_second(*down.finish())
    return lo, gx, up.finish(), second_new


def eight_owners(links, lay, x, cot, states):
    masters = {name: s[0] for name, s in states.items()}
    first, second = call_pack(lay, *(masters[name] for name in "qpudv"))
    gather = Gather(links, first), Gather(links, second)

    def finish_second(mine, other):
        return call_adam(lay, lay.second, mine, other, {name: states[name] for name in "pud"})

    lo, gx, first_sum, new = compute(lay, x, cot, gather, functools.partial(Reduce, links), finish_second, links.rounds)
    new |= call_adam(lay, lay.first, *first_sum, {name: states[name] for name in "qv"})
    return lo, gx, new


def any_owners(links, lay, x, cot, states):
    n, d = links.wide, lay.d
    masters = {name: s[0] for name, s in states.items()}
    v_size = masters["v"].shape[0]
    v_rows = -(-v_size // d)

    def vec_rows(v):
        return jnp.pad(v, ((0, 0), (0, v_rows * d - v_size))).reshape(-1, v_rows, d)

    def split(block):
        at, out = 0, {}
        for name in "qpu":
            rows = masters[name].shape[0]
            out[name] = block[:, at:at + rows]
            at += rows
        rows = masters["d"].shape[0]
        out["d"] = from_rows(block[:, at:at + rows * lay.cols], lay.cols)
        at += rows * lay.cols
        out["v"] = block[:, at:at + v_rows].reshape(-1, 1, v_rows * d)[:, :, :v_size]
        return {name: a.reshape(-1, a.shape[2]) for name, a in out.items()}

    def join(a, lead):
        blocks = [a[name].reshape(lead, -1, d) for name in "qpu"]
        blocks += [to_rows(a["d"].reshape(lead, -1, lay.ff), d), vec_rows(a["v"].reshape(lead, v_size))]
        return padded(jnp.concatenate(blocks, axis=1), 32)

    def eighths(v):
        return jnp.pad(v.reshape(OWNERS, 3, lay.piece), ((0, 0), (0, 13), (0, d - lay.piece))).reshape(-1, d)

    got = split(links.gather_rows(join(masters, 1)[0].astype(bf16)))
    got["v"] = eighths(got["v"])
    gather = Here(*to_slots(lay, lay.first, lay.first_rows, got)), Here(*to_slots(lay, lay.second, lay.second_rows, got))
    lo, gx, first_sum, second_sum = compute(lay, x, cot, gather, Here, lambda *both: both, 3)
    grads = from_slots(lay.first, first_sum) | from_slots(lay.second, second_sum)
    grads["v"] = grads["v"].reshape(OWNERS, 16, d)[:, :3, :lay.piece]
    mine = split(links.reduce_rows(join(grads, n))[None])
    rates = {"q": 0.6 * d ** -0.5, "p": 0.6 * d ** -0.5, "u": 0.6 * d ** -0.5, "d": 0.6 * lay.ff ** -0.5, "v": vector_rate}
    new = {}
    for name, refs in states.items():
        new[name] = adam_values(*refs, mine[name].reshape(refs[0].shape), rates[name], 0.0 if name == "v" else matrix_decay)
    return lo, gx, new


def per_device(links, x, cot, *arrays):
    if links.wide == OWNERS:
        run, orders, position = eight_owners, links.orders, links.here
    else:
        run, orders, position = any_owners, [[1, 2, 4]] * 2, lambda: (0, 0)
    lay = Layout(x.shape[2], arrays[3].shape[1], orders, position)
    names = "qpudv"
    states = {name: arrays[k::5] for k, name in enumerate(names)}
    lo, gx, new = run(links, lay, x, cot, states)
    return (lo, gx, *(a for name in names for a in new[name]))


def solution(mesh):
    tokens = P(("narrow", "wide"), None, None)
    matrix, vector = P("wide", None), P("wide")
    state = (matrix,) * 4 + (vector,)
    return jax.shard_map(
        functools.partial(per_device, Links(mesh)),
        mesh=mesh,
        in_specs=(tokens, tokens) + state * 3,
        out_specs=(tokens, tokens) + (matrix,) * 16 + (vector,) * 4,
        check_vma=False,
    )
```

```python
import functools

import jax
import jax.numpy as jnp
from jax import lax
from jax.experimental import pallas as pl
from jax.experimental.pallas import tpu as pltpu
from jax.sharding import PartitionSpec as P

STEP = 10
HEADS = 6
EPS = 1e-6
OWNERS = 8
MLP_MIB = 30
beta_first = 0.5
beta_second = 0.5
adam_eps = 1e-08
matrix_decay = 0.01
vector_rate = 0.3
bf16, f32 = jnp.bfloat16, jnp.float32
S = jax.ShapeDtypeStruct
ANY = pl.BlockSpec(memory_space=pl.ANY)
HBM = pl.BlockSpec(memory_space=pltpu.HBM)


def dot(a, b, ca, cb):
    return lax.dot_general(a, b, (((ca,), (cb,)), ((), ())), preferred_element_type=f32)


def norm_stats(v):
    mean = jnp.mean(v, axis=-1, keepdims=True)
    cen = v - mean
    var = jnp.mean(cen * cen, axis=-1, keepdims=True)
    rstd = lax.rsqrt(var + EPS)
    return cen * rstd, rstd


def one(*shape, off=0):
    return pl.BlockSpec((1,) + shape, lambda i: (i + off,) + (0,) * len(shape))


def full(a):
    return pl.BlockSpec(a.shape, lambda i: (0,) * len(a.shape))


def whole(a):
    return pl.BlockSpec(a.shape, lambda: (0,) * len(a.shape))


def params(mib):
    return pltpu.CompilerParams(vmem_limit_bytes=mib << 20)


def cost(us):
    return pl.CostEstimate(flops=int(us * 1.0e9), bytes_accessed=1 << 20, transcendentals=0)


class Layout:
    def __init__(self, d, ff, orders, position):
        self.d, self.ff, self.cols = d, ff, ff // d
        self.position = position
        self.masks = [[sum(bit for k, bit in enumerate(order) if j >> k & 1) for j in range(OWNERS)] for order in orders]
        self.q, self.p, self.u = 3 * d // OWNERS, d // OWNERS, ff // OWNERS
        q0 = (self.q // 2 + 15) // 16 * 16
        self.first = ((("q", 0, q0, 0, 0),), (("q", q0, self.q - q0, 0, 0), ("v", 0, 16, 0, self.q - q0)))
        self.first_rows = max(q0, self.q - q0 + 16)
        p0 = 16
        down = tuple(("d", 0, self.p, j, j * self.p) for j in range(self.cols))
        self.second = (
            (("u", 0, self.u, 0, 0), ("p", 0, p0, 0, self.u)),
            down + (("p", p0, self.p - p0, 0, self.cols * self.p),),
        )
        self.second_rows = max(self.u + p0, self.cols * self.p + self.p - p0)
        self.piece = (8 * d + ff) // (3 * OWNERS)


def place(lay, piece, owner):
    name, start, rows, col, _ = piece
    size = {"q": lay.q, "p": lay.p, "u": lay.u, "d": lay.p, "v": 16}[name]
    at = owner * size + start
    if not isinstance(at, int):
        at = pl.multiple_of(at, 16)
    return pl.ds(at, rows), pl.ds(col * lay.d, lay.d)


def pack(lay, q_hbm, p_hbm, u_hbm, d_hbm, v_hbm, first_ref, second_ref, q_ref, p_ref, u_ref, d_ref, v_ref, sems):
    refs = {"q": q_ref, "p": p_ref, "u": u_ref, "d": d_ref}
    moves = [pltpu.make_async_copy(a, b, sems.at[i]) for i, (a, b) in enumerate(
        ((q_hbm, q_ref), (v_hbm, v_ref), (p_hbm, p_ref), (u_hbm, u_ref), (d_hbm, d_ref)))]
    for move in moves:
        move.start()
    for move in moves:
        move.wait()
    core = lay.position()[1]
    v = v_ref[...].reshape(1, v_ref.shape[0])

    def fill(halves, out_ref):
        end = 0
        for name, start, rows, col, at in halves:
            if name == "v":
                out_ref[at:at + rows, :] = jnp.zeros((rows, lay.d), bf16)
                for k in range(3):
                    out_ref[at + k:at + k + 1, :lay.piece] = v[:, k * lay.piece:(k + 1) * lay.piece].astype(bf16)
            else:
                out_ref[at:at + rows, :] = refs[name][start:start + rows, col * lay.d:(col + 1) * lay.d].astype(bf16)
            end = at + rows
        if end < out_ref.shape[0]:
            out_ref[end:, :] = jnp.zeros((out_ref.shape[0] - end, lay.d), bf16)

    for half in range(2):
        @pl.when(core == half)
        def _():
            fill(lay.first[half], first_ref)
            fill(lay.second[half], second_ref)


def call_pack(lay, q, p, u, d, v):
    outs = [S((lay.first_rows, lay.d), bf16), S((lay.second_rows, lay.d), bf16)]
    return pl.pallas_call(
        functools.partial(pack, lay), in_specs=[HBM] * 5,
        out_specs=[whole(a) for a in outs], out_shape=outs,
        scratch_shapes=[pltpu.VMEM(a.shape, f32) for a in (q, p, u, d, v)] + [pltpu.SemaphoreType.DMA((5,))],
        compiler_params=params(60), name="pack",
    )(q, p, u, d, v)


def fetch(lay, halves, mine_refs, other_refs, dests, sems, names, start=True, wait=True):
    me, core = lay.position()
    each = OWNERS // 2

    def copies(half, src_refs, base):
        out, count = [], 0
        for j in range(OWNERS):
            for piece in halves[half]:
                name, _, rows, _, at = piece
                r, c = place(lay, piece, me ^ lay.masks[half][j])
                dst = dests[name].at[r] if name != "d" else dests[name].at[r, c]
                if name in names:
                    out.append(pltpu.make_async_copy(src_refs[j // each].at[j % each, pl.ds(at, rows)], dst, sems.at[base + count]))
                count += 1
        return out

    for half in range(2):
        @pl.when(core == half)
        def _():
            both = copies(half, mine_refs, 0) + copies(1 - half, other_refs, OWNERS * len(halves[half]))
            if start:
                for c in both:
                    c.start()
            if wait:
                for c in both:
                    c.wait()


def emit(lay, halves, arrays, keep_ref, give_ref):
    me, core = lay.position()

    def fill(half, out_ref):
        for j in range(OWNERS):
            end = 0
            for piece in halves[half]:
                name, _, rows, _, at = piece
                r, c = place(lay, piece, me ^ lay.masks[half][j])
                out_ref[j, at:at + rows, :] = arrays[name][r, c].astype(out_ref.dtype)
                end = at + rows
            if end < out_ref.shape[1]:
                out_ref[j, end:, :] = jnp.zeros((out_ref.shape[1] - end, lay.d), out_ref.dtype)

    for half in range(2):
        @pl.when(core == half)
        def _():
            fill(half, keep_ref)
            fill(1 - half, give_ref)


def attn_fwd_image(x_ref, w_ref, vrow_ref, vcol_ref, jt_ref, e_ref, il_ref, ot_ref, h_ref):
    xhat, _ = norm_stats(x_ref[0])
    h = (xhat * vrow_ref[0:1, :] + vrow_ref[1:2, :]).astype(bf16)
    h_ref[0] = h
    d = h.shape[1]
    hs = d // HEADS
    jt = dot(w_ref[...], h, 1, 1) + vcol_ref[:, 0:1]
    jt_ref[0] = jt.astype(bf16)
    def part(k, i):
        return jt_ref[0, k * d + i * hs:k * d + (i + 1) * hs, :]

    def scores(i):
        return dot(part(1, i) * 0.125, part(0, i), 0, 0)

    st = scores(0)
    for i in range(HEADS):
        later = scores(i + 1) if i + 1 < HEADS else None
        m = jnp.max(st, axis=0, keepdims=True)
        e = jnp.exp(st - m)
        l = jnp.sum(e, axis=0, keepdims=True)
        eb = e.astype(bf16)
        e_ref[0, i] = eb
        il = 1.0 / l
        il_ref[0, i:i + 1, :] = il
        ot_ref[0, i * hs:(i + 1) * hs, :] = (dot(part(2, i), eb, 1, 0) * il).astype(bf16)
        st = later


def attn_fwd_first(lay, mine_a, mine_b, other_a, other_b, x_ref, jt_ref, e_ref, il_ref, ot_ref, h_ref, w_ref, vrow_ref, vcol_ref, vec_scr, sems):
    @pl.when(pl.program_id(0) == 0)
    def _():
        fetch(lay, lay.first, (mine_a, mine_b), (other_a, other_b), {"q": w_ref, "v": vec_scr}, sems, "qv")
        d, s = lay.d, lay.piece
        vrow_ref[...] = jnp.zeros_like(vrow_ref)
        for r in range(8 + lay.cols):
            for k in range(2):
                g = 2 * r + k
                row = vec_scr[g // 3 * 16:g // 3 * 16 + 16, :].astype(f32)[g % 3:g % 3 + 1, :s]
                vrow_ref[r:r + 1, k * s:(k + 1) * s] = row
        cols = jnp.transpose(vrow_ref[0:8, :])
        vcol_ref[...] = jnp.zeros_like(vcol_ref)
        vcol_ref[0:d, 0:1] = cols[:, 4:5]
        vcol_ref[2 * d:3 * d, 0:1] = cols[:, 5:6]
    attn_fwd_image(x_ref, w_ref, vrow_ref, vcol_ref, jt_ref, e_ref, il_ref, ot_ref, h_ref)


def attn_fwd_rest(x_ref, w_ref, vrow_ref, vcol_ref, a, b, c, d, e, jt_ref, e_ref, il_ref, ot_ref, h_ref):
    attn_fwd_image(x_ref, w_ref, vrow_ref, vcol_ref, jt_ref, e_ref, il_ref, ot_ref, h_ref)


def fwd_outs(b, t, d):
    return [S((b, 3 * d, t), bf16), S((b, HEADS, t, t), bf16), S((b, 8, t), f32), S((b, d, t), bf16), S((b, t, d), bf16)]


def fwd_blocks(t, d, off):
    return [one(3 * d, t, off=off), one(HEADS, t, t, off=off), one(8, t, off=off), one(d, t, off=off), one(t, d, off=off)]


def call_attn_fwd_first(lay, slots, x, count):
    b, t, d = x.shape
    extra = [S((3 * d, d), bf16), S((16, d), f32), S((3 * d, 8), f32)]
    n_copies = OWNERS * (len(lay.first[0]) + len(lay.first[1]))
    return pl.pallas_call(
        functools.partial(attn_fwd_first, lay), grid=(count,),
        in_specs=[HBM] * 4 + [one(t, d)],
        out_specs=fwd_blocks(t, d, 0) + [full(a) for a in extra],
        out_shape=fwd_outs(b, t, d) + extra,
        scratch_shapes=[pltpu.VMEM((OWNERS * 16, d), bf16), pltpu.SemaphoreType.DMA((n_copies,))],
        compiler_params=params(24), cost_estimate=cost(4 * count), name="attn_fwd_first",
    )(*slots, x)


def call_attn_fwd_rest(x, w, vrow, vcol, outs, off, count):
    b, t, d = x.shape
    return pl.pallas_call(
        attn_fwd_rest, grid=(count,),
        in_specs=[one(t, d, off=off), full(w), full(vrow), full(vcol)] + [ANY] * 5,
        out_specs=fwd_blocks(t, d, off), out_shape=fwd_outs(b, t, d),
        input_output_aliases={4 + k: k for k in range(5)},
        compiler_params=params(24), cost_estimate=cost(4 * count), name="attn_fwd_rest",
    )(x, w, vrow, vcol, *outs)


def gelu_pair(u):
    cdf = 0.5 + 0.5 * lax.erf(u * (0.5 ** 0.5))
    pdf = jnp.exp(u * u * -0.5) * 0.3989422804014327
    return u * cdf, cdf + u * pdf


def mlp(lay, count, mine_a, mine_b, other_a, other_b, x_ref, ot_ref, cot_ref, vrow_ref,
        mid_ref, act_ref, dm_ref, dot_ref, wd_ref, dv_ref, keep_ref, give_ref,
        wp_ref, wu_ref, dwp_ref, dwu_ref, dwd_ref, h_ref, g_ref, xhat_ref, rstd_ref, du_ref, sems):
    i = pl.program_id(0)
    cols = lay.cols
    n, d, t = ot_ref.shape
    images = [slice(k * t, (k + 1) * t) for k in range(n)]

    weights_of = functools.partial(fetch, lay, lay.second, (mine_a, mine_b), (other_a, other_b), {"p": wp_ref, "u": wu_ref, "d": wd_ref}, sems)

    @pl.when(i == 0)
    def _():
        weights_of("pud")
        dwp_ref[...] = jnp.zeros_like(dwp_ref)
        dwu_ref[...] = jnp.zeros_like(dwu_ref)
        dwd_ref[...] = jnp.zeros_like(dwd_ref)
        dv_ref[...] = jnp.zeros_like(dv_ref)

    attn = [dot(ot_ref[k], wp_ref[...], 0, 1) for k in range(n)]
    for k, rows in enumerate(images):
        mid = x_ref[k] + (attn[k] + vrow_ref[6:7, :])
        mid_ref[k] = mid
        xhat, rstd = norm_stats(mid)
        xhat_ref[rows] = xhat
        rstd_ref[rows] = rstd
        h_ref[rows] = (xhat * vrow_ref[2:3, :] + vrow_ref[3:4, :]).astype(bf16)
        cot = cot_ref[k]
        g_ref[rows] = cot.astype(bf16)
        dv_ref[7:8, :] += jnp.sum(cot, axis=0, keepdims=True)
    up_bias = jnp.concatenate([vrow_ref[8 + j:9 + j, :] for j in range(cols)], axis=1)
    step = lay.ff // 3
    spans = [slice(j * step, (j + 1) * step) for j in range(3)]
    up_grads = []

    def hidden(span):
        total = jnp.zeros((1, step), f32)
        first = [dot(h_ref[rows], wu_ref[span], 1, 1) for rows in images]
        backs = [dot(g_ref[rows], wd_ref[:, span], 1, 0) for rows in images]
        for k, rows in enumerate(images):
            act, slope = gelu_pair(first[k] + up_bias[:, span])
            act_ref[k, :, span] = act.astype(bf16)
            du = backs[k] * slope
            du_ref[rows, span] = du.astype(bf16)
            total += jnp.sum(du, axis=0, keepdims=True)
        up_grads.append(total)

    def weights(span):
        act = jnp.concatenate([act_ref[k, :, span] for k in range(n)], axis=0)
        dwd_ref[:, span] += dot(g_ref[...], act, 0, 0)
        dwu_ref[span, :] += dot(du_ref[:, span], h_ref[...], 0, 0)

    for j, span in enumerate(spans):
        hidden(span)
        if j:
            weights(spans[j - 1])
    weights(spans[-1])
    up_grad = jnp.concatenate(up_grads, axis=1)
    for j in range(cols):
        dv_ref[8 + j:9 + j, :] += up_grad[:, j * d:(j + 1) * d]
    normed = [dot(du_ref[rows], wu_ref[...], 1, 0) for rows in images]
    for k, rows in enumerate(images):
        dh2 = normed[k]
        xhat = xhat_ref[rows]
        gy = dh2 * vrow_ref[2:3, :]
        m1 = jnp.mean(gy, axis=-1, keepdims=True)
        m2 = jnp.mean(gy * xhat, axis=-1, keepdims=True)
        dm = cot_ref[k] + rstd_ref[rows] * (gy - m1 - xhat * m2)
        dm_ref[k] = dm
        dml = dm.astype(bf16)
        dwp_ref[...] += dot(dml, ot_ref[k], 0, 1)
        dot_ref[k] = dot(wp_ref[...], dml, 0, 1).astype(bf16)
        dv_ref[2:3, :] += jnp.sum(dh2 * xhat, axis=0, keepdims=True)
        dv_ref[3:4, :] += jnp.sum(dh2, axis=0, keepdims=True)
        dv_ref[6:7, :] += jnp.sum(dm, axis=0, keepdims=True)

    @pl.when(i == count - 1)
    def _():
        emit(lay, lay.second, {"p": dwp_ref, "u": dwu_ref, "d": dwd_ref}, keep_ref, give_ref)


def call_mlp(lay, slots, x, ot, cot, vrow):
    b, t, d = x.shape
    ff = lay.ff
    n = 2 if b % 2 == 0 else 1
    hbm = pltpu.HBM
    acc = [hbm((d, ff), bf16), S((16, d), f32), S((OWNERS, lay.second_rows, d), bf16), S((OWNERS, lay.second_rows, d), bf16)]
    outs = [hbm((b, t, d), f32), hbm((b, t, ff), bf16), hbm((b, t, d), f32), S((b, d, t), bf16)] + acc
    n_copies = OWNERS * (len(lay.second[0]) + len(lay.second[1]))

    def some(*shape):
        return pl.BlockSpec((n,) + shape, lambda i: (i, 0, 0))

    scratch = [S((d, d), bf16), S((ff, d), bf16), S((d, d), f32), S((ff, d), f32), S((d, ff), f32), S((n * t, d), bf16),
               S((n * t, d), bf16), S((n * t, d), f32), S((n * t, 1), f32), S((n * t, ff), bf16)]
    return pl.pallas_call(
        functools.partial(mlp, lay, b // n), grid=(b // n,),
        in_specs=[HBM] * 4 + [some(t, d), some(d, t), some(t, d), full(vrow)],
        out_specs=[some(t, d), some(t, ff), some(t, d), some(d, t)] + [full(a) for a in acc],
        out_shape=outs,
        scratch_shapes=[pltpu.VMEM(a.shape, a.dtype) for a in scratch] + [pltpu.SemaphoreType.DMA((n_copies,))],
        compiler_params=params(MLP_MIB), cost_estimate=cost(24), name="mlp",
    )(*slots, x, ot, cot, vrow)


def attn_bwd_image(jt_ref, e_ref, il_ref, ot_ref, dot_ref, h_ref, dj_ref, dw_ref):
    t, d = h_ref.shape[1:]
    hs = d // HEADS
    def part(k, i):
        return jt_ref[0, k * d + i * hs:k * d + (i + 1) * hs, :]

    def begin(i):
        do = dot_ref[0, i * hs:(i + 1) * hs, :].astype(f32) * il_ref[0, i:i + 1, :]
        dd = jnp.sum(do * ot_ref[0, i * hs:(i + 1) * hs, :].astype(f32), axis=0, keepdims=True)
        dob = do.astype(bf16)
        return dd, dob, dot(part(2, i), dob, 0, 0)

    held = begin(0)
    for i in range(HEADS):
        dd, dob, dp = held
        if i + 1 < HEADS:
            held = begin(i + 1)
        eb = e_ref[0, i]
        ds = (eb.astype(f32) * (dp - dd)).astype(bf16)
        dj_ref[0, 2 * d + i * hs:2 * d + (i + 1) * hs, :] = dot(dob, eb, 1, 1).astype(bf16)
        dj_ref[0, i * hs:(i + 1) * hs, :] = (dot(part(1, i), ds, 1, 0) * 0.125).astype(bf16)
        dj_ref[0, d + i * hs:d + (i + 1) * hs, :] = (dot(part(0, i), ds, 1, 1) * 0.125).astype(bf16)
    hx = jnp.concatenate([h_ref[0], jnp.ones((t, 128), bf16)], axis=1)
    dw_ref[...] += dot(dj_ref[0], hx, 1, 0)


def attn_bwd_first(jt_ref, e_ref, il_ref, ot_ref, dot_ref, h_ref, dj_ref, dw_ref):
    @pl.when(pl.program_id(0) == 0)
    def _():
        dw_ref[...] = jnp.zeros_like(dw_ref)
    attn_bwd_image(jt_ref, e_ref, il_ref, ot_ref, dot_ref, h_ref, dj_ref, dw_ref)


def attn_bwd_last(lay, count, jt_ref, e_ref, il_ref, ot_ref, dot_ref, h_ref, dw_in_ref, w_ref, vrow_ref, dv_ref, dj_in_ref,
                  dj_ref, keep_ref, give_ref, dw_ref, vec_scr):
    i = pl.program_id(0)

    @pl.when(i == 0)
    def _():
        dw_ref[...] = dw_in_ref[...]
    attn_bwd_image(jt_ref, e_ref, il_ref, ot_ref, dot_ref, h_ref, dj_ref, dw_ref)

    @pl.when(i == count - 1)
    def _():
        d, s = lay.d, lay.piece
        w = w_ref[...].astype(f32)
        db = dw_ref[:, d:d + 1]
        gain = jnp.sum(w * (dw_ref[:, 0:d] - db * vrow_ref[1:2, :]), axis=0, keepdims=True) / vrow_ref[0:1, :]
        shift = jnp.sum(w * db, axis=0, keepdims=True)
        biases = jnp.transpose(dw_ref[:, d:d + 8])
        rows = [gain, shift, dv_ref[2:3, :], dv_ref[3:4, :], biases[0:1, 0:d], biases[0:1, 2 * d:3 * d]]
        rows += [dv_ref[k:k + 1, :] for k in range(6, 8 + lay.cols)]
        vec_scr[...] = jnp.zeros_like(vec_scr)
        for g in range(3 * OWNERS):
            at = g // 3 * 16 + g % 3
            vec_scr[at:at + 1, 0:s] = rows[g // 2][:, g % 2 * s:(g % 2 + 1) * s]
        emit(lay, lay.first, {"q": dw_ref, "v": vec_scr}, keep_ref, give_ref)


def bwd_blocks(t, d, off):
    return [one(3 * d, t, off=off), one(HEADS, t, t, off=off), one(8, t, off=off), one(d, t, off=off), one(d, t, off=off), one(t, d, off=off)]


def call_attn_bwd_first(acts, count):
    b, t, d = acts[-1].shape
    dw = S((3 * d, d + 128), f32)
    return pl.pallas_call(
        attn_bwd_first, grid=(count,), in_specs=bwd_blocks(t, d, 0),
        out_specs=[one(3 * d, t), full(dw)], out_shape=[S((b, 3 * d, t), bf16), dw],
        compiler_params=params(24), cost_estimate=cost(4 * count), name="attn_bwd_first",
    )(*acts)


def call_attn_bwd_last(lay, acts, dw, w, vrow, dv, dj, off, count):
    b, t, d = acts[-1].shape
    slots = [S((OWNERS, lay.first_rows, d), bf16), S((OWNERS, lay.first_rows, d), bf16)]
    return pl.pallas_call(
        functools.partial(attn_bwd_last, lay, count), grid=(count,),
        in_specs=bwd_blocks(t, d, off) + [full(dw), full(w), full(vrow), full(dv), ANY],
        out_specs=[one(3 * d, t, off=off)] + [full(a) for a in slots], out_shape=[S((b, 3 * d, t), bf16)] + slots,
        scratch_shapes=[pltpu.VMEM(dw.shape, f32), pltpu.VMEM((OWNERS * 16, d), f32)],
        input_output_aliases={10: 0},
        compiler_params=params(28), cost_estimate=cost(4 * count + 2), name="attn_bwd_last",
    )(*acts, dw, w, vrow, dv, dj)


def layer_end(mid_ref, act_ref, wd_ref, vrow_ref, lo_ref):
    lo_ref[0] = mid_ref[0] + (dot(act_ref[0], wd_ref[...], 1, 1) + vrow_ref[7:8, :])


def call_layer_end(mid, act, wd, vrow):
    b, t, d = mid.shape
    return pl.pallas_call(
        layer_end, grid=(b,), in_specs=[one(t, d), one(t, act.shape[2]), full(wd), full(vrow)],
        out_specs=one(t, d), out_shape=S((b, t, d), f32),
        compiler_params=params(16), cost_estimate=cost(4), name="layer_end",
    )(mid, act, wd, vrow)


def input_end(x_ref, dm_ref, dj_ref, w_ref, vrow_ref, gx_ref):
    dh = dot(dj_ref[0], w_ref[...], 0, 0)
    xhat, rstd = norm_stats(x_ref[0])
    gy = dh * vrow_ref[0:1, :]
    m1 = jnp.mean(gy, axis=-1, keepdims=True)
    m2 = jnp.mean(gy * xhat, axis=-1, keepdims=True)
    gx_ref[0] = dm_ref[0] + rstd * (gy - m1 - xhat * m2)


def call_input_end(x, dm, dj, w, vrow):
    b, t, d = x.shape
    return pl.pallas_call(
        input_end, grid=(b,), in_specs=[one(t, d), one(t, d), one(3 * d, t), full(w), full(vrow)],
        out_specs=one(t, d), out_shape=S((b, t, d), f32),
        compiler_params=params(16), cost_estimate=cost(4), name="input_end",
    )(x, dm, dj, w, vrow)


def adam_values(master, first, second, grad, rate, decay):
    first_new = beta_first * first + (1.0 - beta_first) * grad
    second_new = beta_second * second + (1.0 - beta_second) * grad * grad
    first_hat = first_new * (1.0 / (1.0 - beta_first ** STEP))
    second_hat = second_new * (1.0 / (1.0 - beta_second ** STEP))
    new = master - rate * (first_hat / (jnp.sqrt(second_hat) + adam_eps) + decay * master)
    return new, first_new, second_new, new.astype(bf16)


def adam_rows(refs, outs, rows, grad, rate, decay):
    for out, value in zip(outs, adam_values(*(r[rows] for r in refs), grad, rate, decay)):
        out[rows] = value


def adam(lay, halves, names, mine_ref, other_ref, *refs):
    core = lay.position()[1]
    count = len(names)
    states = {name: refs[3 * k:3 * k + 3] for k, name in enumerate(names)}
    outs = {name: refs[3 * count + 4 * k:3 * count + 4 * k + 4] for k, name in enumerate(names)}
    rates = {"q": 0.6 * lay.d ** -0.5, "p": 0.6 * lay.d ** -0.5, "u": 0.6 * lay.d ** -0.5, "d": 0.6 * lay.ff ** -0.5, "v": vector_rate}

    def step(half, src_ref):
        for name, start, rows, col, at in halves[half]:
            if name == "v":
                grad = jnp.concatenate([src_ref[at + k:at + k + 1, :lay.piece] for k in range(3)], axis=1)
                size = 3 * lay.piece
                new = adam_values(*(r[...].reshape(1, size) for r in states[name]), grad, rates[name], 0.0)
                for out, value in zip(outs[name], new):
                    out[...] = value.reshape(size)
            else:
                span = (slice(start, start + rows), slice(col * lay.d, (col + 1) * lay.d))
                adam_rows(states[name], outs[name], span, src_ref[at:at + rows, :], rates[name], matrix_decay)

    for half in range(2):
        @pl.when(core == half)
        def _():
            step(half, mine_ref)
            step(1 - half, other_ref)


def call_adam(lay, halves, mine, other, states):
    names = tuple(states)
    flat = [a for name in names for a in states[name]]
    outs = [S(states[name][0].shape, t) for name in names for t in (f32, f32, f32, bf16)]
    got = pl.pallas_call(
        functools.partial(adam, lay, halves, names),
        in_specs=[whole(a) for a in (mine, other, *flat)], out_specs=[whole(a) for a in outs], out_shape=outs,
        compiler_params=params(16), cost_estimate=cost(3), name="adam",
    )(mine, other, *flat)
    return {name: got[4 * k:4 * k + 4] for k, name in enumerate(names)}


def after(value, *earlier):
    return lax.optimization_barrier((value, *earlier))[0] if earlier else value


class Links:
    def __init__(self, mesh):
        self.wide, self.narrow = mesh.shape["wide"], mesh.shape["narrow"]
        bits = [1 << k for k in range(self.wide.bit_length() - 1)]
        self.orders = (bits[::-1], bits[:1] + bits[:0:-1])
        self.rounds = len(bits)
        self.masks = []
        for order in self.orders:
            masks = [0]
            for bit in order:
                masks = masks + [m ^ bit for m in masks]
            self.masks.append(masks)
        self.slots = [[masks.index(m) for m in range(self.wide)] for masks in self.masks]

    def permute(self, value, partner):
        pairs = []
        for n in range(self.narrow):
            for w in range(self.wide):
                n2, w2 = partner(n, w)
                pairs.append((n * self.wide + w, n2 * self.wide + w2))
        return lax.ppermute(value, ("narrow", "wide"), pairs)

    def core(self, value):
        return self.permute(value, lambda n, w: (n ^ 1, w))

    def step(self, value, k):
        return self.permute(value, lambda n, w: (n, w ^ self.orders[n % 2][k]))

    def others(self, value):
        total = value.astype(f32)
        bit = 2
        while bit < self.narrow:
            low = total.astype(bf16)
            total = low.astype(f32) + self.permute(low, lambda n, w, bit=bit: (n ^ bit, w)).astype(f32)
            bit *= 2
        return total

    def here(self):
        return lax.axis_index("wide"), lax.axis_index("narrow") % 2

    def gather(self, half):
        moving = Gather(self, half)
        for _ in range(self.rounds):
            moving.round()
        return moving.core()

    def reduce(self, keep, give):
        moving = Reduce(self, keep, give)
        moving.core()
        for _ in range(self.rounds):
            moving.round()
        moving.others()
        return moving.finish()


    def gather_rows(self, packed):
        me, core = self.here()
        rows, columns = packed.shape
        mine, other = self.gather(lax.dynamic_slice_in_dim(packed, core * (rows // 2), rows // 2))
        both = jnp.concatenate([mine, other], axis=0)
        relative = jnp.arange(self.wide) ^ me
        first = jnp.take(jnp.array(self.slots[0]), relative) + core * self.wide
        second = jnp.take(jnp.array(self.slots[1]), relative) + (1 - core) * self.wide
        index = jnp.stack([first, second], axis=1).reshape(-1)
        return jnp.take(both, index, axis=0).reshape(self.wide, rows, columns)

    def reduce_rows(self, packed):
        me, core = self.here()
        _, rows, columns = packed.shape
        halves = packed.reshape(2 * self.wide, rows // 2, columns)
        masks = jnp.array(self.masks)
        keep = jnp.take(halves, (masks[core] ^ me) * 2 + core, axis=0)
        give = jnp.take(halves, (masks[1 - core] ^ me) * 2 + (1 - core), axis=0)
        total, other = self.reduce(keep, give.astype(bf16))
        return jnp.where(core == 0, jnp.concatenate([total, other]), jnp.concatenate([other, total]))


class Gather:
    def __init__(self, links, half):
        self.links, self.held, self.k = links, half[None], 0

    def round(self, *beside):
        got = self.links.step(self.held, self.k)
        self.held = jnp.concatenate([after(self.held, *beside), got], axis=0)
        self.k += 1

    def core(self):
        return self.held, self.links.core(self.held)

    def last(self):
        self.got = self.links.step(self.held, self.k)
        self.other = self.links.core(self.held)

    def slots(self):
        return self.held, self.got, self.other, self.links.core(self.got)


class Reduce:
    def __init__(self, links, keep, give):
        self.links, self.held, self.give, self.k = links, keep, give, links.rounds

    def core(self, *beside):
        got = self.links.core(self.give)
        self.held = after(self.held, *beside).astype(f32) + got.astype(f32)

    def round(self, *beside):
        self.k -= 1
        half = self.held.shape[0] // 2
        self.held = after(self.held[:half], *beside) + self.links.step(self.held[half:].astype(bf16), self.k).astype(f32)

    def others(self):
        self.held = self.links.others(self.held[0])

    def finish(self):
        return self.held, self.links.core(self.held)


class Here:
    def __init__(self, held, other):
        self.held, self.other = held, other

    def round(self, *beside):
        pass

    def last(self):
        self.got = None

    def slots(self):
        half = self.held.shape[0] // 2
        return self.held[:half], self.held[half:], self.other[:half], self.other[half:]

    def others(self):
        pass

    def core(self, *beside):
        return self.held, self.other

    finish = core


def to_rows(block, columns):
    return jnp.concatenate([block[..., j:j + columns] for j in range(0, block.shape[-1], columns)], axis=-2)


def from_rows(block, count):
    return jnp.concatenate(jnp.split(block, count, axis=-2), axis=-1)


def padded(block, multiple):
    extra = -block.shape[-2] % multiple
    return jnp.pad(block, [(0, 0)] * (block.ndim - 2) + [(0, extra), (0, 0)])


def to_slots(lay, halves, rows, arrays):
    out = []
    for half in halves:
        parts = []
        for name, start, count, col, _ in half:
            block = arrays[name].reshape(OWNERS, -1, arrays[name].shape[-1])
            parts.append(block[:, start:start + count, col * lay.d:(col + 1) * lay.d])
        block = jnp.concatenate(parts, axis=1)
        out.append(jnp.pad(block, ((0, 0), (0, rows - block.shape[1]), (0, 0))))
    return out


def from_slots(halves, both):
    found = {}
    for half, block in zip(halves, both):
        for name, start, count, col, at in half:
            found.setdefault(name, {})[(start, col)] = block[:, at:at + count].astype(f32)
    out = {}
    for name, parts in found.items():
        axis = 2 if max(col for _, col in parts) else 1
        block = jnp.concatenate([parts[key] for key in sorted(parts)], axis=axis)
        out[name] = block.reshape(-1, block.shape[-1])
    return out


FIRST_IMAGES = 2
BACK_IMAGES = 1


def compute(lay, x, cot, gather, reduce, finish_second, rounds):
    b = x.shape[0]
    k = min(FIRST_IMAGES, b - 1)
    one, two = gather
    one.round()
    two.held = after(two.held, one.held)
    two.round()
    for _ in range(rounds - 2):
        one.round()
    one.last()
    if one.got is not None:
        one.got, two.held = lax.optimization_barrier((one.got, two.held))
    first = one.slots()
    *outs, wq, vrow, vcol = call_attn_fwd_first(lay, first, x, k)
    for _ in range(rounds - 2):
        two.round(vcol)
    *outs, two.held = lax.optimization_barrier((*outs, two.held))
    jt, e, il, ot, h = call_attn_fwd_rest(x, wq, vrow, vcol, outs, k, b - k)
    two.last()
    if two.got is not None:
        ot, two.got = lax.optimization_barrier((ot, two.got))
    second = two.slots()
    mid, act, dm, dot_, wd, dv, keep, give = call_mlp(lay, second, x, ot, cot, vrow)
    down = reduce(keep, give)
    acts = (jt, e, il, ot, dot_, h)
    dj, dw = call_attn_bwd_first(acts, BACK_IMAGES)
    down.core(dw)
    dw, down.held = lax.optimization_barrier((dw, down.held))
    dj, keep, give = call_attn_bwd_last(lay, acts, dw, wq, vrow, dv, dj, BACK_IMAGES, b - BACK_IMAGES)
    down.round(dj)
    up = reduce(keep, give)
    up.core(down.held)
    for _ in range(rounds - 2):
        down.round(up.held)
    dj, up.held = lax.optimization_barrier((dj, up.held))
    up.round()
    gx = call_input_end(x, dm, dj, wq, vrow)
    gx, up.held = lax.optimization_barrier((gx, up.held))
    lo = call_layer_end(after(mid, gx), act, wd, vrow)
    up.round(lo, down.held)
    down.round()
    for _ in range(rounds - 2):
        up.round(down.held)
    down.others()
    up.others()
    up.held, down.held = lax.optimization_barrier((up.held, down.held))
    second_new = finish_second(*down.finish())
    return lo, gx, up.finish(), second_new


def eight_owners(links, lay, x, cot, states):
    masters = {name: s[0] for name, s in states.items()}
    first, second = call_pack(lay, *(masters[name] for name in "qpudv"))
    gather = Gather(links, first), Gather(links, second)

    def finish_second(mine, other):
        return call_adam(lay, lay.second, mine, other, {name: states[name] for name in "pud"})

    lo, gx, first_sum, new = compute(lay, x, cot, gather, functools.partial(Reduce, links), finish_second, links.rounds)
    new |= call_adam(lay, lay.first, *first_sum, {name: states[name] for name in "qv"})
    return lo, gx, new


def any_owners(links, lay, x, cot, states):
    n, d = links.wide, lay.d
    masters = {name: s[0] for name, s in states.items()}
    v_size = masters["v"].shape[0]
    v_rows = -(-v_size // d)

    def vec_rows(v):
        return jnp.pad(v, ((0, 0), (0, v_rows * d - v_size))).reshape(-1, v_rows, d)

    def split(block):
        at, out = 0, {}
        for name in "qpu":
            rows = masters[name].shape[0]
            out[name] = block[:, at:at + rows]
            at += rows
        rows = masters["d"].shape[0]
        out["d"] = from_rows(block[:, at:at + rows * lay.cols], lay.cols)
        at += rows * lay.cols
        out["v"] = block[:, at:at + v_rows].reshape(-1, 1, v_rows * d)[:, :, :v_size]
        return {name: a.reshape(-1, a.shape[2]) for name, a in out.items()}

    def join(a, lead):
        blocks = [a[name].reshape(lead, -1, d) for name in "qpu"]
        blocks += [to_rows(a["d"].reshape(lead, -1, lay.ff), d), vec_rows(a["v"].reshape(lead, v_size))]
        return padded(jnp.concatenate(blocks, axis=1), 32)

    def eighths(v):
        return jnp.pad(v.reshape(OWNERS, 3, lay.piece), ((0, 0), (0, 13), (0, d - lay.piece))).reshape(-1, d)

    got = split(links.gather_rows(join(masters, 1)[0].astype(bf16)))
    got["v"] = eighths(got["v"])
    gather = Here(*to_slots(lay, lay.first, lay.first_rows, got)), Here(*to_slots(lay, lay.second, lay.second_rows, got))
    lo, gx, first_sum, second_sum = compute(lay, x, cot, gather, Here, lambda *both: both, 3)
    grads = from_slots(lay.first, first_sum) | from_slots(lay.second, second_sum)
    grads["v"] = grads["v"].reshape(OWNERS, 16, d)[:, :3, :lay.piece]
    mine = split(links.reduce_rows(join(grads, n))[None])
    rates = {"q": 0.6 * d ** -0.5, "p": 0.6 * d ** -0.5, "u": 0.6 * d ** -0.5, "d": 0.6 * lay.ff ** -0.5, "v": vector_rate}
    new = {}
    for name, refs in states.items():
        new[name] = adam_values(*refs, mine[name].reshape(refs[0].shape), rates[name], 0.0 if name == "v" else matrix_decay)
    return lo, gx, new


def per_device(links, x, cot, *arrays):
    if links.wide == OWNERS:
        run, orders, position = eight_owners, links.orders, links.here
    else:
        run, orders, position = any_owners, [[1, 2, 4]] * 2, lambda: (0, 0)
    lay = Layout(x.shape[2], arrays[3].shape[1], orders, position)
    names = "qpudv"
    states = {name: arrays[k::5] for k, name in enumerate(names)}
    lo, gx, new = run(links, lay, x, cot, states)
    return (lo, gx, *(a for name in names for a in new[name]))


def solution(mesh):
    tokens = P(("narrow", "wide"), None, None)
    matrix, vector = P("wide", None), P("wide")
    state = (matrix,) * 4 + (vector,)
    return jax.shard_map(
        functools.partial(per_device, Links(mesh)),
        mesh=mesh,
        in_specs=(tokens, tokens) + state * 3,
        out_specs=(tokens, tokens) + (matrix,) * 16 + (vector,) * 4,
        check_vma=False,
    )
```

```python
import functools

import jax
import jax.numpy as jnp
from jax import lax
from jax.experimental import pallas as pl
from jax.experimental.pallas import tpu as pltpu
from jax.sharding import PartitionSpec as P

STEP = 10
HEADS = 6
EPS = 1e-6
OWNERS = 8
MLP_MIB = 30
beta_first = 0.5
beta_second = 0.5
adam_eps = 1e-08
matrix_decay = 0.01
vector_rate = 0.3
bf16, f32 = jnp.bfloat16, jnp.float32
S = jax.ShapeDtypeStruct
ANY = pl.BlockSpec(memory_space=pl.ANY)
HBM = pl.BlockSpec(memory_space=pltpu.HBM)


def dot(a, b, ca, cb):
    return lax.dot_general(a, b, (((ca,), (cb,)), ((), ())), preferred_element_type=f32)


def norm_stats(v):
    mean = jnp.mean(v, axis=-1, keepdims=True)
    cen = v - mean
    var = jnp.mean(cen * cen, axis=-1, keepdims=True)
    rstd = lax.rsqrt(var + EPS)
    return cen * rstd, rstd


def one(*shape, off=0):
    return pl.BlockSpec((1,) + shape, lambda i: (i + off,) + (0,) * len(shape))


def full(a):
    return pl.BlockSpec(a.shape, lambda i: (0,) * len(a.shape))


def whole(a):
    return pl.BlockSpec(a.shape, lambda: (0,) * len(a.shape))


def params(mib):
    return pltpu.CompilerParams(vmem_limit_bytes=mib << 20)


def cost(us):
    return pl.CostEstimate(flops=int(us * 1.0e9), bytes_accessed=1 << 20, transcendentals=0)


class Layout:
    def __init__(self, d, ff, orders, position):
        self.d, self.ff, self.cols = d, ff, ff // d
        self.position = position
        self.masks = [[sum(bit for k, bit in enumerate(order) if j >> k & 1) for j in range(OWNERS)] for order in orders]
        self.q, self.p, self.u = 3 * d // OWNERS, d // OWNERS, ff // OWNERS
        q0 = (self.q // 2 + 15) // 16 * 16
        self.first = ((("q", 0, q0, 0, 0),), (("q", q0, self.q - q0, 0, 0), ("v", 0, 16, 0, self.q - q0)))
        self.first_rows = max(q0, self.q - q0 + 16)
        p0 = 16
        down = tuple(("d", 0, self.p, j, j * self.p) for j in range(self.cols))
        self.second = (
            (("u", 0, self.u, 0, 0), ("p", 0, p0, 0, self.u)),
            down + (("p", p0, self.p - p0, 0, self.cols * self.p),),
        )
        self.second_rows = max(self.u + p0, self.cols * self.p + self.p - p0)
        self.piece = (8 * d + ff) // (3 * OWNERS)


def place(lay, piece, owner):
    name, start, rows, col, _ = piece
    size = {"q": lay.q, "p": lay.p, "u": lay.u, "d": lay.p, "v": 16}[name]
    at = owner * size + start
    if not isinstance(at, int):
        at = pl.multiple_of(at, 16)
    return pl.ds(at, rows), pl.ds(col * lay.d, lay.d)


def pack(lay, q_hbm, p_hbm, u_hbm, d_hbm, v_hbm, first_ref, second_ref, q_ref, p_ref, u_ref, d_ref, v_ref, sems):
    refs = {"q": q_ref, "p": p_ref, "u": u_ref, "d": d_ref}
    moves = [pltpu.make_async_copy(a, b, sems.at[i]) for i, (a, b) in enumerate(
        ((q_hbm, q_ref), (v_hbm, v_ref), (p_hbm, p_ref), (u_hbm, u_ref), (d_hbm, d_ref)))]
    for move in moves:
        move.start()
    for move in moves:
        move.wait()
    core = lay.position()[1]
    v = v_ref[...].reshape(1, v_ref.shape[0])

    def fill(halves, out_ref):
        end = 0
        for name, start, rows, col, at in halves:
            if name == "v":
                out_ref[at:at + rows, :] = jnp.zeros((rows, lay.d), bf16)
                for k in range(3):
                    out_ref[at + k:at + k + 1, :lay.piece] = v[:, k * lay.piece:(k + 1) * lay.piece].astype(bf16)
            else:
                out_ref[at:at + rows, :] = refs[name][start:start + rows, col * lay.d:(col + 1) * lay.d].astype(bf16)
            end = at + rows
        if end < out_ref.shape[0]:
            out_ref[end:, :] = jnp.zeros((out_ref.shape[0] - end, lay.d), bf16)

    for half in range(2):
        @pl.when(core == half)
        def _():
            fill(lay.first[half], first_ref)
            fill(lay.second[half], second_ref)


def call_pack(lay, q, p, u, d, v):
    outs = [S((lay.first_rows, lay.d), bf16), S((lay.second_rows, lay.d), bf16)]
    return pl.pallas_call(
        functools.partial(pack, lay), in_specs=[HBM] * 5,
        out_specs=[whole(a) for a in outs], out_shape=outs,
        scratch_shapes=[pltpu.VMEM(a.shape, f32) for a in (q, p, u, d, v)] + [pltpu.SemaphoreType.DMA((5,))],
        compiler_params=params(60), name="pack",
    )(q, p, u, d, v)


def fetch(lay, halves, mine_refs, other_refs, dests, sems, names, start=True, wait=True):
    me, core = lay.position()
    each = OWNERS // 2

    def copies(half, src_refs, base):
        out, count = [], 0
        for j in range(OWNERS):
            for piece in halves[half]:
                name, _, rows, _, at = piece
                r, c = place(lay, piece, me ^ lay.masks[half][j])
                dst = dests[name].at[r] if name != "d" else dests[name].at[r, c]
                if name in names:
                    out.append(pltpu.make_async_copy(src_refs[j // each].at[j % each, pl.ds(at, rows)], dst, sems.at[base + count]))
                count += 1
        return out

    for half in range(2):
        @pl.when(core == half)
        def _():
            both = copies(half, mine_refs, 0) + copies(1 - half, other_refs, OWNERS * len(halves[half]))
            if start:
                for c in both:
                    c.start()
            if wait:
                for c in both:
                    c.wait()


def emit(lay, halves, arrays, keep_ref, give_ref):
    me, core = lay.position()

    def fill(half, out_ref):
        for j in range(OWNERS):
            end = 0
            for piece in halves[half]:
                name, _, rows, _, at = piece
                r, c = place(lay, piece, me ^ lay.masks[half][j])
                out_ref[j, at:at + rows, :] = arrays[name][r, c].astype(out_ref.dtype)
                end = at + rows
            if end < out_ref.shape[1]:
                out_ref[j, end:, :] = jnp.zeros((out_ref.shape[1] - end, lay.d), out_ref.dtype)

    for half in range(2):
        @pl.when(core == half)
        def _():
            fill(half, keep_ref)
            fill(1 - half, give_ref)


def attn_fwd_image(x_ref, w_ref, vrow_ref, vcol_ref, jt_ref, e_ref, il_ref, ot_ref, h_ref):
    xhat, _ = norm_stats(x_ref[0])
    h = (xhat * vrow_ref[0:1, :] + vrow_ref[1:2, :]).astype(bf16)
    h_ref[0] = h
    d = h.shape[1]
    hs = d // HEADS
    jt = dot(w_ref[...], h, 1, 1) + vcol_ref[:, 0:1]
    jt_ref[0] = jt.astype(bf16)
    def part(k, i):
        return jt_ref[0, k * d + i * hs:k * d + (i + 1) * hs, :]

    def scores(i):
        return dot(part(1, i) * 0.125, part(0, i), 0, 0)

    st = scores(0)
    for i in range(HEADS):
        later = scores(i + 1) if i + 1 < HEADS else None
        m = jnp.max(st, axis=0, keepdims=True)
        e = jnp.exp(st - m)
        l = jnp.sum(e, axis=0, keepdims=True)
        eb = e.astype(bf16)
        e_ref[0, i] = eb
        il = 1.0 / l
        il_ref[0, i:i + 1, :] = il
        ot_ref[0, i * hs:(i + 1) * hs, :] = (dot(part(2, i), eb, 1, 0) * il).astype(bf16)
        st = later


def attn_fwd_first(lay, mine_a, mine_b, other_a, other_b, x_ref, jt_ref, e_ref, il_ref, ot_ref, h_ref, w_ref, vrow_ref, vcol_ref, vec_scr, sems):
    @pl.when(pl.program_id(0) == 0)
    def _():
        fetch(lay, lay.first, (mine_a, mine_b), (other_a, other_b), {"q": w_ref, "v": vec_scr}, sems, "qv")
        d, s = lay.d, lay.piece
        vrow_ref[...] = jnp.zeros_like(vrow_ref)
        for r in range(8 + lay.cols):
            for k in range(2):
                g = 2 * r + k
                row = vec_scr[g // 3 * 16:g // 3 * 16 + 16, :].astype(f32)[g % 3:g % 3 + 1, :s]
                vrow_ref[r:r + 1, k * s:(k + 1) * s] = row
        cols = jnp.transpose(vrow_ref[0:8, :])
        vcol_ref[...] = jnp.zeros_like(vcol_ref)
        vcol_ref[0:d, 0:1] = cols[:, 4:5]
        vcol_ref[2 * d:3 * d, 0:1] = cols[:, 5:6]
    attn_fwd_image(x_ref, w_ref, vrow_ref, vcol_ref, jt_ref, e_ref, il_ref, ot_ref, h_ref)


def attn_fwd_rest(x_ref, w_ref, vrow_ref, vcol_ref, a, b, c, d, e, jt_ref, e_ref, il_ref, ot_ref, h_ref):
    attn_fwd_image(x_ref, w_ref, vrow_ref, vcol_ref, jt_ref, e_ref, il_ref, ot_ref, h_ref)


def fwd_outs(b, t, d):
    return [S((b, 3 * d, t), bf16), S((b, HEADS, t, t), bf16), S((b, 8, t), f32), S((b, d, t), bf16), S((b, t, d), bf16)]


def fwd_blocks(t, d, off):
    return [one(3 * d, t, off=off), one(HEADS, t, t, off=off), one(8, t, off=off), one(d, t, off=off), one(t, d, off=off)]


def call_attn_fwd_first(lay, slots, x, count):
    b, t, d = x.shape
    extra = [S((3 * d, d), bf16), S((16, d), f32), S((3 * d, 8), f32)]
    n_copies = OWNERS * (len(lay.first[0]) + len(lay.first[1]))
    return pl.pallas_call(
        functools.partial(attn_fwd_first, lay), grid=(count,),
        in_specs=[HBM] * 4 + [one(t, d)],
        out_specs=fwd_blocks(t, d, 0) + [full(a) for a in extra],
        out_shape=fwd_outs(b, t, d) + extra,
        scratch_shapes=[pltpu.VMEM((OWNERS * 16, d), bf16), pltpu.SemaphoreType.DMA((n_copies,))],
        compiler_params=params(24), cost_estimate=cost(4 * count), name="attn_fwd_first",
    )(*slots, x)


def call_attn_fwd_rest(x, w, vrow, vcol, outs, off, count):
    b, t, d = x.shape
    return pl.pallas_call(
        attn_fwd_rest, grid=(count,),
        in_specs=[one(t, d, off=off), full(w), full(vrow), full(vcol)] + [ANY] * 5,
        out_specs=fwd_blocks(t, d, off), out_shape=fwd_outs(b, t, d),
        input_output_aliases={4 + k: k for k in range(5)},
        compiler_params=params(24), cost_estimate=cost(4 * count), name="attn_fwd_rest",
    )(x, w, vrow, vcol, *outs)


def gelu_pair(u):
    cdf = 0.5 + 0.5 * lax.erf(u * (0.5 ** 0.5))
    pdf = jnp.exp(u * u * -0.5) * 0.3989422804014327
    return u * cdf, cdf + u * pdf


def mlp(lay, count, mine_a, mine_b, other_a, other_b, x_ref, ot_ref, cot_ref, vrow_ref,
        mid_ref, act_ref, dm_ref, dot_ref, wd_ref, dv_ref, keep_ref, give_ref,
        wp_ref, wu_ref, dwp_ref, dwu_ref, dwd_ref, h_ref, g_ref, xhat_ref, rstd_ref, du_ref, sems):
    i = pl.program_id(0)
    cols = lay.cols
    n, d, t = ot_ref.shape
    images = [slice(k * t, (k + 1) * t) for k in range(n)]

    weights_of = functools.partial(fetch, lay, lay.second, (mine_a, mine_b), (other_a, other_b), {"p": wp_ref, "u": wu_ref, "d": wd_ref}, sems)

    @pl.when(i == 0)
    def _():
        weights_of("pud")
        dwp_ref[...] = jnp.zeros_like(dwp_ref)
        dwu_ref[...] = jnp.zeros_like(dwu_ref)
        dwd_ref[...] = jnp.zeros_like(dwd_ref)
        dv_ref[...] = jnp.zeros_like(dv_ref)

    attn = [dot(ot_ref[k], wp_ref[...], 0, 1) for k in range(n)]
    for k, rows in enumerate(images):
        mid = x_ref[k] + (attn[k] + vrow_ref[6:7, :])
        mid_ref[k] = mid
        xhat, rstd = norm_stats(mid)
        xhat_ref[rows] = xhat
        rstd_ref[rows] = rstd
        h_ref[rows] = (xhat * vrow_ref[2:3, :] + vrow_ref[3:4, :]).astype(bf16)
        cot = cot_ref[k]
        g_ref[rows] = cot.astype(bf16)
        dv_ref[7:8, :] += jnp.sum(cot, axis=0, keepdims=True)
    up_bias = jnp.concatenate([vrow_ref[8 + j:9 + j, :] for j in range(cols)], axis=1)
    step = lay.ff // 3
    spans = [slice(j * step, (j + 1) * step) for j in range(3)]
    up_grads = []

    def hidden(span):
        total = jnp.zeros((1, step), f32)
        first = [dot(h_ref[rows], wu_ref[span], 1, 1) for rows in images]
        backs = [dot(g_ref[rows], wd_ref[:, span], 1, 0) for rows in images]
        for k, rows in enumerate(images):
            act, slope = gelu_pair(first[k] + up_bias[:, span])
            act_ref[k, :, span] = act.astype(bf16)
            du = backs[k] * slope
            du_ref[rows, span] = du.astype(bf16)
            total += jnp.sum(du, axis=0, keepdims=True)
        up_grads.append(total)

    def weights(span):
        act = jnp.concatenate([act_ref[k, :, span] for k in range(n)], axis=0)
        dwd_ref[:, span] += dot(g_ref[...], act, 0, 0)
        dwu_ref[span, :] += dot(du_ref[:, span], h_ref[...], 0, 0)

    for j, span in enumerate(spans):
        hidden(span)
        if j:
            weights(spans[j - 1])
    weights(spans[-1])
    up_grad = jnp.concatenate(up_grads, axis=1)
    for j in range(cols):
        dv_ref[8 + j:9 + j, :] += up_grad[:, j * d:(j + 1) * d]
    normed = [dot(du_ref[rows], wu_ref[...], 1, 0) for rows in images]
    for k, rows in enumerate(images):
        dh2 = normed[k]
        xhat = xhat_ref[rows]
        gy = dh2 * vrow_ref[2:3, :]
        m1 = jnp.mean(gy, axis=-1, keepdims=True)
        m2 = jnp.mean(gy * xhat, axis=-1, keepdims=True)
        dm = cot_ref[k] + rstd_ref[rows] * (gy - m1 - xhat * m2)
        dm_ref[k] = dm
        dml = dm.astype(bf16)
        dwp_ref[...] += dot(dml, ot_ref[k], 0, 1)
        dot_ref[k] = dot(wp_ref[...], dml, 0, 1).astype(bf16)
        dv_ref[2:3, :] += jnp.sum(dh2 * xhat, axis=0, keepdims=True)
        dv_ref[3:4, :] += jnp.sum(dh2, axis=0, keepdims=True)
        dv_ref[6:7, :] += jnp.sum(dm, axis=0, keepdims=True)

    @pl.when(i == count - 1)
    def _():
        emit(lay, lay.second, {"p": dwp_ref, "u": dwu_ref, "d": dwd_ref}, keep_ref, give_ref)


def call_mlp(lay, slots, x, ot, cot, vrow):
    b, t, d = x.shape
    ff = lay.ff
    n = 2 if b % 2 == 0 else 1
    hbm = pltpu.HBM
    acc = [hbm((d, ff), bf16), S((16, d), f32), S((OWNERS, lay.second_rows, d), bf16), S((OWNERS, lay.second_rows, d), bf16)]
    outs = [hbm((b, t, d), f32), hbm((b, t, ff), bf16), hbm((b, t, d), f32), S((b, d, t), bf16)] + acc
    n_copies = OWNERS * (len(lay.second[0]) + len(lay.second[1]))

    def some(*shape):
        return pl.BlockSpec((n,) + shape, lambda i: (i, 0, 0))

    scratch = [S((d, d), bf16), S((ff, d), bf16), S((d, d), f32), S((ff, d), f32), S((d, ff), f32), S((n * t, d), bf16),
               S((n * t, d), bf16), S((n * t, d), f32), S((n * t, 1), f32), S((n * t, ff), bf16)]
    return pl.pallas_call(
        functools.partial(mlp, lay, b // n), grid=(b // n,),
        in_specs=[HBM] * 4 + [some(t, d), some(d, t), some(t, d), full(vrow)],
        out_specs=[some(t, d), some(t, ff), some(t, d), some(d, t)] + [full(a) for a in acc],
        out_shape=outs,
        scratch_shapes=[pltpu.VMEM(a.shape, a.dtype) for a in scratch] + [pltpu.SemaphoreType.DMA((n_copies,))],
        compiler_params=params(MLP_MIB), cost_estimate=cost(24), name="mlp",
    )(*slots, x, ot, cot, vrow)


def attn_bwd_image(jt_ref, e_ref, il_ref, ot_ref, dot_ref, h_ref, dj_ref, dw_ref):
    t, d = h_ref.shape[1:]
    hs = d // HEADS
    def part(k, i):
        return jt_ref[0, k * d + i * hs:k * d + (i + 1) * hs, :]

    def begin(i):
        do = dot_ref[0, i * hs:(i + 1) * hs, :].astype(f32) * il_ref[0, i:i + 1, :]
        dd = jnp.sum(do * ot_ref[0, i * hs:(i + 1) * hs, :].astype(f32), axis=0, keepdims=True)
        dob = do.astype(bf16)
        return dd, dob, dot(part(2, i), dob, 0, 0)

    held = begin(0)
    for i in range(HEADS):
        dd, dob, dp = held
        if i + 1 < HEADS:
            held = begin(i + 1)
        eb = e_ref[0, i]
        ds = (eb.astype(f32) * (dp - dd)).astype(bf16)
        dj_ref[0, 2 * d + i * hs:2 * d + (i + 1) * hs, :] = dot(dob, eb, 1, 1).astype(bf16)
        dj_ref[0, i * hs:(i + 1) * hs, :] = (dot(part(1, i), ds, 1, 0) * 0.125).astype(bf16)
        dj_ref[0, d + i * hs:d + (i + 1) * hs, :] = (dot(part(0, i), ds, 1, 1) * 0.125).astype(bf16)
    hx = jnp.concatenate([h_ref[0], jnp.ones((t, 128), bf16)], axis=1)
    dw_ref[...] += dot(dj_ref[0], hx, 1, 0)


def attn_bwd_first(jt_ref, e_ref, il_ref, ot_ref, dot_ref, h_ref, dj_ref, dw_ref):
    @pl.when(pl.program_id(0) == 0)
    def _():
        dw_ref[...] = jnp.zeros_like(dw_ref)
    attn_bwd_image(jt_ref, e_ref, il_ref, ot_ref, dot_ref, h_ref, dj_ref, dw_ref)


def attn_bwd_last(lay, count, jt_ref, e_ref, il_ref, ot_ref, dot_ref, h_ref, dw_in_ref, w_ref, vrow_ref, dv_ref, dj_in_ref,
                  dj_ref, keep_ref, give_ref, dw_ref, vec_scr):
    i = pl.program_id(0)

    @pl.when(i == 0)
    def _():
        dw_ref[...] = dw_in_ref[...]
    attn_bwd_image(jt_ref, e_ref, il_ref, ot_ref, dot_ref, h_ref, dj_ref, dw_ref)

    @pl.when(i == count - 1)
    def _():
        d, s = lay.d, lay.piece
        w = w_ref[...].astype(f32)
        db = dw_ref[:, d:d + 1]
        gain = jnp.sum(w * (dw_ref[:, 0:d] - db * vrow_ref[1:2, :]), axis=0, keepdims=True) / vrow_ref[0:1, :]
        shift = jnp.sum(w * db, axis=0, keepdims=True)
        biases = jnp.transpose(dw_ref[:, d:d + 8])
        rows = [gain, shift, dv_ref[2:3, :], dv_ref[3:4, :], biases[0:1, 0:d], biases[0:1, 2 * d:3 * d]]
        rows += [dv_ref[k:k + 1, :] for k in range(6, 8 + lay.cols)]
        vec_scr[...] = jnp.zeros_like(vec_scr)
        for g in range(3 * OWNERS):
            at = g // 3 * 16 + g % 3
            vec_scr[at:at + 1, 0:s] = rows[g // 2][:, g % 2 * s:(g % 2 + 1) * s]
        emit(lay, lay.first, {"q": dw_ref, "v": vec_scr}, keep_ref, give_ref)


def bwd_blocks(t, d, off):
    return [one(3 * d, t, off=off), one(HEADS, t, t, off=off), one(8, t, off=off), one(d, t, off=off), one(d, t, off=off), one(t, d, off=off)]


def call_attn_bwd_first(acts, count):
    b, t, d = acts[-1].shape
    dw = S((3 * d, d + 128), f32)
    return pl.pallas_call(
        attn_bwd_first, grid=(count,), in_specs=bwd_blocks(t, d, 0),
        out_specs=[one(3 * d, t), full(dw)], out_shape=[S((b, 3 * d, t), bf16), dw],
        compiler_params=params(24), cost_estimate=cost(4 * count), name="attn_bwd_first",
    )(*acts)


def call_attn_bwd_last(lay, acts, dw, w, vrow, dv, dj, off, count):
    b, t, d = acts[-1].shape
    slots = [S((OWNERS, lay.first_rows, d), bf16), S((OWNERS, lay.first_rows, d), bf16)]
    return pl.pallas_call(
        functools.partial(attn_bwd_last, lay, count), grid=(count,),
        in_specs=bwd_blocks(t, d, off) + [full(dw), full(w), full(vrow), full(dv), ANY],
        out_specs=[one(3 * d, t, off=off)] + [full(a) for a in slots], out_shape=[S((b, 3 * d, t), bf16)] + slots,
        scratch_shapes=[pltpu.VMEM(dw.shape, f32), pltpu.VMEM((OWNERS * 16, d), f32)],
        input_output_aliases={10: 0},
        compiler_params=params(28), cost_estimate=cost(4 * count + 2), name="attn_bwd_last",
    )(*acts, dw, w, vrow, dv, dj)


def layer_end(mid_ref, act_ref, wd_ref, vrow_ref, lo_ref):
    lo_ref[0] = mid_ref[0] + (dot(act_ref[0], wd_ref[...], 1, 1) + vrow_ref[7:8, :])


def call_layer_end(mid, act, wd, vrow):
    b, t, d = mid.shape
    return pl.pallas_call(
        layer_end, grid=(b,), in_specs=[one(t, d), one(t, act.shape[2]), full(wd), full(vrow)],
        out_specs=one(t, d), out_shape=S((b, t, d), f32),
        compiler_params=params(16), cost_estimate=cost(4), name="layer_end",
    )(mid, act, wd, vrow)


def input_end(x_ref, dm_ref, dj_ref, w_ref, vrow_ref, gx_ref):
    dh = dot(dj_ref[0], w_ref[...], 0, 0)
    xhat, rstd = norm_stats(x_ref[0])
    gy = dh * vrow_ref[0:1, :]
    m1 = jnp.mean(gy, axis=-1, keepdims=True)
    m2 = jnp.mean(gy * xhat, axis=-1, keepdims=True)
    gx_ref[0] = dm_ref[0] + rstd * (gy - m1 - xhat * m2)


def call_input_end(x, dm, dj, w, vrow):
    b, t, d = x.shape
    return pl.pallas_call(
        input_end, grid=(b,), in_specs=[one(t, d), one(t, d), one(3 * d, t), full(w), full(vrow)],
        out_specs=one(t, d), out_shape=S((b, t, d), f32),
        compiler_params=params(16), cost_estimate=cost(4), name="input_end",
    )(x, dm, dj, w, vrow)


def adam_values(master, first, second, grad, rate, decay):
    first_new = beta_first * first + (1.0 - beta_first) * grad
    second_new = beta_second * second + (1.0 - beta_second) * grad * grad
    first_hat = first_new * (1.0 / (1.0 - beta_first ** STEP))
    second_hat = second_new * (1.0 / (1.0 - beta_second ** STEP))
    new = master - rate * (first_hat / (jnp.sqrt(second_hat) + adam_eps) + decay * master)
    return new, first_new, second_new, new.astype(bf16)


def adam_rows(refs, outs, rows, grad, rate, decay):
    for out, value in zip(outs, adam_values(*(r[rows] for r in refs), grad, rate, decay)):
        out[rows] = value


def adam(lay, halves, names, mine_ref, other_ref, *refs):
    core = lay.position()[1]
    count = len(names)
    states = {name: refs[3 * k:3 * k + 3] for k, name in enumerate(names)}
    outs = {name: refs[3 * count + 4 * k:3 * count + 4 * k + 4] for k, name in enumerate(names)}
    rates = {"q": 0.6 * lay.d ** -0.5, "p": 0.6 * lay.d ** -0.5, "u": 0.6 * lay.d ** -0.5, "d": 0.6 * lay.ff ** -0.5, "v": vector_rate}

    def step(half, src_ref):
        for name, start, rows, col, at in halves[half]:
            if name == "v":
                grad = jnp.concatenate([src_ref[at + k:at + k + 1, :lay.piece] for k in range(3)], axis=1)
                size = 3 * lay.piece
                new = adam_values(*(r[...].reshape(1, size) for r in states[name]), grad, rates[name], 0.0)
                for out, value in zip(outs[name], new):
                    out[...] = value.reshape(size)
            else:
                span = (slice(start, start + rows), slice(col * lay.d, (col + 1) * lay.d))
                adam_rows(states[name], outs[name], span, src_ref[at:at + rows, :], rates[name], matrix_decay)

    for half in range(2):
        @pl.when(core == half)
        def _():
            step(half, mine_ref)
            step(1 - half, other_ref)


def call_adam(lay, halves, mine, other, states):
    names = tuple(states)
    flat = [a for name in names for a in states[name]]
    outs = [S(states[name][0].shape, t) for name in names for t in (f32, f32, f32, bf16)]
    got = pl.pallas_call(
        functools.partial(adam, lay, halves, names),
        in_specs=[whole(a) for a in (mine, other, *flat)], out_specs=[whole(a) for a in outs], out_shape=outs,
        compiler_params=params(16), cost_estimate=cost(3), name="adam",
    )(mine, other, *flat)
    return {name: got[4 * k:4 * k + 4] for k, name in enumerate(names)}


def after(value, *earlier):
    return lax.optimization_barrier((value, *earlier))[0] if earlier else value


class Links:
    def __init__(self, mesh):
        self.wide, self.narrow = mesh.shape["wide"], mesh.shape["narrow"]
        bits = [1 << k for k in range(self.wide.bit_length() - 1)]
        self.orders = (bits[::-1], bits[:1] + bits[:0:-1])
        self.rounds = len(bits)
        self.masks = []
        for order in self.orders:
            masks = [0]
            for bit in order:
                masks = masks + [m ^ bit for m in masks]
            self.masks.append(masks)
        self.slots = [[masks.index(m) for m in range(self.wide)] for masks in self.masks]

    def permute(self, value, partner):
        pairs = []
        for n in range(self.narrow):
            for w in range(self.wide):
                n2, w2 = partner(n, w)
                pairs.append((n * self.wide + w, n2 * self.wide + w2))
        return lax.ppermute(value, ("narrow", "wide"), pairs)

    def core(self, value):
        return self.permute(value, lambda n, w: (n ^ 1, w))

    def step(self, value, k):
        return self.permute(value, lambda n, w: (n, w ^ self.orders[n % 2][k]))

    def others(self, value):
        total = value.astype(f32)
        bit = 2
        while bit < self.narrow:
            low = total.astype(bf16)
            total = low.astype(f32) + self.permute(low, lambda n, w, bit=bit: (n ^ bit, w)).astype(f32)
            bit *= 2
        return total

    def here(self):
        return lax.axis_index("wide"), lax.axis_index("narrow") % 2

    def gather(self, half):
        moving = Gather(self, half)
        for _ in range(self.rounds):
            moving.round()
        return moving.core()

    def reduce(self, keep, give):
        moving = Reduce(self, keep, give)
        moving.core()
        for _ in range(self.rounds):
            moving.round()
        moving.others()
        return moving.finish()


    def gather_rows(self, packed):
        me, core = self.here()
        rows, columns = packed.shape
        mine, other = self.gather(lax.dynamic_slice_in_dim(packed, core * (rows // 2), rows // 2))
        both = jnp.concatenate([mine, other], axis=0)
        relative = jnp.arange(self.wide) ^ me
        first = jnp.take(jnp.array(self.slots[0]), relative) + core * self.wide
        second = jnp.take(jnp.array(self.slots[1]), relative) + (1 - core) * self.wide
        index = jnp.stack([first, second], axis=1).reshape(-1)
        return jnp.take(both, index, axis=0).reshape(self.wide, rows, columns)

    def reduce_rows(self, packed):
        me, core = self.here()
        _, rows, columns = packed.shape
        halves = packed.reshape(2 * self.wide, rows // 2, columns)
        masks = jnp.array(self.masks)
        keep = jnp.take(halves, (masks[core] ^ me) * 2 + core, axis=0)
        give = jnp.take(halves, (masks[1 - core] ^ me) * 2 + (1 - core), axis=0)
        total, other = self.reduce(keep, give.astype(bf16))
        return jnp.where(core == 0, jnp.concatenate([total, other]), jnp.concatenate([other, total]))


class Gather:
    def __init__(self, links, half):
        self.links, self.held, self.k = links, half[None], 0

    def round(self, *beside):
        got = self.links.step(self.held, self.k)
        self.held = jnp.concatenate([after(self.held, *beside), got], axis=0)
        self.k += 1

    def core(self):
        return self.held, self.links.core(self.held)

    def last(self, *before):
        self.got = self.links.step(self.held, self.k)
        self.other = self.links.core(after(self.held, *before))

    def slots(self):
        return self.held, self.got, self.other, self.links.core(self.got)


class Reduce:
    def __init__(self, links, keep, give):
        self.links, self.held, self.give, self.k = links, keep, give, links.rounds

    def core(self, *beside):
        got = self.links.core(self.give)
        self.held = after(self.held, *beside).astype(f32) + got.astype(f32)

    def round(self, *beside):
        self.k -= 1
        half = self.held.shape[0] // 2
        self.held = after(self.held[:half], *beside) + self.links.step(self.held[half:].astype(bf16), self.k).astype(f32)

    def others(self):
        self.held = self.links.others(self.held[0])

    def finish(self):
        return self.held, self.links.core(self.held)


class Here:
    def __init__(self, held, other):
        self.held, self.other = held, other

    def round(self, *beside):
        pass

    def last(self, *before):
        self.got = None

    def slots(self):
        half = self.held.shape[0] // 2
        return self.held[:half], self.held[half:], self.other[:half], self.other[half:]

    def others(self):
        pass

    def core(self, *beside):
        return self.held, self.other

    finish = core


def to_rows(block, columns):
    return jnp.concatenate([block[..., j:j + columns] for j in range(0, block.shape[-1], columns)], axis=-2)


def from_rows(block, count):
    return jnp.concatenate(jnp.split(block, count, axis=-2), axis=-1)


def padded(block, multiple):
    extra = -block.shape[-2] % multiple
    return jnp.pad(block, [(0, 0)] * (block.ndim - 2) + [(0, extra), (0, 0)])


def to_slots(lay, halves, rows, arrays):
    out = []
    for half in halves:
        parts = []
        for name, start, count, col, _ in half:
            block = arrays[name].reshape(OWNERS, -1, arrays[name].shape[-1])
            parts.append(block[:, start:start + count, col * lay.d:(col + 1) * lay.d])
        block = jnp.concatenate(parts, axis=1)
        out.append(jnp.pad(block, ((0, 0), (0, rows - block.shape[1]), (0, 0))))
    return out


def from_slots(halves, both):
    found = {}
    for half, block in zip(halves, both):
        for name, start, count, col, at in half:
            found.setdefault(name, {})[(start, col)] = block[:, at:at + count].astype(f32)
    out = {}
    for name, parts in found.items():
        axis = 2 if max(col for _, col in parts) else 1
        block = jnp.concatenate([parts[key] for key in sorted(parts)], axis=axis)
        out[name] = block.reshape(-1, block.shape[-1])
    return out


FIRST_IMAGES = 2
BACK_IMAGES = 1


def compute(lay, x, cot, gather, reduce, finish_second, rounds):
    b = x.shape[0]
    k = min(FIRST_IMAGES, b - 1)
    one, two = gather
    one.round()
    two.held = after(two.held, one.held)
    two.round()
    for _ in range(rounds - 2):
        one.round()
    one.last()
    if one.got is not None:
        one.got, two.held = lax.optimization_barrier((one.got, two.held))
    first = one.slots()
    *outs, wq, vrow, vcol = call_attn_fwd_first(lay, first, x, k)
    for _ in range(rounds - 2):
        two.round(vcol)
    *outs, two.held = lax.optimization_barrier((*outs, two.held))
    jt, e, il, ot, h = call_attn_fwd_rest(x, wq, vrow, vcol, outs, k, b - k)
    two.last(ot)
    if two.got is not None:
        ot, two.got = lax.optimization_barrier((ot, two.got))
    second = two.slots()
    mid, act, dm, dot_, wd, dv, keep, give = call_mlp(lay, second, x, ot, cot, vrow)
    down = reduce(keep, give)
    acts = (jt, e, il, ot, dot_, h)
    dj, dw = call_attn_bwd_first(acts, BACK_IMAGES)
    down.core(dw)
    dw, down.held = lax.optimization_barrier((dw, down.held))
    dj, keep, give = call_attn_bwd_last(lay, acts, dw, wq, vrow, dv, dj, BACK_IMAGES, b - BACK_IMAGES)
    down.round(dj)
    up = reduce(keep, give)
    up.core(down.held)
    for _ in range(rounds - 2):
        down.round(up.held)
    dj, up.held = lax.optimization_barrier((dj, up.held))
    up.round()
    gx = call_input_end(x, dm, dj, wq, vrow)
    gx, up.held = lax.optimization_barrier((gx, up.held))
    lo = call_layer_end(after(mid, gx), act, wd, vrow)
    up.round(lo, down.held)
    down.round()
    for _ in range(rounds - 2):
        up.round(down.held)
    down.others()
    up.others()
    up.held, down.held = lax.optimization_barrier((up.held, down.held))
    second_new = finish_second(*down.finish())
    return lo, gx, up.finish(), second_new


def eight_owners(links, lay, x, cot, states):
    masters = {name: s[0] for name, s in states.items()}
    first, second = call_pack(lay, *(masters[name] for name in "qpudv"))
    gather = Gather(links, first), Gather(links, second)

    def finish_second(mine, other):
        return call_adam(lay, lay.second, mine, other, {name: states[name] for name in "pud"})

    lo, gx, first_sum, new = compute(lay, x, cot, gather, functools.partial(Reduce, links), finish_second, links.rounds)
    new |= call_adam(lay, lay.first, *first_sum, {name: states[name] for name in "qv"})
    return lo, gx, new


def any_owners(links, lay, x, cot, states):
    n, d = links.wide, lay.d
    masters = {name: s[0] for name, s in states.items()}
    v_size = masters["v"].shape[0]
    v_rows = -(-v_size // d)

    def vec_rows(v):
        return jnp.pad(v, ((0, 0), (0, v_rows * d - v_size))).reshape(-1, v_rows, d)

    def split(block):
        at, out = 0, {}
        for name in "qpu":
            rows = masters[name].shape[0]
            out[name] = block[:, at:at + rows]
            at += rows
        rows = masters["d"].shape[0]
        out["d"] = from_rows(block[:, at:at + rows * lay.cols], lay.cols)
        at += rows * lay.cols
        out["v"] = block[:, at:at + v_rows].reshape(-1, 1, v_rows * d)[:, :, :v_size]
        return {name: a.reshape(-1, a.shape[2]) for name, a in out.items()}

    def join(a, lead):
        blocks = [a[name].reshape(lead, -1, d) for name in "qpu"]
        blocks += [to_rows(a["d"].reshape(lead, -1, lay.ff), d), vec_rows(a["v"].reshape(lead, v_size))]
        return padded(jnp.concatenate(blocks, axis=1), 32)

    def eighths(v):
        return jnp.pad(v.reshape(OWNERS, 3, lay.piece), ((0, 0), (0, 13), (0, d - lay.piece))).reshape(-1, d)

    got = split(links.gather_rows(join(masters, 1)[0].astype(bf16)))
    got["v"] = eighths(got["v"])
    gather = Here(*to_slots(lay, lay.first, lay.first_rows, got)), Here(*to_slots(lay, lay.second, lay.second_rows, got))
    lo, gx, first_sum, second_sum = compute(lay, x, cot, gather, Here, lambda *both: both, 3)
    grads = from_slots(lay.first, first_sum) | from_slots(lay.second, second_sum)
    grads["v"] = grads["v"].reshape(OWNERS, 16, d)[:, :3, :lay.piece]
    mine = split(links.reduce_rows(join(grads, n))[None])
    rates = {"q": 0.6 * d ** -0.5, "p": 0.6 * d ** -0.5, "u": 0.6 * d ** -0.5, "d": 0.6 * lay.ff ** -0.5, "v": vector_rate}
    new = {}
    for name, refs in states.items():
        new[name] = adam_values(*refs, mine[name].reshape(refs[0].shape), rates[name], 0.0 if name == "v" else matrix_decay)
    return lo, gx, new


def per_device(links, x, cot, *arrays):
    if links.wide == OWNERS:
        run, orders, position = eight_owners, links.orders, links.here
    else:
        run, orders, position = any_owners, [[1, 2, 4]] * 2, lambda: (0, 0)
    lay = Layout(x.shape[2], arrays[3].shape[1], orders, position)
    names = "qpudv"
    states = {name: arrays[k::5] for k, name in enumerate(names)}
    lo, gx, new = run(links, lay, x, cot, states)
    return (lo, gx, *(a for name in names for a in new[name]))


def solution(mesh):
    tokens = P(("narrow", "wide"), None, None)
    matrix, vector = P("wide", None), P("wide")
    state = (matrix,) * 4 + (vector,)
    return jax.shard_map(
        functools.partial(per_device, Links(mesh)),
        mesh=mesh,
        in_specs=(tokens, tokens) + state * 3,
        out_specs=(tokens, tokens) + (matrix,) * 16 + (vector,) * 4,
        check_vma=False,
    )
```
